512 devices in a mesh: batch: 8 (over z), pair: 2 (over core), ctx: 32 (over y, x).
Axes of the slice: x: 4, y: 8, z: 8, core: 2. Of those that a mesh axis runs over, the one named last changes fastest.
Arguments:
- prompt_keys: bfloat16 [8, 2048, 512], P('batch', 'ctx', 'pair'), may hold values from -6 to 6
- prompt_values: bfloat16 [8, 2048, 512], P('batch', 'ctx', 'pair'), may hold values from -6 to 6
- queries: bfloat16 [8, 2, 1024, 4096], P('batch', 'pair', 'ctx'), may hold values from -6 to 6
- resp_keys: bfloat16 [8, 2, 1024, 512], P('batch', 'pair', 'ctx'), may hold values from -6 to 6
- resp_values: bfloat16 [8, 2, 1024, 512], P('batch', 'pair', 'ctx'), may hold values from -6 to 6
- resp_grads: bfloat16 [8, 2, 1024, 4096], P('batch', 'pair', 'ctx'), may hold values from -640 to 640
- resp_lse: bfloat16 [8, 2, 1024, 32], P('batch', 'pair', 'ctx'), may hold values from 6 to 9
- resp_delta: bfloat16 [8, 2, 1024, 32], P('batch', 'pair', 'ctx'), may hold values from -6144 to 6144
- logratio: float32 [8, 2, 1024], P('batch', None, 'ctx'), may hold values from -4 to 4
- lengths: int32 [8, 3], P('batch'), may hold values from 256 to 2048, as said below
Outputs:
- prompt_key_grad: bfloat16 [8, 2048, 512], P('batch', 'ctx', 'pair')
- prompt_value_grad: bfloat16 [8, 2048, 512], P('batch', 'ctx', 'pair')
- query_grad: bfloat16 [8, 2, 1024, 4096], P('batch', None, 'ctx', 'pair')
- key_grad: bfloat16 [8, 2, 1024, 512], P('batch', None, 'ctx', 'pair')
- value_grad: bfloat16 [8, 2, 1024, 512], P('batch', None, 'ctx', 'pair')
- pair_gate: float32 [8], P('batch')
The draws below stay inside these ranges and needn't reach their ends.
Inputs may be any that keep to these rules, and one draw needn't show every extreme that they name: `lengths`: column 0 holds 512 to 2048, and 2048 in some pair; columns 1 and 2 hold 256 to 1024, and 1024 in some response.
All inputs are finite; a program needn't handle non-finite values.
Results may differ from the reference program's by a relative error of at most 0.02.
Values may be sent and summed in bfloat16 or wider, within the bound.
No kernel may reach another device: no remote copies, remote signals or barrier semaphores. Data moves between devices by JAX's collectives and lax.ppermute only.
A program may use at most 128 MiB of HBM per device.

```python
import jax
import jax.numpy as jnp
from jax import lax

DH = 128
HQ = 32
HK = 4
RTOK_DEV = 32
PROMPT = 2048
RESP = 1024
PAIRS = 8
N_CTX = 32


def draw_logratio(key, part):
    key = jax.random.fold_in(key, 7)
    first_key = jax.random.fold_in(key, 0)
    positions = jnp.arange(RESP, dtype=jnp.float32)
    rising = 0.3 * (1.0 + 2.0 * positions / RESP)
    values = jax.random.normal(first_key, (PAIRS, 2, RESP), jnp.float32) * rising
    return jnp.clip(values, -4.0, 4.0)


def draw_lengths(key, part):
    key = jax.random.fold_in(key, 13)
    key_list = jax.random.split(key, 4)
    prompt_len = jax.random.randint(key_list[0], (PAIRS,), PROMPT // 4, PROMPT + 1)
    full_pair = jax.random.randint(key_list[1], (), 0, PAIRS)
    prompt_len = jnp.where(jnp.arange(PAIRS) == full_pair, PROMPT, prompt_len)
    resp_len = jax.random.randint(key_list[2], (PAIRS * 2,), RESP // 4, RESP + 1)
    full_resp = jax.random.randint(key_list[3], (), 0, PAIRS * 2)
    resp_len = jnp.where(jnp.arange(PAIRS * 2) == full_resp, RESP, resp_len).reshape(PAIRS, 2)
    return jnp.concatenate([prompt_len[:, None], resp_len], axis=1).astype(jnp.int32)


def levels(key, dims, cuts, least, high):
    level, own = 1.0, jax.random.fold_in(key, 6)
    for position, shards_of in cuts:
        steps = jnp.exp(jax.random.uniform(jax.random.fold_in(own, position), (shards_of,), jnp.float32, least / len(cuts), high / len(cuts)))
        level = level * jnp.repeat(steps, dims[position] // shards_of).reshape([-1 if axis == position else 1 for axis in range(len(dims))])
    return level


def normal_values(rng, extent, deviation, most, cuts=(), kind=jnp.bfloat16):
    loudness = levels(rng, extent, cuts, -0.22, 0.18) if cuts else 1.0
    result = jax.random.normal(rng, extent, jnp.float32) * deviation * loudness
    return jnp.minimum(jnp.maximum(result, -most), most).astype(kind)


def setup_inputs(seed: int = 0) -> dict:
    seeds = jax.random.split(jax.random.key(seed), 11)
    return {
        "prompt_keys": normal_values(seeds[0], (PAIRS, PROMPT, HK * DH), 1.0, 6.0, ((0, 8), (1, 32), (2, 2))),
        "prompt_values": normal_values(seeds[1], (PAIRS, PROMPT, HK * DH), 1.0, 6.0, ((0, 8), (1, 32), (2, 2))),
        "queries": normal_values(seeds[2], (PAIRS, 2, RESP, HQ * DH), 1.0, 6.0, ((0, 8), (1, 2), (2, 32))),
        "resp_keys": normal_values(seeds[3], (PAIRS, 2, RESP, HK * DH), 1.0, 6.0, ((0, 8), (1, 2), (2, 32))),
        "resp_values": normal_values(seeds[4], (PAIRS, 2, RESP, HK * DH), 1.0, 6.0, ((0, 8), (1, 2), (2, 32))),
        "resp_grads": normal_values(seeds[5], (PAIRS, 2, RESP, HQ * DH), 100.0, 640.0, ((0, 8), (1, 2), (2, 32))),
        "resp_lse": jnp.clip(6.0 + 3.0 * jax.random.uniform(seeds[6], (PAIRS, 2, RESP, HQ), jnp.float32) ** levels(seeds[6], (PAIRS, 2, RESP, HQ), ((0, 8), (1, 2), (2, 32)), -0.2, 0.2), 6.0, 9.0).astype(jnp.bfloat16),
        "resp_delta": normal_values(seeds[7], (PAIRS, 2, RESP, HQ), 1000.0, 6144.0, ((0, 8), (1, 2), (2, 32))),
        "logratio": draw_logratio(jax.random.fold_in(seeds[10], 71), 0),
        "lengths": draw_lengths(jax.random.fold_in(seeds[10], 71), 0),
    }


beta_coef = 0.1


def rounded_result(values):
    return lax.optimization_barrier(values.astype(jnp.bfloat16)).astype(jnp.float32)


def one_pair(prompt_keys, prompt_values, queries, resp_keys, resp_values, resp_grads, resp_lse, resp_delta, logratio, lengths):
    group_size = HQ // HK
    scale_factor = DH ** -0.5
    sign_column = jnp.array([-1.0, 1.0], dtype=jnp.float32)[:, None, None]
    query_all = queries.astype(jnp.float32).reshape(2, RESP, HK, group_size, DH)
    grad_all = (resp_grads.astype(jnp.float32) * sign_column).reshape(2, RESP, HK, group_size, DH)
    lse_all = resp_lse.astype(jnp.float32).reshape(2, RESP, HK, group_size)
    delta_all = (resp_delta.astype(jnp.float32) * sign_column).reshape(2, RESP, HK, group_size)
    prompt_key_rows = prompt_keys.astype(jnp.float32).reshape(PROMPT, HK, DH)
    prompt_value_rows = prompt_values.astype(jnp.float32).reshape(PROMPT, HK, DH)
    resp_key_rows = resp_keys.astype(jnp.float32).reshape(2, RESP, HK, DH)
    resp_value_rows = resp_values.astype(jnp.float32).reshape(2, RESP, HK, DH)
    prompt_live = jnp.arange(PROMPT, dtype=jnp.int32) < lengths[0]
    resp_positions = jnp.arange(RESP, dtype=jnp.int32)

    def block_step(loop_carry_state, block_index):
        prompt_key_accumulator, prompt_value_accumulator, response_key_accumulator, response_value_accumulator = loop_carry_state
        first_row = block_index * RTOK_DEV
        query_block = lax.dynamic_slice_in_dim(query_all, first_row, RTOK_DEV, 1)
        gradient_tile_rows = lax.dynamic_slice_in_dim(grad_all, first_row, RTOK_DEV, 1)
        lse_block = lax.dynamic_slice_in_dim(lse_all, first_row, RTOK_DEV, 1)
        delta_block = lax.dynamic_slice_in_dim(delta_all, first_row, RTOK_DEV, 1)
        rows_here = first_row + jnp.arange(RTOK_DEV, dtype=jnp.int32)
        row_live = rows_here[None, :] < lengths[1:3][:, None]

        scores = scale_factor * jnp.einsum("srkgd,pkd->srkgp", query_block, prompt_key_rows)
        allowed = row_live[:, :, None, None, None] & prompt_live[None, None, None, None, :]
        weights = jnp.where(allowed, jnp.exp(scores - lse_block[..., None]), 0.0)
        weight_grads = jnp.einsum("srkgd,pkd->srkgp", gradient_tile_rows, prompt_value_rows)
        score_grads = rounded_result(weights * (weight_grads - delta_block[..., None]))
        weight_lower_precision = rounded_result(weights)
        query_prompt = scale_factor * jnp.einsum("srkgp,pkd->srkgd", score_grads, prompt_key_rows)
        prompt_key_accumulator = prompt_key_accumulator + rounded_result(scale_factor * jnp.einsum("joyin,joyit->nyt", score_grads, query_block))
        prompt_value_accumulator = prompt_value_accumulator + rounded_result(jnp.einsum("joyin,joyit->nyt", weight_lower_precision, gradient_tile_rows))

        scores = scale_factor * jnp.einsum("srkgd,stkd->srkgt", query_block, resp_key_rows)
        causal = resp_positions[None, None, :] <= rows_here[None, :, None]
        allowed = (row_live[:, :, None] & causal)[:, :, None, None, :]
        weights = jnp.where(allowed, jnp.exp(scores - lse_block[..., None]), 0.0)
        weight_grads = jnp.einsum("srkgd,stkd->srkgt", gradient_tile_rows, resp_value_rows)
        score_grads = rounded_result(weights * (weight_grads - delta_block[..., None]))
        weight_lower_precision = rounded_result(weights)
        query_resp = scale_factor * jnp.einsum("srkgt,stkd->srkgd", score_grads, resp_key_rows)
        response_key_accumulator = response_key_accumulator + rounded_result(scale_factor * jnp.einsum("vnhax,vnhaq->vxhq", score_grads, query_block))
        response_value_accumulator = response_value_accumulator + rounded_result(jnp.einsum("vnhax,vnhaq->vxhq", weight_lower_precision, gradient_tile_rows))
        query_gradient_total = (query_prompt + query_resp).reshape(2, RTOK_DEV, HQ * DH)
        return (prompt_key_accumulator, prompt_value_accumulator, response_key_accumulator, response_value_accumulator), query_gradient_total

    prompt_zero = jnp.zeros((PROMPT, HK, DH), jnp.float32)
    resp_zero = jnp.zeros((2, RESP, HK, DH), jnp.float32)
    sums, query_blocks = lax.scan(block_step, (prompt_zero, prompt_zero, resp_zero, resp_zero), jnp.arange(N_CTX, dtype=jnp.int32))
    query_gradient_total = jnp.transpose(query_blocks, (1, 0, 2, 3)).reshape(2, RESP, HQ * DH)
    chosen = jnp.sum(jnp.where(resp_positions < lengths[1], logratio[0], 0.0))
    rejected = jnp.sum(jnp.where(resp_positions < lengths[2], logratio[1], 0.0))
    gate = beta_coef * jax.nn.sigmoid(-beta_coef * (chosen - rejected))
    prompt_key_grad = (gate * sums[0]).reshape(PROMPT, HK * DH).astype(jnp.bfloat16)
    prompt_value_grad = (gate * sums[1]).reshape(PROMPT, HK * DH).astype(jnp.bfloat16)
    query_grad = (gate * query_gradient_total).astype(jnp.bfloat16)
    key_grad = (gate * sums[2]).reshape(2, RESP, HK * DH).astype(jnp.bfloat16)
    value_grad = (gate * sums[3]).reshape(2, RESP, HK * DH).astype(jnp.bfloat16)
    return prompt_key_grad, prompt_value_grad, query_grad, key_grad, value_grad, gate


def reference(prompt_keys, prompt_values, queries, resp_keys, resp_values, resp_grads, resp_lse, resp_delta, logratio, lengths):
    results = lax.map(lambda arrays: one_pair(*arrays), (prompt_keys, prompt_values, queries, resp_keys, resp_values, resp_grads, resp_lse, resp_delta, logratio, lengths))
    return (results[0], results[1], results[2], results[3], results[4], results[5])
```

```python
import functools

import jax
import jax.numpy as jnp
from jax import lax
from jax.experimental import pallas as pl
from jax.experimental.pallas import tpu as pltpu
from jax.sharding import Mesh, PartitionSpec as P

beta_coef = 0.1
f32, bf16 = jnp.float32, jnp.bfloat16
LANES = 128
CTX = ("y", "x")
VMEM = pltpu.VMEM
SMEM = pltpu.SMEM

POS = 32
HEADS = 4
GROUP = 8
TILE = POS * GROUP
ROWS_Y = 8
CTX_N = 32
PROMPT_HALF = 32
RESP_HALF = 16
STAT_ROWS = 16
QUERY_ROWS = 2 * TILE + STAT_ROWS
DEAD = 1e30


def dot(a, b, dims):
    return lax.dot_general(a, b, (dims, ((), ())), preferred_element_type=f32)


def call(kernel, out_shape, n_in, smem=(), flops=0, scratch=(), size=0):
    specs = [pl.BlockSpec(memory_space=SMEM if i in smem else VMEM) for i in range(n_in)]
    many = isinstance(out_shape, tuple)
    return pl.pallas_call(
        kernel,
        out_shape=out_shape,
        in_specs=specs,
        out_specs=tuple(pl.BlockSpec(memory_space=VMEM) for _ in out_shape)
        if many
        else pl.BlockSpec(memory_space=VMEM),
        scratch_shapes=list(scratch),
        compiler_params=pltpu.CompilerParams(vmem_limit_bytes=40 * 2**20),
        cost_estimate=pl.CostEstimate(flops=flops, bytes_accessed=size, transcendentals=0),
    )


def pack_kernel(q_ref, g_ref, lse_ref, delta_ref, pk_ref, pv_ref, rk_ref, rv_ref, query_ref, pair_ref):
    sign = jnp.where(lax.axis_index("pair") == 0, -1.0, 1.0).astype(f32)
    for p in range(2):
        for h in range(2):
            columns = slice(h * LANES, (h + 1) * LANES)
            rows = slice(p * PROMPT_HALF, (p + 1) * PROMPT_HALF)
            pair_ref[p, h * 32 : h * 32 + 32, :] = pk_ref[rows, columns]
            pair_ref[p, 64 + h * 32 : 96 + h * 32, :] = pv_ref[rows, columns]
        for h in range(HEADS):
            columns = slice(h * LANES, (h + 1) * LANES)
            rows = slice(p * RESP_HALF, (p + 1) * RESP_HALF)
            pair_ref[p, 128 + h * 16 : 144 + h * 16, :] = rk_ref[rows, columns]
            pair_ref[p, 192 + h * 16 : 208 + h * 16, :] = rv_ref[rows, columns]
    for x in range(HEADS):
        for h in range(GROUP):
            columns = slice((x * GROUP + h) * LANES, (x * GROUP + h + 1) * LANES)
            query = q_ref[:, columns]
            grad = (g_ref[:, columns].astype(f32) * sign).astype(bf16)
            for p in range(2):
                query_ref[p * HEADS + x, h * POS : (h + 1) * POS, :] = query
                query_ref[p * HEADS + x, TILE + h * POS : TILE + (h + 1) * POS, :] = grad

    heads = HEADS * GROUP
    lane = lax.broadcasted_iota(jnp.int32, (POS, TILE), 1)
    spread = (lane % POS == lax.broadcasted_iota(jnp.int32, (POS, TILE), 0)).astype(bf16)
    lane = lax.broadcasted_iota(jnp.int32, (heads, TILE), 1)
    keep = lax.broadcasted_iota(jnp.int32, (heads, TILE), 0) % GROUP == lane // POS

    def rows_of(ref):
        spread_out = jnp.where(keep, dot(ref[...], spread, ((0,), (0,))), 0.0)
        return jnp.sum(spread_out.reshape(HEADS, GROUP, TILE), axis=1)

    lse, delta = rows_of(lse_ref), rows_of(delta_ref) * sign
    row = lax.broadcasted_iota(jnp.int32, (STAT_ROWS, LANES), 0)
    for x in range(HEADS):
        parts = [r[x : x + 1, i * LANES : (i + 1) * LANES] for r in (lse, delta) for i in range(2)]
        block = jnp.zeros((STAT_ROWS, LANES), f32)
        for i, part in enumerate(parts):
            block = jnp.where(row == i, part, block)
        for p in range(2):
            query_ref[p * HEADS + x, 2 * TILE :, :] = block.astype(bf16)


def spread_kernel(lengths_ref, logratio_ref, pair_ref, prompt_ref, resp_ref):
    core = lax.axis_index("pair")
    ctx = lax.axis_index("y") * HEADS + lax.axis_index("x")
    first = ctx * 2 * PROMPT_HALF + core * PROMPT_HALF
    key_live = first + lax.broadcasted_iota(jnp.int32, (PROMPT_HALF, LANES), 0) < lengths_ref[0, 0]
    position = ctx * POS + lax.broadcasted_iota(jnp.int32, (1, POS), 1)
    chosen = jnp.where(position < lengths_ref[0, 1], logratio_ref[0:1, :], 0.0)
    rejected = jnp.where(position < lengths_ref[0, 2], logratio_ref[1:2, :], 0.0)
    margin = jnp.sum(chosen - rejected, axis=1, keepdims=True)
    high = margin.astype(bf16).astype(f32)
    middle = (margin - high).astype(bf16).astype(f32)
    low = margin - high - middle
    lane = lax.broadcasted_iota(jnp.int32, (16, LANES), 1)
    row = lax.broadcasted_iota(jnp.int32, (16, LANES), 0)
    block = jnp.where(lane == 0, high, jnp.where(lane == 1, middle, jnp.where(lane == 2, low, 0.0)))
    block = jnp.where(row == 0, block, 0.0).astype(bf16)
    for x in range(HEADS):
        half, odd = x // 2, x % 2
        key = pair_ref[half, odd * 32 : odd * 32 + 32, :]
        key = jnp.where(key_live, key.astype(f32), 0.0).astype(bf16)
        value = pair_ref[half, 64 + odd * 32 : 96 + odd * 32, :]
        for y in range(ROWS_Y):
            to = y * HEADS + x
            prompt_ref[to, 0:32, :] = key
            prompt_ref[to, 32:64, :] = value
            for s in range(2):
                resp_ref[to, 32 * s : 32 * s + 16, :] = pair_ref[s, 128 + 16 * x : 144 + 16 * x, :]
                resp_ref[to, 32 * s + 16 : 32 * s + 32, :] = pair_ref[s, 192 + 16 * x : 208 + 16 * x, :]
            resp_ref[to, 64:80, :] = block


def row_stats(lengths_ref, query_ref, tile):
    block = query_ref[tile, 2 * TILE :, :].astype(f32)
    lse = jnp.concatenate([block[0:1], block[1:2]], axis=1) * 1.4426950408889634
    delta = jnp.concatenate([block[2:3], block[3:4]], axis=1)
    lane = lax.broadcasted_iota(jnp.int32, (1, TILE), 1)
    side = tile // HEADS
    first = (lax.axis_index("y") * HEADS + tile % HEADS) * POS
    position = first + lane % POS
    lse = jnp.where(position < lengths_ref[0, 1 + side], lse, DEAD)
    return lse, delta, position


def cell(key, value, query, grad, lse, delta, allowed=None):
    scale = LANES**-0.5
    scores = dot(key, query, ((1,), (1,)))
    weights = jnp.exp2(scores * (scale * 1.4426950408889634) - lse)
    if allowed is not None:
        weights = jnp.where(allowed, weights, 0.0)
    weight_grads = dot(value, grad, ((1,), (1,)))
    score_grads = (weights * (weight_grads - delta)).astype(bf16)
    return weights.astype(bf16), score_grads


def prompt_kernel(lengths_ref, query_ref, kv_ref, acc_ref, out_ref, key_acc, value_acc):
    scale = LANES**-0.5
    key_acc[...] = jnp.zeros_like(key_acc)
    value_acc[...] = jnp.zeros_like(value_acc)
    per = 8
    rows = per * PROMPT_HALF

    @pl.loop(0, 2 * HEADS)
    def _(tile):
        lse, delta, _ = row_stats(lengths_ref, query_ref, tile)
        query = query_ref[tile, 0:TILE, :]
        grad = query_ref[tile, TILE : 2 * TILE, :]
        total = None
        for c in range(CTX_N // per):
            key = kv_ref[c * per : (c + 1) * per, 0:PROMPT_HALF, :].reshape(rows, LANES)
            value = kv_ref[c * per : (c + 1) * per, PROMPT_HALF:, :].reshape(rows, LANES)
            weights, score_grads = cell(key, value, query, grad, lse, delta)
            at = slice(c * rows, (c + 1) * rows)
            value_acc[at, :] += dot(weights, grad, ((1,), (0,)))
            key_acc[at, :] += dot(score_grads, query, ((1,), (0,)))
            term = dot(score_grads, key, ((0,), (0,)))
            total = term if total is None else total + term
        acc_ref[tile] = total

    out_ref[:, 0:PROMPT_HALF, :] = (key_acc[...] * scale).astype(bf16).reshape(CTX_N, PROMPT_HALF, LANES)
    out_ref[:, PROMPT_HALF:, :] = value_acc[...].astype(bf16).reshape(CTX_N, PROMPT_HALF, LANES)


def resp_kernel(lengths_ref, query_ref, kv_ref, acc_ref, out_ref, dq_ref, gate_ref, key_acc, value_acc):
    scale = LANES**-0.5
    margin = jnp.sum(kv_ref[:, 64:80, :].astype(f32), axis=(0, 1), keepdims=True).reshape(1, LANES)
    margin = jnp.sum(margin, axis=1, keepdims=True)
    gate_ref[...] = jnp.broadcast_to(beta_coef * jax.nn.sigmoid(-beta_coef * margin), gate_ref.shape)
    key_acc[...] = jnp.zeros_like(key_acc)
    value_acc[...] = jnp.zeros_like(value_acc)
    core = lax.axis_index("pair")
    per = 16
    rows = per * RESP_HALF
    for s in range(2):

        @pl.loop(0, HEADS)
        def _(x):
            tile = s * HEADS + x
            lse, delta, position = row_stats(lengths_ref, query_ref, tile)
            query = query_ref[tile, 0:TILE, :]
            grad = query_ref[tile, TILE : 2 * TILE, :]
            total = acc_ref[tile]
            for c in range(CTX_N // per):
                k0 = 32 * s
                key = kv_ref[c * per : (c + 1) * per, k0 : k0 + 16, :].reshape(rows, LANES)
                value = kv_ref[c * per : (c + 1) * per, k0 + 16 : k0 + 32, :].reshape(rows, LANES)
                index = lax.broadcasted_iota(jnp.int32, (rows, 1), 0)
                key_position = (c * per + index // RESP_HALF) * POS + core * RESP_HALF + index % RESP_HALF
                weights, score_grads = cell(key, value, query, grad, lse, delta, key_position <= position)
                at = slice((s * (CTX_N // per) + c) * rows, (s * (CTX_N // per) + c + 1) * rows)
                value_acc[at, :] += dot(weights, grad, ((1,), (0,)))
                key_acc[at, :] += dot(score_grads, query, ((1,), (0,)))
                total += dot(score_grads, key, ((0,), (0,)))
            dq_ref[x, s * TILE : (s + 1) * TILE, :] = (total * scale).astype(bf16)

        at = slice(s * CTX_N * RESP_HALF, (s + 1) * CTX_N * RESP_HALF)
        shape = (CTX_N, RESP_HALF, LANES)
        out_ref[:, 32 * s : 32 * s + 16, :] = (key_acc[at, :] * scale).astype(bf16).reshape(shape)
        out_ref[:, 32 * s + 16 : 32 * s + 32, :] = value_acc[at, :].astype(bf16).reshape(shape)


def sum_kernel(prompt, lengths_ref, gate_ref, part_ref, pair_ref):
    gate = gate_ref[0:1, 0:1]
    if prompt:
        ctx = lax.axis_index("y") * HEADS + lax.axis_index("x")
        first = ctx * 2 * PROMPT_HALF + lax.axis_index("pair") * PROMPT_HALF
        row = lax.broadcasted_iota(jnp.int32, (64, LANES), 0) % PROMPT_HALF
        live = first + row < lengths_ref[0, 0]
    for x in range(HEADS):
        total = part_ref[x].astype(f32)
        for y in range(1, ROWS_Y):
            total += part_ref[y * HEADS + x].astype(f32)
        total = total * gate
        if prompt:
            total = jnp.where(live, total, 0.0)
        pair_ref[x // 2, (x % 2) * 64 : (x % 2) * 64 + 64, :] = total.astype(bf16)


def prompt_final_kernel(pair_ref, key_ref, value_ref):
    for p in range(2):
        for h in range(2):
            columns = slice(h * LANES, (h + 1) * LANES)
            key_ref[0, p * 32 : p * 32 + 32, columns] = pair_ref[p, h * 64 : h * 64 + 32, :]
            value_ref[0, p * 32 : p * 32 + 32, columns] = pair_ref[p, h * 64 + 32 : h * 64 + 64, :]


def resp_final_kernel(pair_ref, key_ref, value_ref):
    for p in range(2):
        for h in range(2):
            columns = slice(h * LANES, (h + 1) * LANES)
            for s in range(2):
                at = h * 64 + 32 * s
                key_ref[0, s, p * 16 : p * 16 + 16, columns] = pair_ref[p, at : at + 16, :]
                value_ref[0, s, p * 16 : p * 16 + 16, columns] = pair_ref[p, at + 16 : at + 32, :]


def query_final_kernel(gate_ref, pair_ref, out_ref):
    gate = gate_ref[0:1, 0:1]
    for h in range(2):
        for s in range(2):
            for g in range(GROUP):
                rows = slice(h * 2 * TILE + s * TILE + g * POS, h * 2 * TILE + s * TILE + (g + 1) * POS)
                total = pair_ref[0, rows, :].astype(f32) + pair_ref[1, rows, :].astype(f32)
                column = (h * GROUP + g) * LANES
                out_ref[0, s, :, column : column + LANES] = (gate * total).astype(bf16)


def swap(values, axes):
    return lax.all_to_all(values, axes, split_axis=0, concat_axis=0, tiled=True)


def per_device(
    prompt_keys,
    prompt_values,
    queries,
    resp_keys,
    resp_values,
    resp_grads,
    resp_lse,
    resp_delta,
    logratio,
    lengths,
):
    shape = jax.ShapeDtypeStruct
    query_send, pair_send = call(
        pack_kernel,
        (shape((8, QUERY_ROWS, LANES), bf16), shape((2, 256, LANES), bf16)),
        8,
        size=2 * 2**20,
    )(
        queries[0, 0],
        resp_grads[0, 0],
        resp_lse[0, 0],
        resp_delta[0, 0],
        prompt_keys[0],
        prompt_values[0],
        resp_keys[0, 0],
        resp_values[0, 0],
    )
    query_rows = swap(query_send, ("pair", "x"))
    pair_rows = swap(pair_send, "pair")
    prompt_send, resp_send = call(
        spread_kernel,
        (shape((CTX_N, 64, LANES), bf16), shape((CTX_N, 80, LANES), bf16)),
        3,
        smem=(0,),
        size=2 * 2**20,
    )(lengths, logratio[0], pair_rows)
    prompt_kv = swap(prompt_send, CTX)
    resp_kv = swap(resp_send, CTX)
    acc, prompt_part = call(
        prompt_kernel,
        (shape((8, TILE, LANES), f32), shape((CTX_N, 64, LANES), bf16)),
        3,
        smem=(0,),
        scratch=(pltpu.VMEM((1024, LANES), f32), pltpu.VMEM((1024, LANES), f32)),
        flops=5 * 2 * 2048 * 1024 * 128 * 2,
        size=3 * 2**20,
    )(lengths, query_rows, prompt_kv)
    prompt_back = swap(prompt_part, CTX)
    resp_part, query_part, gate = call(
        resp_kernel,
        (
            shape((CTX_N, 64, LANES), bf16),
            shape((HEADS, 2 * TILE, LANES), bf16),
            shape((8, LANES), f32),
        ),
        4,
        smem=(0,),
        scratch=(pltpu.VMEM((1024, LANES), f32), pltpu.VMEM((1024, LANES), f32)),
        flops=5 * 2 * 1024 * 1024 * 128 * 2,
        size=3 * 2**20,
    )(lengths, query_rows, resp_kv, acc)
    resp_back = swap(resp_part, CTX)
    query_back = swap(query_part, "x")

    pair_shape = shape((2, 128, LANES), bf16)
    prompt_pair = call(functools.partial(sum_kernel, True), pair_shape, 3, smem=(0,), size=2**19)(
        lengths, gate, prompt_back
    )
    prompt_pair = swap(prompt_pair, "pair")
    prompt_key_grad, prompt_value_grad = call(
        prompt_final_kernel, (shape((1, 64, 256), bf16),) * 2, 1, size=2**17
    )(prompt_pair)

    query_pair = swap(query_back.reshape(2, 4 * TILE, LANES), "pair")
    query_grad = call(query_final_kernel, shape((1, 2, POS, 2048), bf16), 2, size=2**20)(gate, query_pair)

    resp_pair = call(functools.partial(sum_kernel, False), pair_shape, 3, smem=(0,), size=2**19)(
        lengths, gate, resp_back
    )
    resp_pair = swap(resp_pair, "pair")
    key_grad, value_grad = call(resp_final_kernel, (shape((1, 2, POS, 256), bf16),) * 2, 1, size=2**17)(
        resp_pair
    )
    return prompt_key_grad, prompt_value_grad, query_grad, key_grad, value_grad, gate[0, 0:1]


def solution(mesh):
    batch, pair, ctx = mesh.devices.shape
    split = Mesh(mesh.devices.reshape(batch, pair, ctx // HEADS, HEADS), ("batch", "pair", "y", "x"))
    prompt_spec = P("batch", CTX, "pair")
    resp_spec = P("batch", "pair", CTX, None)
    out_spec = P("batch", None, CTX, "pair")
    return jax.shard_map(
        per_device,
        mesh=split,
        in_specs=(
            prompt_spec,
            prompt_spec,
            resp_spec,
            resp_spec,
            resp_spec,
            resp_spec,
            resp_spec,
            resp_spec,
            P("batch", None, CTX),
            P("batch", None),
        ),
        out_specs=(prompt_spec, prompt_spec, out_spec, out_spec, out_spec, P("batch")),
        check_vma=False,
    )
```

```python
import jax
import jax.numpy as jnp
from jax import lax
from jax.experimental import pallas as pl
from jax.experimental.pallas import tpu as pltpu
from jax.sharding import Mesh, PartitionSpec as P

beta_coef = 0.1
f32, bf16 = jnp.float32, jnp.bfloat16
LANES = 128
CTX = ("y", "x")

X = 4
ROWS_Y = 8
CTX_N = 32
POS = 32
GROUP = 8
TILE = POS * GROUP
PROMPT_HALF = 32
RESP_HALF = 16
STAT_ROWS = 16
QUERY_ROWS = 2 * TILE + STAT_ROWS
SIDE = 2 * RESP_HALF
KV_ROWS = 2 * PROMPT_HALF + 2 * SIDE
LOG2E = 1.4426950408889634
SCALE = LANES**-0.5
DEAD = 1e30


def dot(a, b, dims):
    return lax.dot_general(a, b, (dims, ((), ())), preferred_element_type=f32)


def call(kernel, out_shape, spaces, flops=0, scratch=(), size=0):
    space = {"v": pltpu.VMEM, "s": pltpu.SMEM, "a": pl.ANY}
    many = isinstance(out_shape, tuple)
    out_spec = pl.BlockSpec(memory_space=pltpu.VMEM)
    return pl.pallas_call(
        kernel,
        out_shape=out_shape,
        in_specs=[pl.BlockSpec(memory_space=space[s]) for s in spaces],
        out_specs=tuple(out_spec for _ in out_shape) if many else out_spec,
        scratch_shapes=list(scratch),
        compiler_params=pltpu.CompilerParams(vmem_limit_bytes=24 * 2**20),
        cost_estimate=pl.CostEstimate(flops=flops, bytes_accessed=size, transcendentals=0),
    )


def fetch(pairs, sems):
    copies = [pltpu.make_async_copy(a, b, sems.at[i]) for i, (a, b) in enumerate(pairs)]
    for copy in copies:
        copy.start()
    for copy in copies:
        copy.wait()


def kv_pack_kernel(
    lengths_hbm, logratio_hbm, pk_hbm, pv_hbm, rk_hbm, rv_hbm, kv_ref, lengths, logratio, pk, pv, rk, rv, sems
):
    pairs = (
        (lengths_hbm, lengths),
        (logratio_hbm.at[0], logratio),
        (pk_hbm.at[0], pk),
        (pv_hbm.at[0], pv),
        (rk_hbm.at[0, 0], rk),
        (rv_hbm.at[0, 0], rv),
    )
    fetch(pairs, sems)
    first_core = lax.axis_index("pair") == 0
    ctx = lax.axis_index("y") * X + lax.axis_index("x")
    position = ctx * POS + lax.broadcasted_iota(jnp.int32, (1, POS), 1)
    chosen = jnp.where(position < lengths[0, 1], logratio[0:1, :], 0.0)
    rejected = jnp.where(position < lengths[0, 2], logratio[1:2, :], 0.0)
    margin = jnp.sum(chosen - rejected, axis=1, keepdims=True)
    high = margin.astype(bf16).astype(f32)
    middle = (margin - high).astype(bf16).astype(f32)
    low = margin - high - middle
    lane = lax.broadcasted_iota(jnp.int32, (16, LANES), 1)
    row = lax.broadcasted_iota(jnp.int32, (16, LANES), 0)
    block = jnp.where(lane == 0, high, jnp.where(lane == 1, middle, jnp.where(lane == 2, low, 0.0)))
    block = jnp.where(row == 0, block, 0.0).astype(bf16)
    for x in range(X):
        odd, half = x % 2, x // 2
        columns = slice(odd * LANES, (odd + 1) * LANES)
        others = slice((2 + odd) * LANES, (3 + odd) * LANES)
        rows = slice(half * PROMPT_HALF, (half + 1) * PROMPT_HALF)
        index = ctx * 2 * PROMPT_HALF + half * PROMPT_HALF
        live = index + lax.broadcasted_iota(jnp.int32, (PROMPT_HALF, LANES), 0) < lengths[0, 0]
        parts = [jnp.where(live, pk[rows, columns].astype(f32), 0.0).astype(bf16), pv[rows, columns]]
        rows = slice(half * RESP_HALF, (half + 1) * RESP_HALF)
        low_head = [ref[rows, columns].astype(f32) for ref in (rk, rv)]
        high_head = [ref[rows, others].astype(f32) for ref in (rk, rv)]
        parts += [jnp.where(first_core, a, b).astype(bf16) for a, b in zip(low_head, high_head)]
        parts += [jnp.where(first_core, b, a).astype(bf16) for a, b in zip(low_head, high_head)]
        parts += [block]
        for y in range(ROWS_Y):
            at = 0
            for part in parts:
                kv_ref[y * X + x, at : at + part.shape[0], :] = part
                at += part.shape[0]


def query_pack_kernel(q_hbm, g_hbm, lse_hbm, delta_hbm, own_ref, other_ref, q, g, lse, delta, sems):
    core, parity = lax.axis_index("pair"), lax.axis_index("x") % 2
    pairs = [(lse_hbm.at[0, 0], lse), (delta_hbm.at[0, 0], delta)]
    heads = []
    for i in range(4):
        head = 2 * (core if i < 2 else 1 - core) + (parity + i) % 2
        heads.append(head)
        columns = pl.ds(pl.multiple_of(head * GROUP * LANES, GROUP * LANES), GROUP * LANES)
        pairs += [(q_hbm.at[0, 0, :, columns], q.at[i]), (g_hbm.at[0, 0, :, columns], g.at[i])]
    fetch(pairs, sems)
    sign = jnp.where(core == 0, -1.0, 1.0).astype(f32)

    count = X * GROUP
    lane = lax.broadcasted_iota(jnp.int32, (POS, TILE), 1)
    spread = (lane % POS == lax.broadcasted_iota(jnp.int32, (POS, TILE), 0)).astype(bf16)
    head_of = lax.broadcasted_iota(jnp.int32, (count, TILE), 0)
    lane = lax.broadcasted_iota(jnp.int32, (count, TILE), 1)
    lse_rows = dot(lse[...], spread, ((0,), (0,)))
    delta_rows = dot(delta[...], spread, ((0,), (0,))) * sign
    row = lax.broadcasted_iota(jnp.int32, (STAT_ROWS, LANES), 0)
    for i in range(4):
        ref, slot = (own_ref, other_ref)[i // 2], i % 2
        for h in range(GROUP):
            columns = slice(h * LANES, (h + 1) * LANES)
            ref[slot, h * POS : (h + 1) * POS, :] = q[i, :, columns]
            grad = (g[i, :, columns].astype(f32) * sign).astype(bf16)
            ref[slot, TILE + h * POS : TILE + (h + 1) * POS, :] = grad
        keep = head_of == heads[i] * GROUP + lane // POS
        block = jnp.zeros((STAT_ROWS, LANES), f32)
        for n, rows in enumerate((lse_rows, delta_rows)):
            line = jnp.sum(jnp.where(keep, rows, 0.0), axis=0, keepdims=True)
            block = jnp.where(row == 2 * n, line[:, :LANES], block)
            block = jnp.where(row == 2 * n + 1, line[:, LANES:], block)
        ref[slot, 2 * TILE :, :] = block.astype(bf16)


def join_kernel(own_ref, other_ref, same_ref, odd_ref):
    for i, ref in enumerate((same_ref, odd_ref)):
        ref[0] = own_ref[i]
        ref[1] = other_ref[i]


def row_stats(lengths_ref, block, k, j):
    block = block.astype(f32)
    lse = jnp.concatenate([block[0:1], block[1:2]], axis=1) * LOG2E
    delta = jnp.concatenate([block[2:3], block[3:4]], axis=1)
    core = lax.axis_index("pair")
    response = core + j - 2 * core * j
    x = (lax.axis_index("x") + X - k) % X
    position = (lax.axis_index("y") * X + x) * POS + lax.broadcasted_iota(jnp.int32, (1, TILE), 1) % POS
    return jnp.where(position < lengths_ref[0, 1 + response], lse, DEAD), delta, position


def cell(key, value, query, grad, lse, delta, allowed=None):
    scores = dot(key, query, ((1,), (1,)))
    weights = jnp.exp2(scores * (SCALE * LOG2E) - lse)
    if allowed is not None:
        weights = jnp.where(allowed, weights, 0.0)
    weight_grads = dot(value, grad, ((1,), (1,)))
    score_grads = (weights * (weight_grads - delta)).astype(bf16)
    return weights.astype(bf16), score_grads


def prompt_kernel(lengths_ref, q0, q1, q2, q3, kv_ref, acc_ref, out_ref, rows_ref, key_acc, value_acc):
    for k, ref in enumerate((q0, q1, q2, q3)):
        rows_ref[2 * k : 2 * k + 2] = ref[...]
    key_acc[...] = jnp.zeros_like(key_acc)
    value_acc[...] = jnp.zeros_like(value_acc)
    per = 8
    rows = per * PROMPT_HALF

    @pl.loop(0, 2 * X)
    def _(tile):
        lse, delta, _ = row_stats(lengths_ref, rows_ref[tile, 2 * TILE :, :], tile // 2, tile % 2)
        query = rows_ref[tile, 0:TILE, :]
        grad = rows_ref[tile, TILE : 2 * TILE, :]
        total = None
        for c in range(CTX_N // per):
            at = slice(c * per, (c + 1) * per)
            key = kv_ref[at, 0:PROMPT_HALF, :].reshape(rows, LANES)
            value = kv_ref[at, PROMPT_HALF : 2 * PROMPT_HALF, :].reshape(rows, LANES)
            weights, score_grads = cell(key, value, query, grad, lse, delta)
            at = slice(c * rows, (c + 1) * rows)
            value_acc[at, :] += dot(weights, grad, ((1,), (0,)))
            key_acc[at, :] += dot(score_grads, query, ((1,), (0,)))
            term = dot(score_grads, key, ((0,), (0,)))
            total = term if total is None else total + term
        acc_ref[tile] = total

    shape = (CTX_N, PROMPT_HALF, LANES)
    out_ref[:, 0:PROMPT_HALF, :] = (key_acc[...] * SCALE).astype(bf16).reshape(shape)
    out_ref[:, PROMPT_HALF:, :] = value_acc[...].astype(bf16).reshape(shape)


def resp_kernel(
    lengths_ref, q0, q1, q2, q3, kv_ref, side_ref, acc_ref, prompt_ref,
    out_ref, d0, d1, d2, d3, gate_ref, key_acc, value_acc,
):
    margin = jnp.sum(kv_ref[:, KV_ROWS:, :].astype(f32), axis=(0, 1), keepdims=True).reshape(1, LANES)
    margin = jnp.sum(margin, axis=1, keepdims=True)
    gate_ref[...] = jnp.broadcast_to(beta_coef * jax.nn.sigmoid(-beta_coef * margin), gate_ref.shape)
    out_ref[:, 0 : 2 * PROMPT_HALF, :] = prompt_ref[...]
    key_acc[...] = jnp.zeros_like(key_acc)
    value_acc[...] = jnp.zeros_like(value_acc)
    half = lax.axis_index("x") // 2
    per = 16
    rows = per * RESP_HALF
    for j, (source, first) in enumerate(((kv_ref, 2 * PROMPT_HALF), (side_ref, 0))):
        for k, (q_ref, d_ref) in enumerate(((q0, d0), (q1, d1), (q2, d2), (q3, d3))):
            lse, delta, position = row_stats(lengths_ref, q_ref[j, 2 * TILE :, :], k, j)
            query = q_ref[j, 0:TILE, :]
            grad = q_ref[j, TILE : 2 * TILE, :]
            total = acc_ref[2 * k + j]
            for c in range(CTX_N // per):
                at = slice(c * per, (c + 1) * per)
                key = source[at, first : first + RESP_HALF, :].reshape(rows, LANES)
                value = source[at, first + RESP_HALF : first + SIDE, :].reshape(rows, LANES)
                index = lax.broadcasted_iota(jnp.int32, (rows, 1), 0)
                key_position = (c * per + index // RESP_HALF) * POS + half * RESP_HALF + index % RESP_HALF
                weights, score_grads = cell(key, value, query, grad, lse, delta, key_position <= position)
                first_row = (j * (CTX_N // per) + c) * rows
                at = slice(first_row, first_row + rows)
                value_acc[at, :] += dot(weights, grad, ((1,), (0,)))
                key_acc[at, :] += dot(score_grads, query, ((1,), (0,)))
                total += dot(score_grads, key, ((0,), (0,)))
            d_ref[j] = (total * SCALE).astype(bf16)

        at = slice(j * CTX_N * RESP_HALF, (j + 1) * CTX_N * RESP_HALF)
        shape = (CTX_N, RESP_HALF, LANES)
        to = 2 * PROMPT_HALF + j * SIDE
        out_ref[:, to : to + RESP_HALF, :] = (key_acc[at, :] * SCALE).astype(bf16).reshape(shape)
        out_ref[:, to + RESP_HALF : to + SIDE, :] = value_acc[at, :].astype(bf16).reshape(shape)


def kv_final_kernel(lengths_ref, gate_ref, part_ref, pk_ref, pv_ref, rk_ref, rv_ref):
    gate = gate_ref[0:1, 0:1]
    core = lax.axis_index("pair")
    ctx = lax.axis_index("y") * X + lax.axis_index("x")
    for x in range(X):
        odd, half = x % 2, x // 2
        columns = slice(odd * LANES, (odd + 1) * LANES)
        total = part_ref[x].astype(f32)
        for y in range(1, ROWS_Y):
            total += part_ref[y * X + x].astype(f32)
        total = total * gate
        rows = slice(half * PROMPT_HALF, (half + 1) * PROMPT_HALF)
        index = ctx * 2 * PROMPT_HALF + half * PROMPT_HALF
        live = index + lax.broadcasted_iota(jnp.int32, (PROMPT_HALF, LANES), 0) < lengths_ref[0, 0]
        pk_ref[0, rows, columns] = jnp.where(live, total[0:PROMPT_HALF], 0.0).astype(bf16)
        pv_ref[0, rows, columns] = jnp.where(live, total[PROMPT_HALF : 2 * PROMPT_HALF], 0.0).astype(bf16)
        rows = slice(half * RESP_HALF, (half + 1) * RESP_HALF)
        for j in range(2):
            response = core + j - 2 * core * j
            at = 2 * PROMPT_HALF + j * SIDE
            rk_ref[0, response, rows, columns] = total[at : at + RESP_HALF].astype(bf16)
            rv_ref[0, response, rows, columns] = total[at + RESP_HALF : at + SIDE].astype(bf16)


def query_final_kernel(gate_ref, d0, d1, d2, d3, out_ref):
    gate = gate_ref[0:1, 0:1]
    core = lax.axis_index("pair")
    even = lax.axis_index("x") % 2 == 0
    for j in range(2):
        response = core + j - 2 * core * j
        for h in range(GROUP):
            rows = slice(h * POS, (h + 1) * POS)
            same = gate * (d0[j, rows, :].astype(f32) + d2[j, rows, :].astype(f32))
            odd = gate * (d1[j, rows, :].astype(f32) + d3[j, rows, :].astype(f32))
            first, second = jnp.where(even, same, odd), jnp.where(even, odd, same)
            out_ref[0, response, :, h * LANES : (h + 1) * LANES] = first.astype(bf16)
            out_ref[0, response, :, (GROUP + h) * LANES : (GROUP + h + 1) * LANES] = second.astype(bf16)


def swap(values):
    return lax.all_to_all(values, CTX, split_axis=0, concat_axis=0, tiled=True)


def cross(values):
    return lax.ppermute(values, "pair", [(0, 1), (1, 0)])


def shift(values, by):
    return lax.ppermute(values, "x", [(i, (i + by) % X) for i in range(X)])


def per_device(
    prompt_keys,
    prompt_values,
    queries,
    resp_keys,
    resp_values,
    resp_grads,
    resp_lse,
    resp_delta,
    logratio,
    lengths,
):
    shape = jax.ShapeDtypeStruct
    kv = call(
        kv_pack_kernel,
        shape((CTX_N, KV_ROWS + 16, LANES), bf16),
        "aaaaaa",
        size=2 * 2**20,
        scratch=(
            pltpu.SMEM((1, 3), jnp.int32),
            pltpu.VMEM((2, POS), f32),
            pltpu.VMEM((2 * PROMPT_HALF, 2 * LANES), bf16),
            pltpu.VMEM((2 * PROMPT_HALF, 2 * LANES), bf16),
            pltpu.VMEM((POS, X * LANES), bf16),
            pltpu.VMEM((POS, X * LANES), bf16),
            pltpu.SemaphoreType.DMA((6,)),
        ),
    )(lengths, logratio, prompt_keys, prompt_values, resp_keys, resp_values)
    kv = swap(kv)

    block = shape((2, QUERY_ROWS, LANES), bf16)
    own, other = call(
        query_pack_kernel,
        (block, block),
        "aaaa",
        size=2 * 2**20,
        scratch=(
            pltpu.VMEM((4, POS, GROUP * LANES), bf16),
            pltpu.VMEM((4, POS, GROUP * LANES), bf16),
            pltpu.VMEM((POS, X * GROUP), bf16),
            pltpu.VMEM((POS, X * GROUP), bf16),
            pltpu.SemaphoreType.DMA((10,)),
        ),
    )(queries, resp_grads, resp_lse, resp_delta)
    same, odd = call(join_kernel, (block, block), "vv", size=2**20)(own, cross(other))
    rows = (same, shift(odd, 1), shift(same, 2), shift(odd, 3))

    side = cross(kv[:, KV_ROWS - SIDE : KV_ROWS, :])
    acc, prompt_part = call(
        prompt_kernel,
        (shape((2 * X, TILE, LANES), f32), shape((CTX_N, 2 * PROMPT_HALF, LANES), bf16)),
        "svvvvv",
        scratch=(
            pltpu.VMEM((2 * X, QUERY_ROWS, LANES), bf16),
            pltpu.VMEM((1024, LANES), f32),
            pltpu.VMEM((1024, LANES), f32),
        ),
        flops=5 * 2 * 2048 * 1024 * 128 * 2,
        size=3 * 2**20,
    )(lengths, *rows, kv)
    part, *grads, gate = call(
        resp_kernel,
        (shape((CTX_N, KV_ROWS, LANES), bf16),)
        + (shape((2, TILE, LANES), bf16),) * X
        + (shape((8, LANES), f32),),
        "svvvvvvvv",
        scratch=(pltpu.VMEM((1024, LANES), f32), pltpu.VMEM((1024, LANES), f32)),
        flops=5 * 2 * 1024 * 1024 * 128 * 2,
        size=3 * 2**20,
    )(lengths, *rows, kv, side, acc, prompt_part)
    part = swap(part)
    back = [grads[0]] + [shift(grads[k], X - k) for k in range(1, X)]
    query_grad = call(query_final_kernel, shape((1, 2, POS, 2 * GROUP * LANES), bf16), "vvvvv", size=2**20)(
        gate, *back
    )
    outs = (shape((1, 2 * PROMPT_HALF, 2 * LANES), bf16),) * 2 + (shape((1, 2, POS, 2 * LANES), bf16),) * 2
    pk_grad, pv_grad, key_grad, value_grad = call(kv_final_kernel, outs, "svv", size=2**20)(lengths, gate, part)
    return pk_grad, pv_grad, query_grad, key_grad, value_grad, gate[0, 0:1]


def solution(mesh):
    batch, pair, ctx = mesh.devices.shape
    split = Mesh(mesh.devices.reshape(batch, pair, ctx // X, X), ("batch", "pair", "y", "x"))
    prompt_spec = P("batch", CTX, "pair")
    resp_spec = P("batch", "pair", CTX, None)
    out_spec = P("batch", None, CTX, "pair")
    return jax.shard_map(
        per_device,
        mesh=split,
        in_specs=(
            prompt_spec,
            prompt_spec,
            resp_spec,
            resp_spec,
            resp_spec,
            resp_spec,
            resp_spec,
            resp_spec,
            P("batch", None, CTX),
            P("batch", None),
        ),
        out_specs=(prompt_spec, prompt_spec, out_spec, out_spec, out_spec, P("batch")),
        check_vma=False,
    )
```

```python
import jax
import jax.numpy as jnp
from jax import lax
from jax.experimental import pallas as pl
from jax.experimental.pallas import tpu as pltpu
from jax.sharding import Mesh, PartitionSpec as P

beta_coef = 0.1
f32, bf16 = jnp.float32, jnp.bfloat16
LANES = 128
CTX = ("y", "x")

X = 4
ROWS_Y = 8
CTX_N = 32
POS = 32
GROUP = 8
TILE = POS * GROUP
PROMPT_HALF = 32
RESP_HALF = 16
STAT_ROWS = 16
QUERY_ROWS = 2 * TILE + STAT_ROWS
SIDE = 2 * RESP_HALF
KV_ROWS = 2 * PROMPT_HALF + 2 * SIDE
LOG2E = 1.4426950408889634
SCALE = LANES**-0.5
DEAD = 1e30
BLOCK = 256
MARGIN_ROWS = 8


def dot(a, b, dims):
    return lax.dot_general(a, b, (dims, ((), ())), preferred_element_type=f32)


def call(kernel, out_shape, spaces, flops=0, scratch=(), size=0, limit=24):
    space = {"v": pltpu.VMEM, "s": pltpu.SMEM, "a": pl.ANY}
    many = isinstance(out_shape, tuple)
    out_spec = pl.BlockSpec(memory_space=pltpu.VMEM)
    return pl.pallas_call(
        kernel,
        out_shape=out_shape,
        in_specs=[pl.BlockSpec(memory_space=space[s]) for s in spaces],
        out_specs=tuple(out_spec for _ in out_shape) if many else out_spec,
        scratch_shapes=list(scratch),
        compiler_params=pltpu.CompilerParams(vmem_limit_bytes=limit * 2**20),
        cost_estimate=pl.CostEstimate(flops=flops, bytes_accessed=size, transcendentals=0),
    )


def fetch(pairs, sems):
    copies = [pltpu.make_async_copy(a, b, sems.at[i]) for i, (a, b) in enumerate(pairs)]
    for copy in copies:
        copy.start()
    for copy in copies:
        copy.wait()


def kv_pack_kernel(
    lengths_hbm, logratio_hbm, pk_hbm, pv_hbm, rk_hbm, rv_hbm, kv_ref, lengths, logratio, pk, pv, rk, rv, sems
):
    pairs = (
        (lengths_hbm, lengths),
        (logratio_hbm.at[0], logratio),
        (pk_hbm.at[0], pk),
        (pv_hbm.at[0], pv),
        (rk_hbm.at[0, 0], rk),
        (rv_hbm.at[0, 0], rv),
    )
    fetch(pairs, sems)
    first_core = lax.axis_index("pair") == 0
    ctx = lax.axis_index("y") * X + lax.axis_index("x")
    position = ctx * POS + lax.broadcasted_iota(jnp.int32, (1, POS), 1)
    chosen = jnp.where(position < lengths[0, 1], logratio[0:1, :], 0.0)
    rejected = jnp.where(position < lengths[0, 2], logratio[1:2, :], 0.0)
    margin = jnp.sum(chosen - rejected, axis=1, keepdims=True)
    high = margin.astype(bf16).astype(f32)
    middle = (margin - high).astype(bf16).astype(f32)
    low = margin - high - middle
    lane = lax.broadcasted_iota(jnp.int32, (MARGIN_ROWS, LANES), 1)
    row = lax.broadcasted_iota(jnp.int32, (MARGIN_ROWS, LANES), 0)
    block = jnp.where(lane == 0, high, jnp.where(lane == 1, middle, jnp.where(lane == 2, low, 0.0)))
    block = jnp.where(row == 0, block, 0.0).astype(bf16)
    for x in range(X):
        odd, half = x % 2, x // 2
        columns = slice(odd * LANES, (odd + 1) * LANES)
        others = slice((2 + odd) * LANES, (3 + odd) * LANES)
        rows = slice(half * PROMPT_HALF, (half + 1) * PROMPT_HALF)
        index = ctx * 2 * PROMPT_HALF + half * PROMPT_HALF
        live = index + lax.broadcasted_iota(jnp.int32, (PROMPT_HALF, LANES), 0) < lengths[0, 0]
        parts = [jnp.where(live, pk[rows, columns].astype(f32), 0.0).astype(bf16), pv[rows, columns]]
        rows = slice(half * RESP_HALF, (half + 1) * RESP_HALF)
        low_head = [ref[rows, columns].astype(f32) for ref in (rk, rv)]
        high_head = [ref[rows, others].astype(f32) for ref in (rk, rv)]
        parts += [jnp.where(first_core, a, b).astype(bf16) for a, b in zip(low_head, high_head)]
        parts += [jnp.where(first_core, b, a).astype(bf16) for a, b in zip(low_head, high_head)]
        parts += [block]
        for y in range(ROWS_Y):
            at = 0
            for part in parts:
                kv_ref[y * X + x, at : at + part.shape[0], :] = part
                at += part.shape[0]


def query_pack_kernel(q_hbm, g_hbm, lse_hbm, delta_hbm, own_ref, other_ref, q, g, lse, delta, sems):
    core, parity = lax.axis_index("pair"), lax.axis_index("x") % 2
    pairs = [(lse_hbm.at[0, 0], lse), (delta_hbm.at[0, 0], delta)]
    heads = []
    for i in range(4):
        head = 2 * (core if i < 2 else 1 - core) + (parity + i) % 2
        heads.append(head)
        columns = pl.ds(pl.multiple_of(head * GROUP * LANES, GROUP * LANES), GROUP * LANES)
        pairs += [(q_hbm.at[0, 0, :, columns], q.at[i]), (g_hbm.at[0, 0, :, columns], g.at[i])]
    fetch(pairs, sems)
    sign = jnp.where(core == 0, -1.0, 1.0).astype(f32)

    count = X * GROUP
    lane = lax.broadcasted_iota(jnp.int32, (POS, TILE), 1)
    spread = (lane % POS == lax.broadcasted_iota(jnp.int32, (POS, TILE), 0)).astype(bf16)
    head_of = lax.broadcasted_iota(jnp.int32, (count, TILE), 0)
    lane = lax.broadcasted_iota(jnp.int32, (count, TILE), 1)
    lse_rows = dot(lse[...], spread, ((0,), (0,)))
    delta_rows = dot(delta[...], spread, ((0,), (0,))) * sign
    row = lax.broadcasted_iota(jnp.int32, (STAT_ROWS, LANES), 0)
    for i in range(4):
        ref, slot = (own_ref, other_ref)[i // 2], i % 2
        for h in range(GROUP):
            columns = slice(h * LANES, (h + 1) * LANES)
            ref[slot, h * POS : (h + 1) * POS, :] = q[i, :, columns]
            grad = (g[i, :, columns].astype(f32) * sign).astype(bf16)
            ref[slot, TILE + h * POS : TILE + (h + 1) * POS, :] = grad
        keep = head_of == heads[i] * GROUP + lane // POS
        block = jnp.zeros((STAT_ROWS, LANES), f32)
        for n, rows in enumerate((lse_rows, delta_rows)):
            line = jnp.sum(jnp.where(keep, rows, 0.0), axis=0, keepdims=True)
            block = jnp.where(row == 2 * n, line[:, :LANES], block)
            block = jnp.where(row == 2 * n + 1, line[:, LANES:], block)
        ref[slot, 2 * TILE :, :] = block.astype(bf16)


def join_kernel(own_ref, other_ref, same_ref, odd_ref):
    for i, ref in enumerate((same_ref, odd_ref)):
        ref[0] = own_ref[i]
        ref[1] = other_ref[i]


def row_stats(lengths_ref, block, k, j):
    block = block.astype(f32)
    lse = jnp.concatenate([block[0:1], block[1:2]], axis=1) * LOG2E
    delta = jnp.concatenate([block[2:3], block[3:4]], axis=1)
    core = lax.axis_index("pair")
    response = core + j - 2 * core * j
    x = (lax.axis_index("x") + X - k) % X
    position = (lax.axis_index("y") * X + x) * POS + lax.broadcasted_iota(jnp.int32, (1, TILE), 1) % POS
    return jnp.where(position < lengths_ref[0, 1 + response], lse, DEAD), delta, position


def cell(key, value, query, grad, lse, delta, allowed=None):
    scores = dot(key, query, ((1,), (1,)))
    weights = jnp.exp2(scores * (SCALE * LOG2E) - lse)
    if allowed is not None:
        weights = jnp.where(allowed, weights, 0.0)
    weight_grads = dot(value, grad, ((1,), (1,)))
    score_grads = (weights * (weight_grads - delta)).astype(bf16)
    return weights.astype(bf16), score_grads


def staged(blocks, first, second):
    for i, block in enumerate(blocks):
        first(*block, i % 2)
        if i:
            second(*blocks[i - 1], (i - 1) % 2)
    second(*blocks[-1], (len(blocks) - 1) % 2)


def gather_rows(refs, query_rows, grad_rows):
    for k, ref in enumerate(refs):
        for j in range(2):
            at = slice((j * X + k) * TILE, (j * X + k + 1) * TILE)
            query_rows[at, :] = ref[j, 0:TILE, :]
            grad_rows[at, :] = ref[j, TILE : 2 * TILE, :]


def tile_rows(tile):
    return slice(tile * TILE, (tile + 1) * TILE)


def prompt_kernel(
    lengths_ref, q0, q1, q2, q3, kv_ref, acc_ref, out_ref, query_rows, grad_rows, weights, score_grads
):
    refs = (q0, q1, q2, q3)
    gather_rows(refs, query_rows, grad_rows)
    stats = [row_stats(lengths_ref, refs[t % X][t // X, 2 * TILE :, :], t % X, t // X) for t in range(2 * X)]
    per = BLOCK // PROMPT_HALF

    def keys_of(c):
        return kv_ref[c * per : (c + 1) * per, 0:PROMPT_HALF, :].reshape(BLOCK, LANES)

    def first(c, slot):
        key = keys_of(c)
        value = kv_ref[c * per : (c + 1) * per, PROMPT_HALF : 2 * PROMPT_HALF, :].reshape(BLOCK, LANES)
        for t in range(2 * X):
            at = tile_rows(t)
            lse, delta, _ = stats[t]
            weights[slot, :, at], score_grads[slot, :, at] = cell(
                key, value, query_rows[at, :], grad_rows[at, :], lse, delta
            )

    def second(c, slot):
        value_grad = dot(weights[slot], grad_rows[...], ((1,), (0,)))
        key_grad = dot(score_grads[slot], query_rows[...], ((1,), (0,))) * SCALE
        shape = (per, PROMPT_HALF, LANES)
        to = slice(c * per, (c + 1) * per)
        out_ref[to, 0:PROMPT_HALF, :] = key_grad.astype(bf16).reshape(shape)
        out_ref[to, PROMPT_HALF:, :] = value_grad.astype(bf16).reshape(shape)
        key = keys_of(c)
        for t in range(2 * X):
            term = dot(score_grads[slot, :, tile_rows(t)], key, ((0,), (0,)))
            acc_ref[t] = term if c == 0 else acc_ref[t] + term

    staged([(c,) for c in range(CTX_N // per)], first, second)


def resp_kernel(
    lengths_ref, q0, q1, q2, q3, kv_ref, side_ref, acc_ref, prompt_ref,
    out_ref, d0, d1, d2, d3, gate_ref, query_rows, grad_rows, weights, score_grads, acc,
):
    margin = jnp.sum(kv_ref[:, KV_ROWS:, :].astype(f32), axis=(0, 1), keepdims=True).reshape(1, LANES)
    margin = jnp.sum(margin, axis=1, keepdims=True)
    gate_ref[...] = jnp.broadcast_to(beta_coef * jax.nn.sigmoid(-beta_coef * margin), gate_ref.shape)
    out_ref[:, 0 : 2 * PROMPT_HALF, :] = prompt_ref[...]
    refs, grads = (q0, q1, q2, q3), (d0, d1, d2, d3)
    gather_rows(refs, query_rows, grad_rows)
    stats = [row_stats(lengths_ref, refs[t % X][t // X, 2 * TILE :, :], t % X, t // X) for t in range(2 * X)]
    half = lax.axis_index("x") // 2
    per = BLOCK // RESP_HALF
    last = CTX_N // per - 1
    sources = ((kv_ref, 2 * PROMPT_HALF), (side_ref, 0))

    def rows_of(j, c, at):
        ref, start = sources[j]
        return ref[c * per : (c + 1) * per, start + at : start + at + RESP_HALF, :].reshape(BLOCK, LANES)

    def first(j, c, slot):
        key, value = rows_of(j, c, 0), rows_of(j, c, RESP_HALF)
        index = lax.broadcasted_iota(jnp.int32, (BLOCK, 1), 0)
        key_position = (c * per + index // RESP_HALF) * POS + half * RESP_HALF + index % RESP_HALF
        for k in range(X):
            at, to = tile_rows(j * X + k), tile_rows(k)
            lse, delta, position = stats[j * X + k]
            weights[slot, :, to], score_grads[slot, :, to] = cell(
                key, value, query_rows[at, :], grad_rows[at, :], lse, delta, key_position <= position
            )

    def second(j, c, slot):
        rows = slice(j * X * TILE, (j + 1) * X * TILE)
        value_grad = dot(weights[slot], grad_rows[rows, :], ((1,), (0,)))
        key_grad = dot(score_grads[slot], query_rows[rows, :], ((1,), (0,))) * SCALE
        shape = (per, RESP_HALF, LANES)
        to = slice(c * per, (c + 1) * per)
        start = 2 * PROMPT_HALF + j * SIDE
        out_ref[to, start : start + RESP_HALF, :] = key_grad.astype(bf16).reshape(shape)
        out_ref[to, start + RESP_HALF : start + SIDE, :] = value_grad.astype(bf16).reshape(shape)
        key = rows_of(j, c, 0)
        for k in range(X):
            total = dot(score_grads[slot, :, tile_rows(k)], key, ((0,), (0,)))
            total += acc_ref[j * X + k] if c == 0 else acc[k]
            if c == last:
                grads[k][j] = (total * SCALE).astype(bf16)
            else:
                acc[k] = total

    staged([(j, c) for j in range(2) for c in range(CTX_N // per)], first, second)


def kv_final_kernel(lengths_ref, gate_ref, part_ref, pk_ref, pv_ref, rk_ref, rv_ref):
    gate = gate_ref[0:1, 0:1]
    core = lax.axis_index("pair")
    ctx = lax.axis_index("y") * X + lax.axis_index("x")
    for x in range(X):
        odd, half = x % 2, x // 2
        columns = slice(odd * LANES, (odd + 1) * LANES)
        total = part_ref[x].astype(f32)
        for y in range(1, ROWS_Y):
            total += part_ref[y * X + x].astype(f32)
        total = total * gate
        rows = slice(half * PROMPT_HALF, (half + 1) * PROMPT_HALF)
        index = ctx * 2 * PROMPT_HALF + half * PROMPT_HALF
        live = index + lax.broadcasted_iota(jnp.int32, (PROMPT_HALF, LANES), 0) < lengths_ref[0, 0]
        pk_ref[0, rows, columns] = jnp.where(live, total[0:PROMPT_HALF], 0.0).astype(bf16)
        pv_ref[0, rows, columns] = jnp.where(live, total[PROMPT_HALF : 2 * PROMPT_HALF], 0.0).astype(bf16)
        rows = slice(half * RESP_HALF, (half + 1) * RESP_HALF)
        for j in range(2):
            response = core + j - 2 * core * j
            at = 2 * PROMPT_HALF + j * SIDE
            rk_ref[0, response, rows, columns] = total[at : at + RESP_HALF].astype(bf16)
            rv_ref[0, response, rows, columns] = total[at + RESP_HALF : at + SIDE].astype(bf16)


def query_final_kernel(gate_ref, d0, d1, d2, d3, out_ref):
    gate = gate_ref[0:1, 0:1]
    core = lax.axis_index("pair")
    even = lax.axis_index("x") % 2 == 0
    for j in range(2):
        response = core + j - 2 * core * j
        for h in range(GROUP):
            rows = slice(h * POS, (h + 1) * POS)
            same = gate * (d0[j, rows, :].astype(f32) + d2[j, rows, :].astype(f32))
            odd = gate * (d1[j, rows, :].astype(f32) + d3[j, rows, :].astype(f32))
            first, second = jnp.where(even, same, odd), jnp.where(even, odd, same)
            out_ref[0, response, :, h * LANES : (h + 1) * LANES] = first.astype(bf16)
            out_ref[0, response, :, (GROUP + h) * LANES : (GROUP + h + 1) * LANES] = second.astype(bf16)


def swap(values):
    return lax.all_to_all(values, CTX, split_axis=0, concat_axis=0, tiled=True)


def cross(values):
    return lax.ppermute(values, "pair", [(0, 1), (1, 0)])


def shift(values, by):
    return lax.ppermute(values, "x", [(i, (i + by) % X) for i in range(X)])


def prompt_call(lengths, rows, kv):
    shape = jax.ShapeDtypeStruct
    return call(
        prompt_kernel,
        (shape((2 * X, TILE, LANES), f32), shape((CTX_N, 2 * PROMPT_HALF, LANES), bf16)),
        "svvvvv",
        scratch=(
            pltpu.VMEM((2 * X * TILE, LANES), bf16),
            pltpu.VMEM((2 * X * TILE, LANES), bf16),
            pltpu.VMEM((2, BLOCK, 2 * X * TILE), bf16),
            pltpu.VMEM((2, BLOCK, 2 * X * TILE), bf16),
        ),
        flops=5 * 2 * 2048 * 1024 * 128 * 2,
        size=3 * 2**20,
    )(lengths, *rows, kv)


def resp_call(lengths, rows, kv, side, acc, prompt_part):
    shape = jax.ShapeDtypeStruct
    return call(
        resp_kernel,
        (shape((CTX_N, KV_ROWS, LANES), bf16),)
        + (shape((2, TILE, LANES), bf16),) * X
        + (shape((8, LANES), f32),),
        "svvvvvvvv",
        scratch=(
            pltpu.VMEM((2 * X * TILE, LANES), bf16),
            pltpu.VMEM((2 * X * TILE, LANES), bf16),
            pltpu.VMEM((2, BLOCK, X * TILE), bf16),
            pltpu.VMEM((2, BLOCK, X * TILE), bf16),
            pltpu.VMEM((X, TILE, LANES), f32),
        ),
        flops=5 * 2 * 1024 * 1024 * 128 * 2,
        size=3 * 2**20,
    )(lengths, *rows, kv, side, acc, prompt_part)


def per_device(
    prompt_keys,
    prompt_values,
    queries,
    resp_keys,
    resp_values,
    resp_grads,
    resp_lse,
    resp_delta,
    logratio,
    lengths,
):
    shape = jax.ShapeDtypeStruct
    kv = call(
        kv_pack_kernel,
        shape((CTX_N, KV_ROWS + MARGIN_ROWS, LANES), bf16),
        "aaaaaa",
        size=2 * 2**20,
        limit=60,
        scratch=(
            pltpu.SMEM((1, 3), jnp.int32),
            pltpu.VMEM((2, POS), f32),
            pltpu.VMEM((2 * PROMPT_HALF, 2 * LANES), bf16),
            pltpu.VMEM((2 * PROMPT_HALF, 2 * LANES), bf16),
            pltpu.VMEM((POS, X * LANES), bf16),
            pltpu.VMEM((POS, X * LANES), bf16),
            pltpu.SemaphoreType.DMA((6,)),
        ),
    )(lengths, logratio, prompt_keys, prompt_values, resp_keys, resp_values)
    kv = swap(kv)

    block = shape((2, QUERY_ROWS, LANES), bf16)
    own, other = call(
        query_pack_kernel,
        (block, block),
        "aaaa",
        size=2 * 2**20,
        scratch=(
            pltpu.VMEM((4, POS, GROUP * LANES), bf16),
            pltpu.VMEM((4, POS, GROUP * LANES), bf16),
            pltpu.VMEM((POS, X * GROUP), bf16),
            pltpu.VMEM((POS, X * GROUP), bf16),
            pltpu.SemaphoreType.DMA((10,)),
        ),
    )(queries, resp_grads, resp_lse, resp_delta)
    same, odd = call(join_kernel, (block, block), "vv", size=2**20)(own, cross(other))
    rows = (same, shift(odd, 1), shift(same, 2), shift(odd, 3))

    side = cross(kv[:, KV_ROWS - SIDE : KV_ROWS, :])
    acc, prompt_part = prompt_call(lengths, rows, kv)
    part, *grads, gate = resp_call(lengths, rows, kv, side, acc, prompt_part)
    part = swap(part)
    back = [grads[0]] + [shift(grads[k], X - k) for k in range(1, X)]
    query_grad = call(query_final_kernel, shape((1, 2, POS, 2 * GROUP * LANES), bf16), "vvvvv", size=2**20)(
        gate, *back
    )
    outs = (shape((1, 2 * PROMPT_HALF, 2 * LANES), bf16),) * 2 + (shape((1, 2, POS, 2 * LANES), bf16),) * 2
    pk_grad, pv_grad, key_grad, value_grad = call(kv_final_kernel, outs, "svv", size=2**20)(lengths, gate, part)
    return pk_grad, pv_grad, query_grad, key_grad, value_grad, gate[0, 0:1]


def solution(mesh):
    batch, pair, ctx = mesh.devices.shape
    split = Mesh(mesh.devices.reshape(batch, pair, ctx // X, X), ("batch", "pair", "y", "x"))
    prompt_spec = P("batch", CTX, "pair")
    resp_spec = P("batch", "pair", CTX, None)
    out_spec = P("batch", None, CTX, "pair")
    return jax.shard_map(
        per_device,
        mesh=split,
        in_specs=(
            prompt_spec,
            prompt_spec,
            resp_spec,
            resp_spec,
            resp_spec,
            resp_spec,
            resp_spec,
            resp_spec,
            P("batch", None, CTX),
            P("batch", None),
        ),
        out_specs=(prompt_spec, prompt_spec, out_spec, out_spec, out_spec, P("batch")),
        check_vma=False,
    )
```

```python
import jax
import jax.numpy as jnp
from jax import lax
from jax.experimental import pallas as pl
from jax.experimental.pallas import tpu as pltpu
from jax.sharding import Mesh, PartitionSpec as P

beta_coef = 0.1
f32, bf16 = jnp.float32, jnp.bfloat16
LANES = 128
CTX = ("y", "x")

X = 4
ROWS_Y = 8
CTX_N = 32
POS = 32
GROUP = 8
TILE = POS * GROUP
PROMPT_HALF = 32
RESP_HALF = 16
STAT_ROWS = 16
QUERY_ROWS = 2 * TILE + STAT_ROWS
SIDE = 2 * RESP_HALF
KV_ROWS = 2 * PROMPT_HALF + 2 * SIDE
LOG2E = 1.4426950408889634
SCALE = LANES**-0.5
DEAD = 1e30
BLOCK = 512
MARGIN_ROWS = 8


def dot(a, b, dims):
    return lax.dot_general(a, b, (dims, ((), ())), preferred_element_type=f32)


def call(kernel, out_shape, spaces, flops=0, scratch=(), size=0, limit=24, out_spaces=""):
    space = {"v": pltpu.VMEM, "s": pltpu.SMEM, "a": pl.ANY}
    many = isinstance(out_shape, tuple)
    out_spaces = out_spaces or "v" * (len(out_shape) if many else 1)
    out_specs = tuple(pl.BlockSpec(memory_space=space[s]) for s in out_spaces)
    return pl.pallas_call(
        kernel,
        out_shape=out_shape,
        in_specs=[pl.BlockSpec(memory_space=space[s]) for s in spaces],
        out_specs=out_specs if many else out_specs[0],
        scratch_shapes=list(scratch),
        compiler_params=pltpu.CompilerParams(vmem_limit_bytes=limit * 2**20),
        cost_estimate=pl.CostEstimate(flops=flops, bytes_accessed=size, transcendentals=0),
    )


def fetch(pairs, sems):
    copies = [pltpu.make_async_copy(a, b, sems.at[i]) for i, (a, b) in enumerate(pairs)]
    for copy in copies:
        copy.start()
    for copy in copies:
        copy.wait()


def kv_pack_kernel(
    lengths_hbm, logratio_hbm, pk_hbm, pv_hbm, rk_hbm, rv_hbm, kv_ref, lengths, logratio, pk, pv, rk, rv, sems
):
    pairs = (
        (lengths_hbm, lengths),
        (logratio_hbm.at[0], logratio),
        (pk_hbm.at[0], pk),
        (pv_hbm.at[0], pv),
        (rk_hbm.at[0, 0], rk),
        (rv_hbm.at[0, 0], rv),
    )
    fetch(pairs, sems)
    first_core = lax.axis_index("pair") == 0
    ctx = lax.axis_index("y") * X + lax.axis_index("x")
    position = ctx * POS + lax.broadcasted_iota(jnp.int32, (1, POS), 1)
    chosen = jnp.where(position < lengths[0, 1], logratio[0:1, :], 0.0)
    rejected = jnp.where(position < lengths[0, 2], logratio[1:2, :], 0.0)
    margin = jnp.sum(chosen - rejected, axis=1, keepdims=True)
    high = margin.astype(bf16).astype(f32)
    middle = (margin - high).astype(bf16).astype(f32)
    low = margin - high - middle
    lane = lax.broadcasted_iota(jnp.int32, (MARGIN_ROWS, LANES), 1)
    row = lax.broadcasted_iota(jnp.int32, (MARGIN_ROWS, LANES), 0)
    block = jnp.where(lane == 0, high, jnp.where(lane == 1, middle, jnp.where(lane == 2, low, 0.0)))
    block = jnp.where(row == 0, block, 0.0).astype(bf16)
    for x in range(X):
        odd, half = x % 2, x // 2
        columns = slice(odd * LANES, (odd + 1) * LANES)
        others = slice((2 + odd) * LANES, (3 + odd) * LANES)
        rows = slice(half * PROMPT_HALF, (half + 1) * PROMPT_HALF)
        index = ctx * 2 * PROMPT_HALF + half * PROMPT_HALF
        live = index + lax.broadcasted_iota(jnp.int32, (PROMPT_HALF, LANES), 0) < lengths[0, 0]
        parts = [jnp.where(live, pk[rows, columns].astype(f32), 0.0).astype(bf16), pv[rows, columns]]
        rows = slice(half * RESP_HALF, (half + 1) * RESP_HALF)
        low_head = [ref[rows, columns].astype(f32) for ref in (rk, rv)]
        high_head = [ref[rows, others].astype(f32) for ref in (rk, rv)]
        parts += [jnp.where(first_core, a, b).astype(bf16) for a, b in zip(low_head, high_head)]
        parts += [jnp.where(first_core, b, a).astype(bf16) for a, b in zip(low_head, high_head)]
        parts += [block]
        for y in range(ROWS_Y):
            at = 0
            for part in parts:
                kv_ref[y * X + x, at : at + part.shape[0], :] = part
                at += part.shape[0]


def query_pack_kernel(q_hbm, g_hbm, lse_hbm, delta_hbm, own_ref, other_ref, q, g, lse, delta, sems):
    core, parity = lax.axis_index("pair"), lax.axis_index("x") % 2
    pairs = [(lse_hbm.at[0, 0], lse), (delta_hbm.at[0, 0], delta)]
    heads = []
    for i in range(4):
        head = 2 * (core if i < 2 else 1 - core) + (parity + i) % 2
        heads.append(head)
        columns = pl.ds(pl.multiple_of(head * GROUP * LANES, GROUP * LANES), GROUP * LANES)
        pairs += [(q_hbm.at[0, 0, :, columns], q.at[i]), (g_hbm.at[0, 0, :, columns], g.at[i])]
    fetch(pairs, sems)
    sign = jnp.where(core == 0, -1.0, 1.0).astype(f32)

    count = X * GROUP
    lane = lax.broadcasted_iota(jnp.int32, (POS, TILE), 1)
    spread = (lane % POS == lax.broadcasted_iota(jnp.int32, (POS, TILE), 0)).astype(bf16)
    head_of = lax.broadcasted_iota(jnp.int32, (count, TILE), 0)
    lane = lax.broadcasted_iota(jnp.int32, (count, TILE), 1)
    lse_rows = dot(lse[...], spread, ((0,), (0,)))
    delta_rows = dot(delta[...], spread, ((0,), (0,))) * sign
    row = lax.broadcasted_iota(jnp.int32, (STAT_ROWS, LANES), 0)
    for i in range(4):
        ref, slot = (own_ref, other_ref)[i // 2], i % 2
        for h in range(GROUP):
            columns = slice(h * LANES, (h + 1) * LANES)
            ref[slot, h * POS : (h + 1) * POS, :] = q[i, :, columns]
            grad = (g[i, :, columns].astype(f32) * sign).astype(bf16)
            ref[slot, TILE + h * POS : TILE + (h + 1) * POS, :] = grad
        keep = head_of == heads[i] * GROUP + lane // POS
        block = jnp.zeros((STAT_ROWS, LANES), f32)
        for n, rows in enumerate((lse_rows, delta_rows)):
            line = jnp.sum(jnp.where(keep, rows, 0.0), axis=0, keepdims=True)
            block = jnp.where(row == 2 * n, line[:, :LANES], block)
            block = jnp.where(row == 2 * n + 1, line[:, LANES:], block)
        ref[slot, 2 * TILE :, :] = block.astype(bf16)


def join_kernel(own_ref, other_ref, same_ref, odd_ref):
    for i, ref in enumerate((same_ref, odd_ref)):
        ref[0] = own_ref[i]
        ref[1] = other_ref[i]


def row_position(k):
    x = (lax.axis_index("x") + X - k) % X
    return (lax.axis_index("y") * X + x) * POS + lax.broadcasted_iota(jnp.int32, (1, TILE), 1) % POS


def row_stats(lengths_ref, block, k, j):
    block = block.astype(f32)
    lse = jnp.concatenate([block[0:1], block[1:2]], axis=1) * LOG2E
    delta = jnp.concatenate([block[2:3], block[3:4]], axis=1)
    core = lax.axis_index("pair")
    response = core + j - 2 * core * j
    return jnp.where(row_position(k) < lengths_ref[0, 1 + response], lse, DEAD), delta


def cell(key, value, query, grad, lse, delta, allowed=None):
    scores = dot(key, query, ((1,), (1,)))
    weights = jnp.exp2(scores * (SCALE * LOG2E) - lse)
    if allowed is not None:
        weights = jnp.where(allowed, weights, 0.0)
    weight_grads = dot(value, grad, ((1,), (1,)))
    score_grads = (weights * (weight_grads - delta)).astype(bf16)
    return weights.astype(bf16), score_grads


def staged(blocks, first, second):
    for i, block in enumerate(blocks):
        first(*block, i % 2)
        if i:
            second(*blocks[i - 1], (i - 1) % 2)
    second(*blocks[-1], (len(blocks) - 1) % 2)


def tile_rows(tile):
    return slice(tile * TILE, (tile + 1) * TILE)


def prompt_kernel(
    lengths_ref, q0, q1, q2, q3, kv_ref, out_ref, score_grads, query_rows, grad_rows, lse_ref, delta_ref, weights
):
    for k, ref in enumerate((q0, q1, q2, q3)):
        for j in range(2):
            t = j * X + k
            at = tile_rows(t)
            query_rows[at, :] = ref[j, 0:TILE, :]
            grad_rows[at, :] = ref[j, TILE : 2 * TILE, :]
            lse, delta = row_stats(lengths_ref, ref[j, 2 * TILE :, :], k, j)
            lse_ref[t : t + 1, :], delta_ref[t : t + 1, :] = lse, delta
    per = BLOCK // PROMPT_HALF

    def first(c, slot):
        rows = slice(c * per, (c + 1) * per)
        key = kv_ref[rows, 0:PROMPT_HALF, :].reshape(BLOCK, LANES)
        value = kv_ref[rows, PROMPT_HALF : 2 * PROMPT_HALF, :].reshape(BLOCK, LANES)
        for t in range(2 * X):
            at = tile_rows(t)
            weights[slot, :, at], score_grads[c * BLOCK : (c + 1) * BLOCK, at] = cell(
                key, value, query_rows[at, :], grad_rows[at, :], lse_ref[t : t + 1, :], delta_ref[t : t + 1, :]
            )

    def second(c, slot):
        value_grad = dot(weights[slot], grad_rows[...], ((1,), (0,)))
        key_grad = dot(score_grads[c * BLOCK : (c + 1) * BLOCK, :], query_rows[...], ((1,), (0,))) * SCALE
        shape = (per, PROMPT_HALF, LANES)
        to = slice(c * per, (c + 1) * per)
        out_ref[to, 0:PROMPT_HALF, :] = key_grad.astype(bf16).reshape(shape)
        out_ref[to, PROMPT_HALF:, :] = value_grad.astype(bf16).reshape(shape)

    staged([(c,) for c in range(CTX_N // per)], first, second)


def resp_kernel(
    kv_ref, side_ref, prompt_ref, query_rows, grad_rows, lse_ref, delta_ref,
    out_hbm, score_grads, gate_ref, weights, parts, sems,
):
    copies = [pltpu.make_async_copy(prompt_ref, out_hbm.at[:, 0 : 2 * PROMPT_HALF, :], sems.at[0])]
    copies[0].start()
    margin = jnp.sum(kv_ref[:, KV_ROWS:, :].astype(f32), axis=(0, 1), keepdims=True).reshape(1, LANES)
    margin = jnp.sum(margin, axis=1, keepdims=True)
    gate_ref[...] = jnp.broadcast_to(beta_coef * jax.nn.sigmoid(-beta_coef * margin), gate_ref.shape)
    half = lax.axis_index("x") // 2
    per = BLOCK // RESP_HALF
    blocks = CTX_N // per
    sources = ((kv_ref, 2 * PROMPT_HALF), (side_ref, 0))

    def first(j, c, slot):
        ref, start = sources[j]
        rows = slice(c * per, (c + 1) * per)
        key = ref[rows, start : start + RESP_HALF, :].reshape(BLOCK, LANES)
        value = ref[rows, start + RESP_HALF : start + SIDE, :].reshape(BLOCK, LANES)
        index = lax.broadcasted_iota(jnp.int32, (BLOCK, 1), 0)
        key_position = (c * per + index // RESP_HALF) * POS + half * RESP_HALF + index % RESP_HALF
        for k in range(X):
            t = j * X + k
            at, to = tile_rows(t), tile_rows(k)
            position = row_position(k)
            weights[slot, :, to], score_grads[j, c * BLOCK : (c + 1) * BLOCK, to] = cell(
                key,
                value,
                query_rows[at, :],
                grad_rows[at, :],
                lse_ref[t : t + 1, :],
                delta_ref[t : t + 1, :],
                key_position <= position,
            )

    def second(j, c, slot):
        rows = slice(j * X * TILE, (j + 1) * X * TILE)
        value_grad = dot(weights[slot], grad_rows[rows, :], ((1,), (0,)))
        key_grad = dot(score_grads[j, c * BLOCK : (c + 1) * BLOCK, :], query_rows[rows, :], ((1,), (0,))) * SCALE
        shape = (per, RESP_HALF, LANES)
        n = j * blocks + c
        parts[n, :, 0:RESP_HALF, :] = key_grad.astype(bf16).reshape(shape)
        parts[n, :, RESP_HALF:, :] = value_grad.astype(bf16).reshape(shape)
        start = 2 * PROMPT_HALF + j * SIDE
        to = out_hbm.at[c * per : (c + 1) * per, start : start + SIDE, :]
        copies.append(pltpu.make_async_copy(parts.at[n], to, sems.at[1 + n]))
        copies[-1].start()

    staged([(j, c) for j in range(2) for c in range(blocks)], first, second)
    for copy in copies:
        copy.wait()


def query_kernel(kv_ref, side_ref, prompt_grads, resp_grads, d0, d1, d2, d3):
    def keys(ref, start, count):
        return ref[:, start : start + count, :].reshape(CTX_N * count, LANES)

    prompt = keys(kv_ref, 0, PROMPT_HALF)
    resp = (keys(kv_ref, 2 * PROMPT_HALF, RESP_HALF), keys(side_ref, 0, RESP_HALF))
    for k, ref in enumerate((d0, d1, d2, d3)):
        for j in range(2):
            total = dot(prompt_grads[:, tile_rows(j * X + k)], prompt, ((0,), (0,)))
            total += dot(resp_grads[j, :, tile_rows(k)], resp[j], ((0,), (0,)))
            ref[j] = (total * SCALE).astype(bf16)


def kv_final_kernel(lengths_ref, gate_ref, part_ref, pk_ref, pv_ref, rk_ref, rv_ref):
    gate = gate_ref[0:1, 0:1]
    core = lax.axis_index("pair")
    ctx = lax.axis_index("y") * X + lax.axis_index("x")
    for x in range(X):
        odd, half = x % 2, x // 2
        columns = slice(odd * LANES, (odd + 1) * LANES)
        total = part_ref[x].astype(f32)
        for y in range(1, ROWS_Y):
            total += part_ref[y * X + x].astype(f32)
        total = total * gate
        rows = slice(half * PROMPT_HALF, (half + 1) * PROMPT_HALF)
        index = ctx * 2 * PROMPT_HALF + half * PROMPT_HALF
        live = index + lax.broadcasted_iota(jnp.int32, (PROMPT_HALF, LANES), 0) < lengths_ref[0, 0]
        pk_ref[0, rows, columns] = jnp.where(live, total[0:PROMPT_HALF], 0.0).astype(bf16)
        pv_ref[0, rows, columns] = jnp.where(live, total[PROMPT_HALF : 2 * PROMPT_HALF], 0.0).astype(bf16)
        rows = slice(half * RESP_HALF, (half + 1) * RESP_HALF)
        for j in range(2):
            response = core + j - 2 * core * j
            at = 2 * PROMPT_HALF + j * SIDE
            rk_ref[0, response, rows, columns] = total[at : at + RESP_HALF].astype(bf16)
            rv_ref[0, response, rows, columns] = total[at + RESP_HALF : at + SIDE].astype(bf16)


def query_final_kernel(gate_ref, d0, d1, d2, d3, out_ref):
    gate = gate_ref[0:1, 0:1]
    core = lax.axis_index("pair")
    even = lax.axis_index("x") % 2 == 0
    for j in range(2):
        response = core + j - 2 * core * j
        for h in range(GROUP):
            rows = slice(h * POS, (h + 1) * POS)
            same = gate * (d0[j, rows, :].astype(f32) + d2[j, rows, :].astype(f32))
            odd = gate * (d1[j, rows, :].astype(f32) + d3[j, rows, :].astype(f32))
            first, second = jnp.where(even, same, odd), jnp.where(even, odd, same)
            out_ref[0, response, :, h * LANES : (h + 1) * LANES] = first.astype(bf16)
            out_ref[0, response, :, (GROUP + h) * LANES : (GROUP + h + 1) * LANES] = second.astype(bf16)


def swap(values):
    return lax.all_to_all(values, CTX, split_axis=0, concat_axis=0, tiled=True)


def cross(values):
    return lax.ppermute(values, "pair", [(0, 1), (1, 0)])


def shift(values, by):
    return lax.ppermute(values, "x", [(i, (i + by) % X) for i in range(X)])


def prompt_call(lengths, rows, kv):
    shape = jax.ShapeDtypeStruct
    count = 2 * X * TILE
    return call(
        prompt_kernel,
        (
            shape((CTX_N, 2 * PROMPT_HALF, LANES), bf16),
            shape((CTX_N * PROMPT_HALF, count), bf16),
            shape((count, LANES), bf16),
            shape((count, LANES), bf16),
            shape((2 * X, TILE), f32),
            shape((2 * X, TILE), f32),
        ),
        "svvvvv",
        scratch=(pltpu.VMEM((2, BLOCK, count), bf16),),
        flops=4 * 2 * 2048 * 1024 * 128 * 2,
        size=3 * 2**20,
    )(lengths, *rows, kv)


def resp_call(kv, side, prompt_part, *rows):
    shape = jax.ShapeDtypeStruct
    blocks = 2 * CTX_N * RESP_HALF // BLOCK
    return call(
        resp_kernel,
        (
            shape((CTX_N, KV_ROWS, LANES), bf16),
            shape((2, CTX_N * RESP_HALF, X * TILE), bf16),
            shape((8, LANES), f32),
        ),
        "vvvvvvv",
        out_spaces="avv",
        scratch=(
            pltpu.VMEM((2, BLOCK, X * TILE), bf16),
            pltpu.VMEM((blocks, BLOCK // RESP_HALF, SIDE, LANES), bf16),
            pltpu.SemaphoreType.DMA((blocks + 1,)),
        ),
        flops=4 * 2 * 1024 * 1024 * 128 * 2,
        size=3 * 2**20,
    )(kv, side, prompt_part, *rows)


def query_call(kv, side, prompt_grads, resp_grads):
    return call(
        query_kernel,
        (jax.ShapeDtypeStruct((2, TILE, LANES), bf16),) * X,
        "vvvv",
        flops=2 * 2048 * 1536 * 128 * 2,
        size=8 * 2**20,
    )(kv, side, prompt_grads, resp_grads)


def per_device(
    prompt_keys,
    prompt_values,
    queries,
    resp_keys,
    resp_values,
    resp_grads,
    resp_lse,
    resp_delta,
    logratio,
    lengths,
):
    shape = jax.ShapeDtypeStruct
    kv = call(
        kv_pack_kernel,
        shape((CTX_N, KV_ROWS + MARGIN_ROWS, LANES), bf16),
        "aaaaaa",
        size=2 * 2**20,
        limit=60,
        scratch=(
            pltpu.SMEM((1, 3), jnp.int32),
            pltpu.VMEM((2, POS), f32),
            pltpu.VMEM((2 * PROMPT_HALF, 2 * LANES), bf16),
            pltpu.VMEM((2 * PROMPT_HALF, 2 * LANES), bf16),
            pltpu.VMEM((POS, X * LANES), bf16),
            pltpu.VMEM((POS, X * LANES), bf16),
            pltpu.SemaphoreType.DMA((6,)),
        ),
    )(lengths, logratio, prompt_keys, prompt_values, resp_keys, resp_values)
    kv = swap(kv)

    block = shape((2, QUERY_ROWS, LANES), bf16)
    own, other = call(
        query_pack_kernel,
        (block, block),
        "aaaa",
        size=2 * 2**20,
        scratch=(
            pltpu.VMEM((4, POS, GROUP * LANES), bf16),
            pltpu.VMEM((4, POS, GROUP * LANES), bf16),
            pltpu.VMEM((POS, X * GROUP), bf16),
            pltpu.VMEM((POS, X * GROUP), bf16),
            pltpu.SemaphoreType.DMA((10,)),
        ),
    )(queries, resp_grads, resp_lse, resp_delta)
    same, odd = call(join_kernel, (block, block), "vv", size=2**20)(own, cross(other))
    rows = (same, shift(odd, 1), shift(same, 2), shift(odd, 3))

    side = cross(kv[:, KV_ROWS - SIDE : KV_ROWS, :])
    prompt_part, prompt_grads, *rows = prompt_call(lengths, rows, kv)
    part, resp_grads, gate = resp_call(kv, side, prompt_part, *rows)
    grads = query_call(kv, side, prompt_grads, resp_grads)
    part = swap(part)
    back = [grads[0]] + [shift(grads[k], X - k) for k in range(1, X)]
    query_grad = call(query_final_kernel, shape((1, 2, POS, 2 * GROUP * LANES), bf16), "vvvvv", size=2**20)(
        gate, *back
    )
    outs = (shape((1, 2 * PROMPT_HALF, 2 * LANES), bf16),) * 2 + (shape((1, 2, POS, 2 * LANES), bf16),) * 2
    pk_grad, pv_grad, key_grad, value_grad = call(kv_final_kernel, outs, "svv", size=2**20)(lengths, gate, part)
    return pk_grad, pv_grad, query_grad, key_grad, value_grad, gate[0, 0:1]


def solution(mesh):
    batch, pair, ctx = mesh.devices.shape
    split = Mesh(mesh.devices.reshape(batch, pair, ctx // X, X), ("batch", "pair", "y", "x"))
    prompt_spec = P("batch", CTX, "pair")
    resp_spec = P("batch", "pair", CTX, None)
    out_spec = P("batch", None, CTX, "pair")
    return jax.shard_map(
        per_device,
        mesh=split,
        in_specs=(
            prompt_spec,
            prompt_spec,
            resp_spec,
            resp_spec,
            resp_spec,
            resp_spec,
            resp_spec,
            resp_spec,
            P("batch", None, CTX),
            P("batch", None),
        ),
        out_specs=(prompt_spec, prompt_spec, out_spec, out_spec, out_spec, P("batch")),
        check_vma=False,
    )
```

```python
import functools

import jax
import jax.numpy as jnp
from jax import lax
from jax.experimental import pallas as pl
from jax.experimental.pallas import tpu as pltpu
from jax.sharding import Mesh, PartitionSpec as P

beta_coef = 0.1
f32, bf16 = jnp.float32, jnp.bfloat16
LANES = 128
CTX = ("y", "x")

X = 4
ROWS_Y = 8
CTX_N = 32
POS = 32
GROUP = 8
TILE = POS * GROUP
PROMPT_HALF = 32
RESP_HALF = 16
STAT_ROWS = 16
QUERY_ROWS = 2 * TILE + STAT_ROWS
SIDE = 2 * RESP_HALF
KV_ROWS = 2 * PROMPT_HALF + 2 * SIDE
LOG2E = 1.4426950408889634
SCALE = LANES**-0.5
DEAD = 1e30
BLOCK = 512
MARGIN_ROWS = 8


def dot(a, b, dims):
    return lax.dot_general(a, b, (dims, ((), ())), preferred_element_type=f32)


def call(kernel, out_shape, spaces, flops=0, scratch=(), size=0, limit=24, out_spaces=""):
    space = {"v": pltpu.VMEM, "s": pltpu.SMEM, "a": pl.ANY}
    many = isinstance(out_shape, tuple)
    out_spaces = out_spaces or "v" * (len(out_shape) if many else 1)
    out_specs = tuple(pl.BlockSpec(memory_space=space[s]) for s in out_spaces)
    return pl.pallas_call(
        kernel,
        out_shape=out_shape,
        in_specs=[pl.BlockSpec(memory_space=space[s]) for s in spaces],
        out_specs=out_specs if many else out_specs[0],
        scratch_shapes=list(scratch),
        compiler_params=pltpu.CompilerParams(vmem_limit_bytes=limit * 2**20),
        cost_estimate=pl.CostEstimate(flops=flops, bytes_accessed=size, transcendentals=0),
    )


def fetch(pairs, sems):
    copies = [pltpu.make_async_copy(a, b, sems.at[i]) for i, (a, b) in enumerate(pairs)]
    for copy in copies:
        copy.start()
    for copy in copies:
        copy.wait()


def kv_pack_kernel(
    lengths_hbm, logratio_hbm, pk_hbm, pv_hbm, rk_hbm, rv_hbm, kv_ref, lengths, logratio, pk, pv, rk, rv, sems
):
    pairs = (
        (lengths_hbm, lengths),
        (logratio_hbm.at[0], logratio),
        (pk_hbm.at[0], pk),
        (pv_hbm.at[0], pv),
        (rk_hbm.at[0, 0], rk),
        (rv_hbm.at[0, 0], rv),
    )
    fetch(pairs, sems)
    first_core = lax.axis_index("pair") == 0
    ctx = lax.axis_index("y") * X + lax.axis_index("x")
    position = ctx * POS + lax.broadcasted_iota(jnp.int32, (1, POS), 1)
    chosen = jnp.where(position < lengths[0, 1], logratio[0:1, :], 0.0)
    rejected = jnp.where(position < lengths[0, 2], logratio[1:2, :], 0.0)
    margin = jnp.sum(chosen - rejected, axis=1, keepdims=True)
    high = margin.astype(bf16).astype(f32)
    middle = (margin - high).astype(bf16).astype(f32)
    low = margin - high - middle
    lane = lax.broadcasted_iota(jnp.int32, (MARGIN_ROWS, LANES), 1)
    row = lax.broadcasted_iota(jnp.int32, (MARGIN_ROWS, LANES), 0)
    block = jnp.where(lane == 0, high, jnp.where(lane == 1, middle, jnp.where(lane == 2, low, 0.0)))
    block = jnp.where(row == 0, block, 0.0).astype(bf16)
    for x in range(X):
        odd, half = x % 2, x // 2
        columns = slice(odd * LANES, (odd + 1) * LANES)
        others = slice((2 + odd) * LANES, (3 + odd) * LANES)
        rows = slice(half * PROMPT_HALF, (half + 1) * PROMPT_HALF)
        index = ctx * 2 * PROMPT_HALF + half * PROMPT_HALF
        live = index + lax.broadcasted_iota(jnp.int32, (PROMPT_HALF, LANES), 0) < lengths[0, 0]
        parts = [jnp.where(live, pk[rows, columns].astype(f32), 0.0).astype(bf16), pv[rows, columns]]
        rows = slice(half * RESP_HALF, (half + 1) * RESP_HALF)
        low_head = [ref[rows, columns].astype(f32) for ref in (rk, rv)]
        high_head = [ref[rows, others].astype(f32) for ref in (rk, rv)]
        parts += [jnp.where(first_core, a, b).astype(bf16) for a, b in zip(low_head, high_head)]
        parts += [jnp.where(first_core, b, a).astype(bf16) for a, b in zip(low_head, high_head)]
        parts += [block]
        for y in range(ROWS_Y):
            at = 0
            for part in parts:
                kv_ref[y * X + x, at : at + part.shape[0], :] = part
                at += part.shape[0]


def query_pack_kernel(q_hbm, g_hbm, lse_hbm, delta_hbm, own_ref, other_ref, q, g, lse, delta, sems):
    core, parity = lax.axis_index("pair"), lax.axis_index("x") % 2
    pairs = [(lse_hbm.at[0, 0], lse), (delta_hbm.at[0, 0], delta)]
    heads = []
    for i in range(4):
        head = 2 * (core if i < 2 else 1 - core) + (parity + i) % 2
        heads.append(head)
        columns = pl.ds(pl.multiple_of(head * GROUP * LANES, GROUP * LANES), GROUP * LANES)
        pairs += [(q_hbm.at[0, 0, :, columns], q.at[i]), (g_hbm.at[0, 0, :, columns], g.at[i])]
    fetch(pairs, sems)
    sign = jnp.where(core == 0, -1.0, 1.0).astype(f32)

    count = X * GROUP
    lane = lax.broadcasted_iota(jnp.int32, (POS, TILE), 1)
    spread = (lane % POS == lax.broadcasted_iota(jnp.int32, (POS, TILE), 0)).astype(bf16)
    head_of = lax.broadcasted_iota(jnp.int32, (count, TILE), 0)
    lane = lax.broadcasted_iota(jnp.int32, (count, TILE), 1)
    lse_rows = dot(lse[...], spread, ((0,), (0,)))
    delta_rows = dot(delta[...], spread, ((0,), (0,))) * sign
    row = lax.broadcasted_iota(jnp.int32, (STAT_ROWS, LANES), 0)
    for i in range(4):
        ref, slot = (own_ref, other_ref)[i // 2], i % 2
        for h in range(GROUP):
            columns = slice(h * LANES, (h + 1) * LANES)
            ref[slot, h * POS : (h + 1) * POS, :] = q[i, :, columns]
            grad = (g[i, :, columns].astype(f32) * sign).astype(bf16)
            ref[slot, TILE + h * POS : TILE + (h + 1) * POS, :] = grad
        keep = head_of == heads[i] * GROUP + lane // POS
        block = jnp.zeros((STAT_ROWS, LANES), f32)
        for n, rows in enumerate((lse_rows, delta_rows)):
            line = jnp.sum(jnp.where(keep, rows, 0.0), axis=0, keepdims=True)
            block = jnp.where(row == 2 * n, line[:, :LANES], block)
            block = jnp.where(row == 2 * n + 1, line[:, LANES:], block)
        ref[slot, 2 * TILE :, :] = block.astype(bf16)


def join_kernel(own_ref, other_ref, same_ref, odd_ref):
    for i, ref in enumerate((same_ref, odd_ref)):
        ref[0] = own_ref[i]
        ref[1] = other_ref[i]


def row_position(k):
    x = (lax.axis_index("x") + X - k) % X
    return (lax.axis_index("y") * X + x) * POS + lax.broadcasted_iota(jnp.int32, (1, TILE), 1) % POS


def key_positions(block, count):
    index = lax.broadcasted_iota(jnp.int32, (count, 1), 0)
    source = block * (count // RESP_HALF) + index // RESP_HALF
    return source * POS + lax.axis_index("x") // 2 * RESP_HALF + index % RESP_HALF


def row_stats(lengths_ref, block, k, j):
    block = block.astype(f32)
    lse = jnp.concatenate([block[0:1], block[1:2]], axis=1) * LOG2E
    delta = jnp.concatenate([block[2:3], block[3:4]], axis=1)
    core = lax.axis_index("pair")
    response = core + j - 2 * core * j
    return jnp.where(row_position(k) < lengths_ref[0, 1 + response], lse, DEAD), delta


def cell(key, value, query, grad, lse, delta, allowed=None):
    scores = dot(key, query, ((1,), (1,)))
    weights = jnp.exp2(scores * (SCALE * LOG2E) - lse)
    if allowed is not None:
        weights = jnp.where(allowed, weights, 0.0)
    weight_grads = dot(value, grad, ((1,), (1,)))
    score_grads = (weights * (weight_grads - delta)).astype(bf16)
    return weights.astype(bf16), score_grads


def staged(blocks, first, second):
    for i, block in enumerate(blocks):
        first(*block, i % 2)
        if i:
            second(*blocks[i - 1], (i - 1) % 2)
    second(*blocks[-1], (len(blocks) - 1) % 2)


def tile_rows(tile):
    return slice(tile * TILE, (tile + 1) * TILE)


def prompt_kernel(
    lengths_ref, q0, q1, q2, q3, kv_ref, out_ref, query_rows, grad_rows, lse_ref, delta_ref, weights, score_grads
):
    for k, ref in enumerate((q0, q1, q2, q3)):
        for j in range(2):
            t = j * X + k
            at = tile_rows(t)
            query_rows[at, :] = ref[j, 0:TILE, :]
            grad_rows[at, :] = ref[j, TILE : 2 * TILE, :]
            lse, delta = row_stats(lengths_ref, ref[j, 2 * TILE :, :], k, j)
            lse_ref[t : t + 1, :], delta_ref[t : t + 1, :] = lse, delta
    per = BLOCK // PROMPT_HALF

    def first(c, slot):
        rows = slice(c * per, (c + 1) * per)
        key = kv_ref[rows, 0:PROMPT_HALF, :].reshape(BLOCK, LANES)
        value = kv_ref[rows, PROMPT_HALF : 2 * PROMPT_HALF, :].reshape(BLOCK, LANES)
        for t in range(2 * X):
            at = tile_rows(t)
            weights[slot, :, at], score_grads[slot, :, at] = cell(
                key, value, query_rows[at, :], grad_rows[at, :], lse_ref[t : t + 1, :], delta_ref[t : t + 1, :]
            )

    def second(c, slot):
        value_grad = dot(weights[slot], grad_rows[...], ((1,), (0,)))
        key_grad = dot(score_grads[slot], query_rows[...], ((1,), (0,))) * SCALE
        shape = (per, PROMPT_HALF, LANES)
        to = slice(c * per, (c + 1) * per)
        out_ref[to, 0:PROMPT_HALF, :] = key_grad.astype(bf16).reshape(shape)
        out_ref[to, PROMPT_HALF:, :] = value_grad.astype(bf16).reshape(shape)

    staged([(c,) for c in range(CTX_N // per)], first, second)


def resp_kernel(
    kv_ref, side_ref, prompt_ref, query_rows, grad_rows, lse_ref, delta_ref,
    out_hbm, gate_ref, weights, score_grads, parts, sems,
):
    copies = [pltpu.make_async_copy(prompt_ref, out_hbm.at[:, 0 : 2 * PROMPT_HALF, :], sems.at[0])]
    copies[0].start()
    margin = jnp.sum(kv_ref[:, KV_ROWS:, :].astype(f32), axis=(0, 1), keepdims=True).reshape(1, LANES)
    margin = jnp.sum(margin, axis=1, keepdims=True)
    gate_ref[...] = jnp.broadcast_to(beta_coef * jax.nn.sigmoid(-beta_coef * margin), gate_ref.shape)
    per = BLOCK // RESP_HALF
    blocks = CTX_N // per
    sources = ((kv_ref, 2 * PROMPT_HALF), (side_ref, 0))

    def first(j, c, slot):
        ref, start = sources[j]
        rows = slice(c * per, (c + 1) * per)
        key = ref[rows, start : start + RESP_HALF, :].reshape(BLOCK, LANES)
        value = ref[rows, start + RESP_HALF : start + SIDE, :].reshape(BLOCK, LANES)
        positions = key_positions(c, BLOCK)
        for k in range(X):
            t = j * X + k
            at, to = tile_rows(t), tile_rows(k)
            weights[slot, :, to], score_grads[slot, :, to] = cell(
                key,
                value,
                query_rows[at, :],
                grad_rows[at, :],
                lse_ref[t : t + 1, :],
                delta_ref[t : t + 1, :],
                positions <= row_position(k),
            )

    def second(j, c, slot):
        rows = slice(j * X * TILE, (j + 1) * X * TILE)
        value_grad = dot(weights[slot], grad_rows[rows, :], ((1,), (0,)))
        key_grad = dot(score_grads[slot], query_rows[rows, :], ((1,), (0,))) * SCALE
        shape = (per, RESP_HALF, LANES)
        n = j * blocks + c
        parts[n, :, 0:RESP_HALF, :] = key_grad.astype(bf16).reshape(shape)
        parts[n, :, RESP_HALF:, :] = value_grad.astype(bf16).reshape(shape)
        start = 2 * PROMPT_HALF + j * SIDE
        to = out_hbm.at[c * per : (c + 1) * per, start : start + SIDE, :]
        copies.append(pltpu.make_async_copy(parts.at[n], to, sems.at[1 + n]))
        copies[-1].start()

    staged([(j, c) for j in range(2) for c in range(blocks)], first, second)
    for copy in copies:
        copy.wait()


def query_kernel(k, kv_ref, side_ref, query_rows, grad_rows, lse_ref, delta_ref, out_ref):
    for j in range(2):
        t = j * X + k
        query, grad = query_rows[tile_rows(t), :], grad_rows[tile_rows(t), :]
        lse, delta = lse_ref[t : t + 1, :], delta_ref[t : t + 1, :]
        total = None
        resp, start = ((kv_ref, 2 * PROMPT_HALF), (side_ref, 0))[j]
        parts = [(kv_ref, c, PROMPT_HALF, 0, None) for c in range(CTX_N * PROMPT_HALF // BLOCK)]
        for c in range(CTX_N * RESP_HALF // BLOCK):
            parts.append((resp, c, RESP_HALF, start, key_positions(c, BLOCK) <= row_position(k)))
        for ref, c, count, start, allowed in parts:
            per = BLOCK // count
            rows = slice(c * per, (c + 1) * per)
            key = ref[rows, start : start + count, :].reshape(BLOCK, LANES)
            value = ref[rows, start + count : start + 2 * count, :].reshape(BLOCK, LANES)
            _, score_grads = cell(key, value, query, grad, lse, delta, allowed)
            term = dot(score_grads, key, ((0,), (0,)))
            total = term if total is None else total + term
        out_ref[j] = (total * SCALE).astype(bf16)


def kv_final_kernel(lengths_ref, gate_ref, part_ref, pk_ref, pv_ref, rk_ref, rv_ref):
    gate = gate_ref[0:1, 0:1]
    core = lax.axis_index("pair")
    ctx = lax.axis_index("y") * X + lax.axis_index("x")
    for x in range(X):
        odd, half = x % 2, x // 2
        columns = slice(odd * LANES, (odd + 1) * LANES)
        total = part_ref[x].astype(f32)
        for y in range(1, ROWS_Y):
            total += part_ref[y * X + x].astype(f32)
        total = total * gate
        rows = slice(half * PROMPT_HALF, (half + 1) * PROMPT_HALF)
        index = ctx * 2 * PROMPT_HALF + half * PROMPT_HALF
        live = index + lax.broadcasted_iota(jnp.int32, (PROMPT_HALF, LANES), 0) < lengths_ref[0, 0]
        pk_ref[0, rows, columns] = jnp.where(live, total[0:PROMPT_HALF], 0.0).astype(bf16)
        pv_ref[0, rows, columns] = jnp.where(live, total[PROMPT_HALF : 2 * PROMPT_HALF], 0.0).astype(bf16)
        rows = slice(half * RESP_HALF, (half + 1) * RESP_HALF)
        for j in range(2):
            response = core + j - 2 * core * j
            at = 2 * PROMPT_HALF + j * SIDE
            rk_ref[0, response, rows, columns] = total[at : at + RESP_HALF].astype(bf16)
            rv_ref[0, response, rows, columns] = total[at + RESP_HALF : at + SIDE].astype(bf16)


def query_final_kernel(gate_ref, d0, d1, d2, d3, out_ref):
    gate = gate_ref[0:1, 0:1]
    core = lax.axis_index("pair")
    even = lax.axis_index("x") % 2 == 0
    for j in range(2):
        response = core + j - 2 * core * j
        for h in range(GROUP):
            rows = slice(h * POS, (h + 1) * POS)
            same = gate * (d0[j, rows, :].astype(f32) + d2[j, rows, :].astype(f32))
            odd = gate * (d1[j, rows, :].astype(f32) + d3[j, rows, :].astype(f32))
            first, second = jnp.where(even, same, odd), jnp.where(even, odd, same)
            out_ref[0, response, :, h * LANES : (h + 1) * LANES] = first.astype(bf16)
            out_ref[0, response, :, (GROUP + h) * LANES : (GROUP + h + 1) * LANES] = second.astype(bf16)


def swap(values):
    return lax.all_to_all(values, CTX, split_axis=0, concat_axis=0, tiled=True)


def cross(values):
    return lax.ppermute(values, "pair", [(0, 1), (1, 0)])


def shift(values, by):
    return lax.ppermute(values, "x", [(i, (i + by) % X) for i in range(X)])


def prompt_call(lengths, rows, kv):
    shape = jax.ShapeDtypeStruct
    count = 2 * X * TILE
    return call(
        prompt_kernel,
        (
            shape((CTX_N, 2 * PROMPT_HALF, LANES), bf16),
            shape((count, LANES), bf16),
            shape((count, LANES), bf16),
            shape((2 * X, TILE), f32),
            shape((2 * X, TILE), f32),
        ),
        "svvvvv",
        scratch=(pltpu.VMEM((2, BLOCK, count), bf16), pltpu.VMEM((2, BLOCK, count), bf16)),
        flops=4 * 2 * 2048 * 1024 * 128 * 2,
        size=3 * 2**20,
    )(lengths, *rows, kv)


def resp_call(kv, side, prompt_part, *rows):
    shape = jax.ShapeDtypeStruct
    blocks = 2 * CTX_N * RESP_HALF // BLOCK
    return call(
        resp_kernel,
        (
            shape((CTX_N, KV_ROWS, LANES), bf16),
            shape((8, LANES), f32),
        ),
        "vvvvvvv",
        out_spaces="av",
        scratch=(
            pltpu.VMEM((2, BLOCK, X * TILE), bf16),
            pltpu.VMEM((2, BLOCK, X * TILE), bf16),
            pltpu.VMEM((blocks, BLOCK // RESP_HALF, SIDE, LANES), bf16),
            pltpu.SemaphoreType.DMA((blocks + 1,)),
        ),
        flops=4 * 2 * 1024 * 1024 * 128 * 2,
        size=3 * 2**20,
    )(kv, side, prompt_part, *rows)


def query_call(k, kv, side, *rows):
    return call(
        functools.partial(query_kernel, k),
        jax.ShapeDtypeStruct((2, TILE, LANES), bf16),
        "vvvvvv",
        flops=3 * 2 * 512 * 1536 * 128 * 2,
        size=3 * 2**20,
    )(kv, side, *rows)


def per_device(
    prompt_keys,
    prompt_values,
    queries,
    resp_keys,
    resp_values,
    resp_grads,
    resp_lse,
    resp_delta,
    logratio,
    lengths,
):
    shape = jax.ShapeDtypeStruct
    kv = call(
        kv_pack_kernel,
        shape((CTX_N, KV_ROWS + MARGIN_ROWS, LANES), bf16),
        "aaaaaa",
        size=2 * 2**20,
        limit=60,
        scratch=(
            pltpu.SMEM((1, 3), jnp.int32),
            pltpu.VMEM((2, POS), f32),
            pltpu.VMEM((2 * PROMPT_HALF, 2 * LANES), bf16),
            pltpu.VMEM((2 * PROMPT_HALF, 2 * LANES), bf16),
            pltpu.VMEM((POS, X * LANES), bf16),
            pltpu.VMEM((POS, X * LANES), bf16),
            pltpu.SemaphoreType.DMA((6,)),
        ),
    )(lengths, logratio, prompt_keys, prompt_values, resp_keys, resp_values)
    kv = swap(kv)

    block = shape((2, QUERY_ROWS, LANES), bf16)
    own, other = call(
        query_pack_kernel,
        (block, block),
        "aaaa",
        size=2 * 2**20,
        scratch=(
            pltpu.VMEM((4, POS, GROUP * LANES), bf16),
            pltpu.VMEM((4, POS, GROUP * LANES), bf16),
            pltpu.VMEM((POS, X * GROUP), bf16),
            pltpu.VMEM((POS, X * GROUP), bf16),
            pltpu.SemaphoreType.DMA((10,)),
        ),
    )(queries, resp_grads, resp_lse, resp_delta)
    same, odd = call(join_kernel, (block, block), "vv", size=2**20)(own, cross(other))
    rows = (same, shift(odd, 1), shift(same, 2), shift(odd, 3))

    side = cross(kv[:, KV_ROWS - SIDE : KV_ROWS, :])
    prompt_part, *rows = prompt_call(lengths, rows, kv)
    part, gate = resp_call(kv, side, prompt_part, *rows)
    grads = [query_call(k, kv, side, *rows) for k in range(X)]
    part = swap(part)
    back = [grads[0]] + [shift(grads[k], X - k) for k in range(1, X)]
    query_grad = call(query_final_kernel, shape((1, 2, POS, 2 * GROUP * LANES), bf16), "vvvvv", size=2**20)(
        gate, *back
    )
    outs = (shape((1, 2 * PROMPT_HALF, 2 * LANES), bf16),) * 2 + (shape((1, 2, POS, 2 * LANES), bf16),) * 2
    pk_grad, pv_grad, key_grad, value_grad = call(kv_final_kernel, outs, "svv", size=2**20)(lengths, gate, part)
    return pk_grad, pv_grad, query_grad, key_grad, value_grad, gate[0, 0:1]


def solution(mesh):
    batch, pair, ctx = mesh.devices.shape
    split = Mesh(mesh.devices.reshape(batch, pair, ctx // X, X), ("batch", "pair", "y", "x"))
    prompt_spec = P("batch", CTX, "pair")
    resp_spec = P("batch", "pair", CTX, None)
    out_spec = P("batch", None, CTX, "pair")
    return jax.shard_map(
        per_device,
        mesh=split,
        in_specs=(
            prompt_spec,
            prompt_spec,
            resp_spec,
            resp_spec,
            resp_spec,
            resp_spec,
            resp_spec,
            resp_spec,
            P("batch", None, CTX),
            P("batch", None),
        ),
        out_specs=(prompt_spec, prompt_spec, out_spec, out_spec, out_spec, P("batch")),
        check_vma=False,
    )
```

```python
import functools

import jax
import jax.numpy as jnp
from jax import lax
from jax.experimental import pallas as pl
from jax.experimental.pallas import tpu as pltpu
from jax.sharding import Mesh, PartitionSpec as P

beta_coef = 0.1
f32, bf16 = jnp.float32, jnp.bfloat16
LANES = 128
CTX = ("y", "xh", "xl")
ROW = ("xh", "xl")
PEERS = ("y", "xl")

X = 4
ROWS_Y = 8
PEERS_N = 16
POS = 32
PROMPT = 64
GROUP = 8
TILE = POS * GROUP
STAT_ROWS = 16
QUERY_ROWS = 2 * TILE + STAT_ROWS
SIDE = 2 * POS
KV_ROWS = 2 * PROMPT + 2 * SIDE
LOG2E = 1.4426950408889634
SCALE = LANES**-0.5
DEAD = 1e30
BLOCK = 512
MARGIN_ROWS = 8


def dot(a, b, dims):
    return lax.dot_general(a, b, (dims, ((), ())), preferred_element_type=f32)


def call(kernel, out_shape, spaces, flops=0, scratch=(), size=0, limit=24, out_spaces=""):
    space = {"v": pltpu.VMEM, "s": pltpu.SMEM, "a": pl.ANY}
    many = isinstance(out_shape, tuple)
    out_spaces = out_spaces or "v" * (len(out_shape) if many else 1)
    out_specs = tuple(pl.BlockSpec(memory_space=space[s]) for s in out_spaces)
    return pl.pallas_call(
        kernel,
        out_shape=out_shape,
        in_specs=[pl.BlockSpec(memory_space=space[s]) for s in spaces],
        out_specs=out_specs if many else out_specs[0],
        scratch_shapes=list(scratch),
        compiler_params=pltpu.CompilerParams(vmem_limit_bytes=limit * 2**20),
        cost_estimate=pl.CostEstimate(flops=flops, bytes_accessed=size, transcendentals=0),
    )


def fetch(pairs, sems):
    copies = [pltpu.make_async_copy(a, b, sems.at[i]) for i, (a, b) in enumerate(pairs)]
    for copy in copies:
        copy.start()
    for copy in copies:
        copy.wait()


def split_margin(margin, rows):
    high = margin.astype(bf16).astype(f32)
    middle = (margin - high).astype(bf16).astype(f32)
    low = margin - high - middle
    lane = lax.broadcasted_iota(jnp.int32, (rows, LANES), 1)
    row = lax.broadcasted_iota(jnp.int32, (rows, LANES), 0)
    block = jnp.where(lane == 0, high, jnp.where(lane == 1, middle, jnp.where(lane == 2, low, 0.0)))
    return jnp.where(row == 0, block, 0.0).astype(bf16)


def gate_of(margin, block):
    other = jnp.sum(block.astype(f32), axis=0, keepdims=True)
    margin = margin + jnp.sum(other, axis=1, keepdims=True)
    return beta_coef * jax.nn.sigmoid(-beta_coef * margin)


def kv_pack_kernel(
    lengths_hbm, logratio_hbm, pk_hbm, pv_hbm, rk_hbm, rv_hbm, kv_ref, lengths, logratio, pk, pv, rk, rv, sems
):
    pairs = (
        (lengths_hbm, lengths),
        (logratio_hbm.at[0], logratio),
        (pk_hbm.at[0], pk),
        (pv_hbm.at[0], pv),
        (rk_hbm.at[0, 0], rk),
        (rv_hbm.at[0, 0], rv),
    )
    fetch(pairs, sems)
    first_core = lax.axis_index("pair") == 0
    ctx = lax.axis_index(CTX)
    position = ctx * POS + lax.broadcasted_iota(jnp.int32, (1, POS), 1)
    chosen = jnp.where(position < lengths[0, 1], logratio[0:1, :], 0.0)
    rejected = jnp.where(position < lengths[0, 2], logratio[1:2, :], 0.0)
    margin = jnp.sum(chosen - rejected, axis=1, keepdims=True)
    block = split_margin(margin, MARGIN_ROWS)
    live = ctx * PROMPT + lax.broadcasted_iota(jnp.int32, (PROMPT, LANES), 0) < lengths[0, 0]
    for xl in range(2):
        columns = slice(xl * LANES, (xl + 1) * LANES)
        others = slice((2 + xl) * LANES, (3 + xl) * LANES)
        parts = [jnp.where(live, pk[:, columns].astype(f32), 0.0).astype(bf16), pv[:, columns]]
        low_head = [ref[:, columns].astype(f32) for ref in (rk, rv)]
        high_head = [ref[:, others].astype(f32) for ref in (rk, rv)]
        parts += [jnp.where(first_core, a, b).astype(bf16) for a, b in zip(low_head, high_head)]
        parts += [jnp.where(first_core, b, a).astype(bf16) for a, b in zip(low_head, high_head)]
        parts += [block]
        for y in range(ROWS_Y):
            at = 0
            for part in parts:
                kv_ref[y * 2 + xl, at : at + part.shape[0], :] = part
                at += part.shape[0]


def query_pack_kernel(q_hbm, g_hbm, lse_hbm, delta_hbm, own_ref, other_ref, q, g, lse, delta, sems):
    core, parity = lax.axis_index("pair"), lax.axis_index("xl")
    pairs = [(lse_hbm.at[0, 0], lse), (delta_hbm.at[0, 0], delta)]
    heads = []
    for i in range(4):
        head = 2 * (core if i < 2 else 1 - core) + (parity + i) % 2
        heads.append(head)
        columns = pl.ds(pl.multiple_of(head * GROUP * LANES, GROUP * LANES), GROUP * LANES)
        pairs += [(q_hbm.at[0, 0, :, columns], q.at[i]), (g_hbm.at[0, 0, :, columns], g.at[i])]
    fetch(pairs, sems)
    sign = jnp.where(core == 0, -1.0, 1.0).astype(f32)

    count = X * GROUP
    lane = lax.broadcasted_iota(jnp.int32, (POS, TILE), 1)
    spread = (lane % POS == lax.broadcasted_iota(jnp.int32, (POS, TILE), 0)).astype(bf16)
    head_of = lax.broadcasted_iota(jnp.int32, (count, TILE), 0)
    lane = lax.broadcasted_iota(jnp.int32, (count, TILE), 1)
    lse_rows = dot(lse[...], spread, ((0,), (0,)))
    delta_rows = dot(delta[...], spread, ((0,), (0,))) * sign
    row = lax.broadcasted_iota(jnp.int32, (STAT_ROWS, LANES), 0)
    for i in range(4):
        ref, slot = (own_ref, other_ref)[i // 2], i % 2
        for h in range(GROUP):
            columns = slice(h * LANES, (h + 1) * LANES)
            ref[slot, h * POS : (h + 1) * POS, :] = q[i, :, columns]
            grad = (g[i, :, columns].astype(f32) * sign).astype(bf16)
            ref[slot, TILE + h * POS : TILE + (h + 1) * POS, :] = grad
        keep = head_of == heads[i] * GROUP + lane // POS
        block = jnp.zeros((STAT_ROWS, LANES), f32)
        for n, rows in enumerate((lse_rows, delta_rows)):
            line = jnp.sum(jnp.where(keep, rows, 0.0), axis=0, keepdims=True)
            block = jnp.where(row == 2 * n, line[:, :LANES], block)
            block = jnp.where(row == 2 * n + 1, line[:, LANES:], block)
        ref[slot, 2 * TILE :, :] = block.astype(bf16)


def join_kernel(own_ref, other_ref, same_ref, odd_ref):
    for i, ref in enumerate((same_ref, odd_ref)):
        ref[0] = own_ref[i]
        ref[1] = other_ref[i]


def row_position(k):
    x = (lax.axis_index(ROW) + X - k) % X
    return (lax.axis_index("y") * X + x) * POS + lax.broadcasted_iota(jnp.int32, (1, TILE), 1) % POS


def key_positions(block, count):
    index = lax.broadcasted_iota(jnp.int32, (count, 1), 0)
    source = block * (count // POS) + index // POS
    ctx = source // 2 * X + 2 * lax.axis_index("xh") + source % 2
    return ctx * POS + index % POS


def row_stats(lengths_ref, block, k, j):
    block = block.astype(f32)
    lse = jnp.concatenate([block[0:1], block[1:2]], axis=1) * LOG2E
    delta = jnp.concatenate([block[2:3], block[3:4]], axis=1)
    core = lax.axis_index("pair")
    response = core + j - 2 * core * j
    return jnp.where(row_position(k) < lengths_ref[0, 1 + response], lse, DEAD), delta


def cell(key, value, query, grad, lse, delta, allowed=None):
    scores = dot(key, query, ((1,), (1,)))
    weights = jnp.exp2(scores * (SCALE * LOG2E) - lse)
    if allowed is not None:
        weights = jnp.where(allowed, weights, 0.0)
    weight_grads = dot(value, grad, ((1,), (1,)))
    score_grads = (weights * (weight_grads - delta)).astype(bf16)
    return weights.astype(bf16), score_grads


def staged(blocks, first, second):
    for i, block in enumerate(blocks):
        first(*block, i % 2)
        if i:
            second(*blocks[i - 1], (i - 1) % 2)
    second(*blocks[-1], (len(blocks) - 1) % 2)


def tile_rows(tile):
    return slice(tile * TILE, (tile + 1) * TILE)


def prompt_kernel(
    lengths_ref, q0, q1, q2, q3, kv_ref, out_ref, query_rows, grad_rows, lse_ref, delta_ref, weights, score_grads
):
    for k, ref in enumerate((q0, q1, q2, q3)):
        for j in range(2):
            t = j * X + k
            at = tile_rows(t)
            query_rows[at, :] = ref[j, 0:TILE, :]
            grad_rows[at, :] = ref[j, TILE : 2 * TILE, :]
            lse, delta = row_stats(lengths_ref, ref[j, 2 * TILE :, :], k, j)
            lse_ref[t : t + 1, :], delta_ref[t : t + 1, :] = lse, delta
    per = BLOCK // PROMPT

    def first(c, slot):
        rows = slice(c * per, (c + 1) * per)
        key = kv_ref[rows, 0:PROMPT, :].reshape(BLOCK, LANES)
        value = kv_ref[rows, PROMPT : 2 * PROMPT, :].reshape(BLOCK, LANES)
        for t in range(2 * X):
            at = tile_rows(t)
            weights[slot, :, at], score_grads[slot, :, at] = cell(
                key, value, query_rows[at, :], grad_rows[at, :], lse_ref[t : t + 1, :], delta_ref[t : t + 1, :]
            )

    def second(c, slot):
        value_grad = dot(weights[slot], grad_rows[...], ((1,), (0,)))
        key_grad = dot(score_grads[slot], query_rows[...], ((1,), (0,))) * SCALE
        shape = (per, PROMPT, LANES)
        to = slice(c * per, (c + 1) * per)
        out_ref[to, 0:PROMPT, :] = key_grad.astype(bf16).reshape(shape)
        out_ref[to, PROMPT:, :] = value_grad.astype(bf16).reshape(shape)

    staged([(c,) for c in range(PEERS_N // per)], first, second)


def resp_kernel(
    kv_ref, side_ref, prompt_ref, query_rows, grad_rows, lse_ref, delta_ref,
    out_hbm, margin_ref, weights, score_grads, parts, sems,
):
    copies = [pltpu.make_async_copy(prompt_ref, out_hbm.at[:, 0 : 2 * PROMPT, :], sems.at[0])]
    copies[0].start()
    margin = jnp.sum(kv_ref[:, KV_ROWS:, :].astype(f32), axis=(0, 1), keepdims=True).reshape(1, LANES)
    margin = jnp.sum(margin, axis=1, keepdims=True)
    margin_ref[...] = jnp.broadcast_to(margin, margin_ref.shape)
    per = BLOCK // POS
    blocks = PEERS_N // per
    sources = ((kv_ref, 2 * PROMPT), (side_ref, 0))

    def first(j, c, slot):
        ref, start = sources[j]
        rows = slice(c * per, (c + 1) * per)
        key = ref[rows, start : start + POS, :].reshape(BLOCK, LANES)
        value = ref[rows, start + POS : start + SIDE, :].reshape(BLOCK, LANES)
        positions = key_positions(c, BLOCK)
        for k in range(X):
            t = j * X + k
            at, to = tile_rows(t), tile_rows(k)
            weights[slot, :, to], score_grads[slot, :, to] = cell(
                key,
                value,
                query_rows[at, :],
                grad_rows[at, :],
                lse_ref[t : t + 1, :],
                delta_ref[t : t + 1, :],
                positions <= row_position(k),
            )

    def second(j, c, slot):
        rows = slice(j * X * TILE, (j + 1) * X * TILE)
        value_grad = dot(weights[slot], grad_rows[rows, :], ((1,), (0,)))
        key_grad = dot(score_grads[slot], query_rows[rows, :], ((1,), (0,))) * SCALE
        shape = (per, POS, LANES)
        n = j * blocks + c
        parts[n, :, 0:POS, :] = key_grad.astype(bf16).reshape(shape)
        parts[n, :, POS:, :] = value_grad.astype(bf16).reshape(shape)
        start = 2 * PROMPT + j * SIDE
        to = out_hbm.at[c * per : (c + 1) * per, start : start + SIDE, :]
        copies.append(pltpu.make_async_copy(parts.at[n], to, sems.at[1 + n]))
        copies[-1].start()

    staged([(j, c) for j in range(2) for c in range(blocks)], first, second)
    for copy in copies:
        copy.wait()


def query_kernel(k, margin_ref, kv_ref, side_ref, query_rows, grad_rows, lse_ref, delta_ref, out_ref):
    for j in range(2):
        t = j * X + k
        query, grad = query_rows[tile_rows(t), :], grad_rows[tile_rows(t), :]
        lse, delta = lse_ref[t : t + 1, :], delta_ref[t : t + 1, :]
        total = None
        resp, start = ((kv_ref, 2 * PROMPT), (side_ref, 0))[j]
        parts = [(kv_ref, c, PROMPT, 0, None) for c in range(PEERS_N * PROMPT // BLOCK)]
        for c in range(PEERS_N * POS // BLOCK):
            parts.append((resp, c, POS, start, key_positions(c, BLOCK) <= row_position(k)))
        for ref, c, count, start, allowed in parts:
            per = BLOCK // count
            rows = slice(c * per, (c + 1) * per)
            key = ref[rows, start : start + count, :].reshape(BLOCK, LANES)
            value = ref[rows, start + count : start + 2 * count, :].reshape(BLOCK, LANES)
            _, score_grads = cell(key, value, query, grad, lse, delta, allowed)
            term = dot(score_grads, key, ((0,), (0,)))
            total = term if total is None else total + term
        out_ref[tile_rows(j), :] = (total * SCALE).astype(bf16)
    if k == 2:
        out_ref[2 * TILE :, :] = split_margin(margin_ref[0:1, 0:1], STAT_ROWS)


def kv_final_kernel(lengths_ref, margin_ref, d2, part_ref, pk_ref, pv_ref, rk_ref, rv_ref):
    gate = gate_of(margin_ref[0:1, 0:1], d2[2 * TILE :, :])
    core = lax.axis_index("pair")
    live = lax.axis_index(CTX) * PROMPT + lax.broadcasted_iota(jnp.int32, (PROMPT, LANES), 0) < lengths_ref[0, 0]
    for xl in range(2):
        columns = slice(xl * LANES, (xl + 1) * LANES)
        total = part_ref[xl].astype(f32)
        for y in range(1, ROWS_Y):
            total += part_ref[y * 2 + xl].astype(f32)
        total = total * gate
        pk_ref[0, :, columns] = jnp.where(live, total[0:PROMPT], 0.0).astype(bf16)
        pv_ref[0, :, columns] = jnp.where(live, total[PROMPT : 2 * PROMPT], 0.0).astype(bf16)
        for j in range(2):
            response = core + j - 2 * core * j
            at = 2 * PROMPT + j * SIDE
            rk_ref[0, response, :, columns] = total[at : at + POS].astype(bf16)
            rv_ref[0, response, :, columns] = total[at + POS : at + SIDE].astype(bf16)


def query_final_kernel(margin_ref, d0, d1, d2, d3, out_ref, gate_ref):
    gate = gate_of(margin_ref[0:1, 0:1], d2[2 * TILE :, :])
    gate_ref[...] = jnp.broadcast_to(gate, gate_ref.shape)
    core = lax.axis_index("pair")
    even = lax.axis_index("xl") == 0
    for j in range(2):
        response = core + j - 2 * core * j
        for h in range(GROUP):
            rows = slice(j * TILE + h * POS, j * TILE + (h + 1) * POS)
            same = gate * (d0[rows, :].astype(f32) + d2[rows, :].astype(f32))
            odd = gate * (d1[rows, :].astype(f32) + d3[rows, :].astype(f32))
            first, second = jnp.where(even, same, odd), jnp.where(even, odd, same)
            out_ref[0, response, :, h * LANES : (h + 1) * LANES] = first.astype(bf16)
            out_ref[0, response, :, (GROUP + h) * LANES : (GROUP + h + 1) * LANES] = second.astype(bf16)


def swap(values):
    return lax.all_to_all(values, PEERS, split_axis=0, concat_axis=0, tiled=True)


def cross(values):
    return lax.ppermute(values, "pair", [(0, 1), (1, 0)])


def shift(values, by):
    return lax.ppermute(values, ROW, [(i, (i + by) % X) for i in range(X)])


def prompt_call(lengths, rows, kv):
    shape = jax.ShapeDtypeStruct
    count = 2 * X * TILE
    return call(
        prompt_kernel,
        (
            shape((PEERS_N, 2 * PROMPT, LANES), bf16),
            shape((count, LANES), bf16),
            shape((count, LANES), bf16),
            shape((2 * X, TILE), f32),
            shape((2 * X, TILE), f32),
        ),
        "svvvvv",
        scratch=(pltpu.VMEM((2, BLOCK, count), bf16), pltpu.VMEM((2, BLOCK, count), bf16)),
        flops=4 * 2 * 2048 * 1024 * 128 * 2,
        size=3 * 2**20,
    )(lengths, *rows, kv)


def resp_call(kv, side, prompt_part, *rows):
    shape = jax.ShapeDtypeStruct
    blocks = 2 * PEERS_N * POS // BLOCK
    return call(
        resp_kernel,
        (
            shape((PEERS_N, KV_ROWS, LANES), bf16),
            shape((8, LANES), f32),
        ),
        "vvvvvvv",
        out_spaces="av",
        scratch=(
            pltpu.VMEM((2, BLOCK, X * TILE), bf16),
            pltpu.VMEM((2, BLOCK, X * TILE), bf16),
            pltpu.VMEM((blocks, BLOCK // POS, SIDE, LANES), bf16),
            pltpu.SemaphoreType.DMA((blocks + 1,)),
        ),
        flops=4 * 2 * 1024 * 1024 * 128 * 2,
        size=3 * 2**20,
    )(kv, side, prompt_part, *rows)


def query_call(k, margin, kv, side, *rows):
    extra = STAT_ROWS if k == 2 else 0
    return call(
        functools.partial(query_kernel, k),
        jax.ShapeDtypeStruct((2 * TILE + extra, LANES), bf16),
        "vvvvvvv",
        flops=3 * 2 * 512 * 1536 * 128 * 2,
        size=3 * 2**20,
    )(margin, kv, side, *rows)


def per_device(
    prompt_keys,
    prompt_values,
    queries,
    resp_keys,
    resp_values,
    resp_grads,
    resp_lse,
    resp_delta,
    logratio,
    lengths,
):
    shape = jax.ShapeDtypeStruct
    kv = call(
        kv_pack_kernel,
        shape((PEERS_N, KV_ROWS + MARGIN_ROWS, LANES), bf16),
        "aaaaaa",
        size=2 * 2**20,
        limit=60,
        scratch=(
            pltpu.SMEM((1, 3), jnp.int32),
            pltpu.VMEM((2, POS), f32),
            pltpu.VMEM((PROMPT, 2 * LANES), bf16),
            pltpu.VMEM((PROMPT, 2 * LANES), bf16),
            pltpu.VMEM((POS, X * LANES), bf16),
            pltpu.VMEM((POS, X * LANES), bf16),
            pltpu.SemaphoreType.DMA((6,)),
        ),
    )(lengths, logratio, prompt_keys, prompt_values, resp_keys, resp_values)
    kv = swap(kv)

    block = shape((2, QUERY_ROWS, LANES), bf16)
    own, other = call(
        query_pack_kernel,
        (block, block),
        "aaaa",
        size=2 * 2**20,
        scratch=(
            pltpu.VMEM((4, POS, GROUP * LANES), bf16),
            pltpu.VMEM((4, POS, GROUP * LANES), bf16),
            pltpu.VMEM((POS, X * GROUP), bf16),
            pltpu.VMEM((POS, X * GROUP), bf16),
            pltpu.SemaphoreType.DMA((10,)),
        ),
    )(queries, resp_grads, resp_lse, resp_delta)
    same, odd = call(join_kernel, (block, block), "vv", size=2**20)(own, cross(other))
    rows = (same, shift(odd, 1), shift(same, 2), shift(odd, 3))

    side = cross(kv[:, KV_ROWS - SIDE : KV_ROWS, :])
    prompt_part, *rows = prompt_call(lengths, rows, kv)
    part, margin = resp_call(kv, side, prompt_part, *rows)
    grads = [query_call(k, margin, kv, side, *rows) for k in range(X)]
    part = swap(part)
    back = [grads[0]] + [shift(grads[k], X - k) for k in range(1, X)]
    query_grad, gate = call(
        query_final_kernel,
        (shape((1, 2, POS, 2 * GROUP * LANES), bf16), shape((8, LANES), f32)),
        "vvvvv",
        size=2**20,
    )(margin, *back)
    outs = (shape((1, PROMPT, 2 * LANES), bf16),) * 2 + (shape((1, 2, POS, 2 * LANES), bf16),) * 2
    pk_grad, pv_grad, key_grad, value_grad = call(kv_final_kernel, outs, "svvv", size=2**20)(
        lengths, margin, back[2], part
    )
    return pk_grad, pv_grad, query_grad, key_grad, value_grad, gate[0, 0:1]


def solution(mesh):
    batch, pair, ctx = mesh.devices.shape
    split = Mesh(mesh.devices.reshape(batch, pair, ctx // X, 2, 2), ("batch", "pair", "y", "xh", "xl"))
    prompt_spec = P("batch", CTX, "pair")
    resp_spec = P("batch", "pair", CTX, None)
    out_spec = P("batch", None, CTX, "pair")
    return jax.shard_map(
        per_device,
        mesh=split,
        in_specs=(
            prompt_spec,
            prompt_spec,
            resp_spec,
            resp_spec,
            resp_spec,
            resp_spec,
            resp_spec,
            resp_spec,
            P("batch", None, CTX),
            P("batch", None),
        ),
        out_specs=(prompt_spec, prompt_spec, out_spec, out_spec, out_spec, P("batch")),
        check_vma=False,
    )
```

```python
import functools

import jax
import jax.numpy as jnp
from jax import lax
from jax.experimental import pallas as pl
from jax.experimental.pallas import tpu as pltpu
from jax.sharding import Mesh, PartitionSpec as P

beta_coef = 0.1
f32, bf16 = jnp.float32, jnp.bfloat16
LANES = 128
CTX = ("y", "xh", "xl")
ROW = ("xh", "xl")
PEERS = ("y", "xl")

X = 4
ROWS_Y = 8
PEERS_N = 16
POS = 32
PROMPT = 64
GROUP = 8
TILE = POS * GROUP
STAT_ROWS = 16
QUERY_ROWS = 2 * TILE + STAT_ROWS
SIDE = 2 * POS
KV_ROWS = 2 * PROMPT + 2 * SIDE
LOG2E = 1.4426950408889634
SCALE = LANES**-0.5
DEAD = 1e30
BLOCK = 512
PROMPT_BLOCK = 256
MARGIN_ROWS = 8


def dot(a, b, dims):
    return lax.dot_general(a, b, (dims, ((), ())), preferred_element_type=f32)


def call(kernel, out_shape, spaces, flops=0, scratch=(), size=0, limit=24, out_spaces=""):
    space = {"v": pltpu.VMEM, "s": pltpu.SMEM, "a": pl.ANY}
    many = isinstance(out_shape, tuple)
    out_spaces = out_spaces or "v" * (len(out_shape) if many else 1)
    out_specs = tuple(pl.BlockSpec(memory_space=space[s]) for s in out_spaces)
    return pl.pallas_call(
        kernel,
        out_shape=out_shape,
        in_specs=[pl.BlockSpec(memory_space=space[s]) for s in spaces],
        out_specs=out_specs if many else out_specs[0],
        scratch_shapes=list(scratch),
        compiler_params=pltpu.CompilerParams(vmem_limit_bytes=limit * 2**20),
        cost_estimate=pl.CostEstimate(flops=flops, bytes_accessed=size, transcendentals=0),
    )


def fetch(pairs, sems):
    copies = [pltpu.make_async_copy(a, b, sems.at[i]) for i, (a, b) in enumerate(pairs)]
    for copy in copies:
        copy.start()
    for copy in copies:
        copy.wait()


def split_margin(margin, rows):
    high = margin.astype(bf16).astype(f32)
    middle = (margin - high).astype(bf16).astype(f32)
    low = margin - high - middle
    lane = lax.broadcasted_iota(jnp.int32, (rows, LANES), 1)
    row = lax.broadcasted_iota(jnp.int32, (rows, LANES), 0)
    block = jnp.where(lane == 0, high, jnp.where(lane == 1, middle, jnp.where(lane == 2, low, 0.0)))
    return jnp.where(row == 0, block, 0.0).astype(bf16)


def gate_of(margin, block):
    other = jnp.sum(block.astype(f32), axis=0, keepdims=True)
    margin = margin + jnp.sum(other, axis=1, keepdims=True)
    return beta_coef * jax.nn.sigmoid(-beta_coef * margin)


def kv_pack_kernel(
    lengths_hbm, logratio_hbm, pk_hbm, pv_hbm, rk_hbm, rv_hbm, kv_ref, lengths, logratio, pk, pv, rk, rv, sems
):
    pairs = (
        (lengths_hbm, lengths),
        (logratio_hbm.at[0], logratio),
        (pk_hbm.at[0], pk),
        (pv_hbm.at[0], pv),
        (rk_hbm.at[0, 0], rk),
        (rv_hbm.at[0, 0], rv),
    )
    fetch(pairs, sems)
    first_core = lax.axis_index("pair") == 0
    ctx = lax.axis_index(CTX)
    position = ctx * POS + lax.broadcasted_iota(jnp.int32, (1, POS), 1)
    chosen = jnp.where(position < lengths[0, 1], logratio[0:1, :], 0.0)
    rejected = jnp.where(position < lengths[0, 2], logratio[1:2, :], 0.0)
    margin = jnp.sum(chosen - rejected, axis=1, keepdims=True)
    block = split_margin(margin, MARGIN_ROWS)
    live = ctx * PROMPT + lax.broadcasted_iota(jnp.int32, (PROMPT, LANES), 0) < lengths[0, 0]
    for xl in range(2):
        columns = slice(xl * LANES, (xl + 1) * LANES)
        others = slice((2 + xl) * LANES, (3 + xl) * LANES)
        parts = [jnp.where(live, pk[:, columns].astype(f32), 0.0).astype(bf16), pv[:, columns]]
        low_head = [ref[:, columns].astype(f32) for ref in (rk, rv)]
        high_head = [ref[:, others].astype(f32) for ref in (rk, rv)]
        parts += [jnp.where(first_core, a, b).astype(bf16) for a, b in zip(low_head, high_head)]
        parts += [jnp.where(first_core, b, a).astype(bf16) for a, b in zip(low_head, high_head)]
        parts += [block]
        for y in range(ROWS_Y):
            at = 0
            for part in parts:
                kv_ref[y * 2 + xl, at : at + part.shape[0], :] = part
                at += part.shape[0]


def query_pack_kernel(q_hbm, g_hbm, lse_hbm, delta_hbm, own_ref, other_ref, q, g, lse, delta, sems):
    core, parity = lax.axis_index("pair"), lax.axis_index("xl")
    pairs = [(lse_hbm.at[0, 0], lse), (delta_hbm.at[0, 0], delta)]
    heads = []
    for i in range(4):
        head = 2 * (core if i < 2 else 1 - core) + (parity + i) % 2
        heads.append(head)
        columns = pl.ds(pl.multiple_of(head * GROUP * LANES, GROUP * LANES), GROUP * LANES)
        pairs += [(q_hbm.at[0, 0, :, columns], q.at[i]), (g_hbm.at[0, 0, :, columns], g.at[i])]
    fetch(pairs, sems)
    sign = jnp.where(core == 0, -1.0, 1.0).astype(f32)

    count = X * GROUP
    lane = lax.broadcasted_iota(jnp.int32, (POS, TILE), 1)
    spread = (lane % POS == lax.broadcasted_iota(jnp.int32, (POS, TILE), 0)).astype(bf16)
    head_of = lax.broadcasted_iota(jnp.int32, (count, TILE), 0)
    lane = lax.broadcasted_iota(jnp.int32, (count, TILE), 1)
    lse_rows = dot(lse[...], spread, ((0,), (0,)))
    delta_rows = dot(delta[...], spread, ((0,), (0,))) * sign
    row = lax.broadcasted_iota(jnp.int32, (STAT_ROWS, LANES), 0)
    for i in range(4):
        ref, slot = (own_ref, other_ref)[i // 2], i % 2
        for h in range(GROUP):
            columns = slice(h * LANES, (h + 1) * LANES)
            ref[slot, h * POS : (h + 1) * POS, :] = q[i, :, columns]
            grad = (g[i, :, columns].astype(f32) * sign).astype(bf16)
            ref[slot, TILE + h * POS : TILE + (h + 1) * POS, :] = grad
        keep = head_of == heads[i] * GROUP + lane // POS
        block = jnp.zeros((STAT_ROWS, LANES), f32)
        for n, rows in enumerate((lse_rows, delta_rows)):
            line = jnp.sum(jnp.where(keep, rows, 0.0), axis=0, keepdims=True)
            block = jnp.where(row == 2 * n, line[:, :LANES], block)
            block = jnp.where(row == 2 * n + 1, line[:, LANES:], block)
        ref[slot, 2 * TILE :, :] = block.astype(bf16)


def join_kernel(own_ref, other_ref, same_ref, odd_ref):
    for i, ref in enumerate((same_ref, odd_ref)):
        ref[0] = own_ref[i]
        ref[1] = other_ref[i]


def row_position(k):
    x = (lax.axis_index(ROW) + X - k) % X
    return (lax.axis_index("y") * X + x) * POS + lax.broadcasted_iota(jnp.int32, (1, TILE), 1) % POS


def key_positions(block, count):
    index = lax.broadcasted_iota(jnp.int32, (count, 1), 0)
    source = block * (count // POS) + index // POS
    ctx = source // 2 * X + 2 * lax.axis_index("xh") + source % 2
    return ctx * POS + index % POS


def row_stats(lengths_ref, block, k, j):
    block = block.astype(f32)
    lse = jnp.concatenate([block[0:1], block[1:2]], axis=1) * LOG2E
    delta = jnp.concatenate([block[2:3], block[3:4]], axis=1)
    core = lax.axis_index("pair")
    response = core + j - 2 * core * j
    return jnp.where(row_position(k) < lengths_ref[0, 1 + response], lse, DEAD), delta


def cell(key, value, query, grad, lse, delta, allowed=None):
    scores = dot(key, query, ((1,), (1,)))
    weights = jnp.exp2(scores * (SCALE * LOG2E) - lse)
    if allowed is not None:
        weights = jnp.where(allowed, weights, 0.0)
    weight_grads = dot(value, grad, ((1,), (1,)))
    score_grads = (weights * (weight_grads - delta)).astype(bf16)
    return weights.astype(bf16), score_grads


def staged(blocks, first, second):
    for i, block in enumerate(blocks):
        first(*block, i % 2)
        if i:
            second(*blocks[i - 1], (i - 1) % 2)
    second(*blocks[-1], (len(blocks) - 1) % 2)


def tile_rows(tile):
    return slice(tile * TILE, (tile + 1) * TILE)


def prompt_kernel(first_half, lengths_ref, qa, qb, kv_ref, *refs):
    if first_half:
        key_sum, value_sum = refs[:2]
    else:
        key_sum, value_sum, out_ref = refs[:3]
    query_rows, grad_rows, lse_ref, delta_ref, weights, score_grads = refs[-6:]
    for n, ref in enumerate((qa, qb)):
        for j in range(2):
            t = j * 2 + n
            at = tile_rows(t)
            query_rows[at, :] = ref[j, 0:TILE, :]
            grad_rows[at, :] = ref[j, TILE : 2 * TILE, :]
            k = n if first_half else 2 + n
            lse, delta = row_stats(lengths_ref, ref[j, 2 * TILE :, :], k, j)
            lse_ref[t : t + 1, :], delta_ref[t : t + 1, :] = lse, delta
    per = PROMPT_BLOCK // PROMPT

    def first(c, slot):
        rows = slice(c * per, (c + 1) * per)
        key = kv_ref[rows, 0:PROMPT, :].reshape(PROMPT_BLOCK, LANES)
        value = kv_ref[rows, PROMPT : 2 * PROMPT, :].reshape(PROMPT_BLOCK, LANES)
        for t in range(X):
            at = tile_rows(t)
            weights[slot, :, at], score_grads[slot, :, at] = cell(
                key, value, query_rows[at, :], grad_rows[at, :], lse_ref[t : t + 1, :], delta_ref[t : t + 1, :]
            )

    def second(c, slot):
        value_grad = dot(weights[slot], grad_rows[...], ((1,), (0,)))
        key_grad = dot(score_grads[slot], query_rows[...], ((1,), (0,)))
        at = slice(c * PROMPT_BLOCK, (c + 1) * PROMPT_BLOCK)
        if first_half:
            key_sum[at, :], value_sum[at, :] = key_grad, value_grad
        else:
            shape = (per, PROMPT, LANES)
            to = slice(c * per, (c + 1) * per)
            out_ref[to, 0:PROMPT, :] = ((key_sum[at, :] + key_grad) * SCALE).astype(bf16).reshape(shape)
            out_ref[to, PROMPT:, :] = (value_sum[at, :] + value_grad).astype(bf16).reshape(shape)

    staged([(c,) for c in range(PEERS_N // per)], first, second)


def resp_kernel(
    kv_ref, side_ref, prompt_ref, query_a, grad_a, lse_a, delta_a, query_b, grad_b, lse_b, delta_b,
    out_hbm, margin_ref, weights, score_grads, parts, sems,
):
    halves = ((query_a, grad_a, lse_a, delta_a), (query_b, grad_b, lse_b, delta_b))
    copies = [pltpu.make_async_copy(prompt_ref, out_hbm.at[:, 0 : 2 * PROMPT, :], sems.at[0])]
    copies[0].start()
    margin = jnp.sum(kv_ref[:, KV_ROWS:, :].astype(f32), axis=(0, 1), keepdims=True).reshape(1, LANES)
    margin = jnp.sum(margin, axis=1, keepdims=True)
    margin_ref[...] = jnp.broadcast_to(margin, margin_ref.shape)
    per = BLOCK // POS
    blocks = PEERS_N // per
    sources = ((kv_ref, 2 * PROMPT), (side_ref, 0))

    def first(j, c, slot):
        ref, start = sources[j]
        rows = slice(c * per, (c + 1) * per)
        key = ref[rows, start : start + POS, :].reshape(BLOCK, LANES)
        value = ref[rows, start + POS : start + SIDE, :].reshape(BLOCK, LANES)
        positions = key_positions(c, BLOCK)
        for k in range(X):
            query_rows, grad_rows, lse_ref, delta_ref = halves[k // 2]
            t = j * 2 + k % 2
            at, to = tile_rows(t), tile_rows(k)
            weights[slot, :, to], score_grads[slot, :, to] = cell(
                key,
                value,
                query_rows[at, :],
                grad_rows[at, :],
                lse_ref[t : t + 1, :],
                delta_ref[t : t + 1, :],
                positions <= row_position(k),
            )

    def second(j, c, slot):
        rows = slice(j * 2 * TILE, (j + 1) * 2 * TILE)
        value_grad, key_grad = None, None
        for n, (query_rows, grad_rows, _, _) in enumerate(halves):
            columns = slice(n * 2 * TILE, (n + 1) * 2 * TILE)
            value_term = dot(weights[slot, :, columns], grad_rows[rows, :], ((1,), (0,)))
            key_term = dot(score_grads[slot, :, columns], query_rows[rows, :], ((1,), (0,)))
            value_grad = value_term if n == 0 else value_grad + value_term
            key_grad = key_term if n == 0 else key_grad + key_term
        key_grad *= SCALE
        shape = (per, POS, LANES)
        n = j * blocks + c
        parts[n, :, 0:POS, :] = key_grad.astype(bf16).reshape(shape)
        parts[n, :, POS:, :] = value_grad.astype(bf16).reshape(shape)
        start = 2 * PROMPT + j * SIDE
        to = out_hbm.at[c * per : (c + 1) * per, start : start + SIDE, :]
        copies.append(pltpu.make_async_copy(parts.at[n], to, sems.at[1 + n]))
        copies[-1].start()

    staged([(j, c) for j in range(2) for c in range(blocks)], first, second)
    for copy in copies:
        copy.wait()


def query_kernel(k, lengths_ref, margin_ref, q_ref, kv_ref, side_ref, out_ref):
    items = []
    for j in range(2):
        resp, start = ((kv_ref, 2 * PROMPT), (side_ref, 0))[j]
        items += [(j, kv_ref, c, PROMPT, 0) for c in range(PEERS_N * PROMPT // BLOCK)]
        items += [(j, resp, c, POS, start) for c in range(PEERS_N * POS // BLOCK)]
    totals, waiting = [None, None], None
    for item in items + [None]:
        if item:
            j, ref, c, count, start = item
            per = BLOCK // count
            rows = slice(c * per, (c + 1) * per)
            key = ref[rows, start : start + count, :].reshape(BLOCK, LANES)
            value = ref[rows, start + count : start + 2 * count, :].reshape(BLOCK, LANES)
            allowed = key_positions(c, BLOCK) <= row_position(k) if count == POS else None
            lse, delta = row_stats(lengths_ref, q_ref[j, 2 * TILE :, :], k, j)
            _, score_grads = cell(
                key, value, q_ref[j, 0:TILE, :], q_ref[j, TILE : 2 * TILE, :], lse, delta, allowed
            )
        if waiting:
            n, grads, keys = waiting
            term = dot(grads, keys, ((0,), (0,)))
            totals[n] = term if totals[n] is None else totals[n] + term
        waiting = (j, score_grads, key)
    for j in range(2):
        out_ref[tile_rows(j), :] = (totals[j] * SCALE).astype(bf16)
    if k == 2:
        out_ref[2 * TILE :, :] = split_margin(margin_ref[0:1, 0:1], STAT_ROWS)


def kv_final_kernel(lengths_ref, margin_ref, d2, part_ref, pk_ref, pv_ref, rk_ref, rv_ref):
    gate = gate_of(margin_ref[0:1, 0:1], d2[2 * TILE :, :])
    core = lax.axis_index("pair")
    live = lax.axis_index(CTX) * PROMPT + lax.broadcasted_iota(jnp.int32, (PROMPT, LANES), 0) < lengths_ref[0, 0]
    for xl in range(2):
        columns = slice(xl * LANES, (xl + 1) * LANES)
        total = part_ref[xl].astype(f32)
        for y in range(1, ROWS_Y):
            total += part_ref[y * 2 + xl].astype(f32)
        total = total * gate
        pk_ref[0, :, columns] = jnp.where(live, total[0:PROMPT], 0.0).astype(bf16)
        pv_ref[0, :, columns] = jnp.where(live, total[PROMPT : 2 * PROMPT], 0.0).astype(bf16)
        for j in range(2):
            response = core + j - 2 * core * j
            at = 2 * PROMPT + j * SIDE
            rk_ref[0, response, :, columns] = total[at : at + POS].astype(bf16)
            rv_ref[0, response, :, columns] = total[at + POS : at + SIDE].astype(bf16)


def query_final_kernel(margin_ref, d0, d1, d2, d3, out_ref, gate_ref):
    gate = gate_of(margin_ref[0:1, 0:1], d2[2 * TILE :, :])
    gate_ref[...] = jnp.broadcast_to(gate, gate_ref.shape)
    core = lax.axis_index("pair")
    even = lax.axis_index("xl") == 0
    for j in range(2):
        response = core + j - 2 * core * j
        for h in range(GROUP):
            rows = slice(j * TILE + h * POS, j * TILE + (h + 1) * POS)
            same = gate * (d0[rows, :].astype(f32) + d2[rows, :].astype(f32))
            odd = gate * (d1[rows, :].astype(f32) + d3[rows, :].astype(f32))
            first, second = jnp.where(even, same, odd), jnp.where(even, odd, same)
            out_ref[0, response, :, h * LANES : (h + 1) * LANES] = first.astype(bf16)
            out_ref[0, response, :, (GROUP + h) * LANES : (GROUP + h + 1) * LANES] = second.astype(bf16)


def swap(values):
    return lax.all_to_all(values, PEERS, split_axis=0, concat_axis=0, tiled=True)


def cross(values):
    return lax.ppermute(values, "pair", [(0, 1), (1, 0)])


def shift(values, by):
    return lax.ppermute(values, ROW, [(i, (i + by) % X) for i in range(X)])


def prompt_call(lengths, rows, kv):
    shape = jax.ShapeDtypeStruct
    count = X * TILE
    tables = (
        shape((count, LANES), bf16),
        shape((count, LANES), bf16),
        shape((X, TILE), f32),
        shape((X, TILE), f32),
    )
    sums = (shape((PEERS_N * PROMPT, LANES), f32),) * 2
    scratch = (pltpu.VMEM((2, PROMPT_BLOCK, count), bf16), pltpu.VMEM((2, PROMPT_BLOCK, count), bf16))
    cost = dict(flops=2 * 2 * 2048 * 1024 * 128 * 2, size=2 * 2**20, scratch=scratch)
    key_sum, value_sum, *first = call(functools.partial(prompt_kernel, True), sums + tables, "svvv", **cost)(
        lengths, rows[0], rows[1], kv
    )
    part, *second = call(
        functools.partial(prompt_kernel, False),
        (shape((PEERS_N, 2 * PROMPT, LANES), bf16),) + tables,
        "svvvvv",
        **cost,
    )(lengths, rows[2], rows[3], kv, key_sum, value_sum)
    return part, *first, *second


def resp_call(kv, side, prompt_part, *rows):
    shape = jax.ShapeDtypeStruct
    blocks = 2 * PEERS_N * POS // BLOCK
    return call(
        resp_kernel,
        (
            shape((PEERS_N, KV_ROWS, LANES), bf16),
            shape((8, LANES), f32),
        ),
        "v" * 11,
        out_spaces="av",
        scratch=(
            pltpu.VMEM((2, BLOCK, X * TILE), bf16),
            pltpu.VMEM((2, BLOCK, X * TILE), bf16),
            pltpu.VMEM((blocks, BLOCK // POS, SIDE, LANES), bf16),
            pltpu.SemaphoreType.DMA((blocks + 1,)),
        ),
        flops=4 * 2 * 1024 * 1024 * 128 * 2,
        size=3 * 2**20,
    )(kv, side, prompt_part, *rows)


def query_call(k, lengths, margin, rows, kv, side):
    extra = STAT_ROWS if k == 2 else 0
    return call(
        functools.partial(query_kernel, k),
        jax.ShapeDtypeStruct((2 * TILE + extra, LANES), bf16),
        "svvvv",
        flops=3 * 2 * 512 * 1536 * 128 * 2,
        size=3 * 2**20,
    )(lengths, margin, rows, kv, side)


def per_device(
    prompt_keys,
    prompt_values,
    queries,
    resp_keys,
    resp_values,
    resp_grads,
    resp_lse,
    resp_delta,
    logratio,
    lengths,
):
    shape = jax.ShapeDtypeStruct
    kv = call(
        kv_pack_kernel,
        shape((PEERS_N, KV_ROWS + MARGIN_ROWS, LANES), bf16),
        "aaaaaa",
        size=2 * 2**20,
        limit=60,
        scratch=(
            pltpu.SMEM((1, 3), jnp.int32),
            pltpu.VMEM((2, POS), f32),
            pltpu.VMEM((PROMPT, 2 * LANES), bf16),
            pltpu.VMEM((PROMPT, 2 * LANES), bf16),
            pltpu.VMEM((POS, X * LANES), bf16),
            pltpu.VMEM((POS, X * LANES), bf16),
            pltpu.SemaphoreType.DMA((6,)),
        ),
    )(lengths, logratio, prompt_keys, prompt_values, resp_keys, resp_values)
    kv = swap(kv)

    block = shape((2, QUERY_ROWS, LANES), bf16)
    own, other = call(
        query_pack_kernel,
        (block, block),
        "aaaa",
        size=2 * 2**20,
        scratch=(
            pltpu.VMEM((4, POS, GROUP * LANES), bf16),
            pltpu.VMEM((4, POS, GROUP * LANES), bf16),
            pltpu.VMEM((POS, X * GROUP), bf16),
            pltpu.VMEM((POS, X * GROUP), bf16),
            pltpu.SemaphoreType.DMA((10,)),
        ),
    )(queries, resp_grads, resp_lse, resp_delta)
    same, odd = call(join_kernel, (block, block), "vv", size=2**20)(own, cross(other))
    rows = (same, shift(odd, 1), shift(same, 2), shift(odd, 3))

    side = cross(kv[:, KV_ROWS - SIDE : KV_ROWS, :])
    prompt_part, *tables = prompt_call(lengths, rows, kv)
    part, margin = resp_call(kv, side, prompt_part, *tables)
    grads = [query_call(k, lengths, margin, rows[k], kv, side) for k in range(X)]
    part = swap(part)
    back = [grads[0]] + [shift(grads[k], X - k) for k in range(1, X)]
    query_grad, gate = call(
        query_final_kernel,
        (shape((1, 2, POS, 2 * GROUP * LANES), bf16), shape((8, LANES), f32)),
        "vvvvv",
        size=2**20,
    )(margin, *back)
    outs = (shape((1, PROMPT, 2 * LANES), bf16),) * 2 + (shape((1, 2, POS, 2 * LANES), bf16),) * 2
    pk_grad, pv_grad, key_grad, value_grad = call(kv_final_kernel, outs, "svvv", size=2**20)(
        lengths, margin, back[2], part
    )
    return pk_grad, pv_grad, query_grad, key_grad, value_grad, gate[0, 0:1]


def solution(mesh):
    batch, pair, ctx = mesh.devices.shape
    split = Mesh(mesh.devices.reshape(batch, pair, ctx // X, 2, 2), ("batch", "pair", "y", "xh", "xl"))
    prompt_spec = P("batch", CTX, "pair")
    resp_spec = P("batch", "pair", CTX, None)
    out_spec = P("batch", None, CTX, "pair")
    return jax.shard_map(
        per_device,
        mesh=split,
        in_specs=(
            prompt_spec,
            prompt_spec,
            resp_spec,
            resp_spec,
            resp_spec,
            resp_spec,
            resp_spec,
            resp_spec,
            P("batch", None, CTX),
            P("batch", None),
        ),
        out_specs=(prompt_spec, prompt_spec, out_spec, out_spec, out_spec, P("batch")),
        check_vma=False,
    )
```

```python
import functools

import jax
import jax.numpy as jnp
from jax import lax
from jax.experimental import pallas as pl
from jax.experimental.pallas import tpu as pltpu
from jax.sharding import Mesh, PartitionSpec as P

beta_coef = 0.1
f32, bf16 = jnp.float32, jnp.bfloat16
LANES = 128
CTX = ("y", "xh", "xl")
ROW = ("xh", "xl")
PEERS = ("y", "xl")

X = 4
ROWS_Y = 8
PEERS_N = 16
POS = 32
PROMPT = 64
GROUP = 8
TILE = POS * GROUP
STAT_ROWS = 16
QUERY_ROWS = 2 * TILE + STAT_ROWS
SIDE = 2 * POS
KV_ROWS = 2 * PROMPT + 2 * SIDE
LOG2E = 1.4426950408889634
SCALE = LANES**-0.5
DEAD = 1e30
BLOCK = 512
PROMPT_BLOCK = 256
MARGIN_ROWS = 8


def dot(a, b, dims):
    return lax.dot_general(a, b, (dims, ((), ())), preferred_element_type=f32)


def call(kernel, out_shape, spaces, flops=0, scratch=(), size=0, limit=24, out_spaces=""):
    space = {"v": pltpu.VMEM, "s": pltpu.SMEM, "a": pl.ANY}
    many = isinstance(out_shape, tuple)
    out_spaces = out_spaces or "v" * (len(out_shape) if many else 1)
    out_specs = tuple(pl.BlockSpec(memory_space=space[s]) for s in out_spaces)
    return pl.pallas_call(
        kernel,
        out_shape=out_shape,
        in_specs=[pl.BlockSpec(memory_space=space[s]) for s in spaces],
        out_specs=out_specs if many else out_specs[0],
        scratch_shapes=list(scratch),
        compiler_params=pltpu.CompilerParams(vmem_limit_bytes=limit * 2**20),
        cost_estimate=pl.CostEstimate(flops=flops, bytes_accessed=size, transcendentals=0),
    )


def fetch(pairs, sems):
    copies = [pltpu.make_async_copy(a, b, sems.at[i]) for i, (a, b) in enumerate(pairs)]
    for copy in copies:
        copy.start()
    for copy in copies:
        copy.wait()


def split_margin(margin, rows):
    high = margin.astype(bf16).astype(f32)
    middle = (margin - high).astype(bf16).astype(f32)
    low = margin - high - middle
    lane = lax.broadcasted_iota(jnp.int32, (rows, LANES), 1)
    row = lax.broadcasted_iota(jnp.int32, (rows, LANES), 0)
    block = jnp.where(lane == 0, high, jnp.where(lane == 1, middle, jnp.where(lane == 2, low, 0.0)))
    return jnp.where(row == 0, block, 0.0).astype(bf16)


def gate_of(margin, block):
    other = jnp.sum(block.astype(f32), axis=0, keepdims=True)
    margin = margin + jnp.sum(other, axis=1, keepdims=True)
    return beta_coef * jax.nn.sigmoid(-beta_coef * margin)


def kv_pack_kernel(
    lengths_hbm, logratio_hbm, pk_hbm, pv_hbm, rk_hbm, rv_hbm, kv_ref, lengths, logratio, pk, pv, rk, rv, sems
):
    pairs = (
        (lengths_hbm, lengths),
        (logratio_hbm.at[0], logratio),
        (pk_hbm.at[0], pk),
        (pv_hbm.at[0], pv),
        (rk_hbm.at[0, 0], rk),
        (rv_hbm.at[0, 0], rv),
    )
    fetch(pairs, sems)
    first_core = lax.axis_index("pair") == 0
    ctx = lax.axis_index(CTX)
    position = ctx * POS + lax.broadcasted_iota(jnp.int32, (1, POS), 1)
    chosen = jnp.where(position < lengths[0, 1], logratio[0:1, :], 0.0)
    rejected = jnp.where(position < lengths[0, 2], logratio[1:2, :], 0.0)
    margin = jnp.sum(chosen - rejected, axis=1, keepdims=True)
    block = split_margin(margin, MARGIN_ROWS)
    live = ctx * PROMPT + lax.broadcasted_iota(jnp.int32, (PROMPT, LANES), 0) < lengths[0, 0]
    for xl in range(2):
        columns = slice(xl * LANES, (xl + 1) * LANES)
        others = slice((2 + xl) * LANES, (3 + xl) * LANES)
        parts = [jnp.where(live, pk[:, columns].astype(f32), 0.0).astype(bf16), pv[:, columns]]
        low_head = [ref[:, columns].astype(f32) for ref in (rk, rv)]
        high_head = [ref[:, others].astype(f32) for ref in (rk, rv)]
        parts += [jnp.where(first_core, a, b).astype(bf16) for a, b in zip(low_head, high_head)]
        parts += [jnp.where(first_core, b, a).astype(bf16) for a, b in zip(low_head, high_head)]
        parts += [block]
        for y in range(ROWS_Y):
            at = 0
            for part in parts:
                kv_ref[y * 2 + xl, at : at + part.shape[0], :] = part
                at += part.shape[0]


def query_pack_kernel(q_hbm, g_hbm, lse_hbm, delta_hbm, own_ref, other_ref, q, g, lse, delta, sems):
    core, parity = lax.axis_index("pair"), lax.axis_index("xl")
    pairs = [(lse_hbm.at[0, 0], lse), (delta_hbm.at[0, 0], delta)]
    heads = []
    for i in range(4):
        head = 2 * (core if i < 2 else 1 - core) + (parity + i) % 2
        heads.append(head)
        columns = pl.ds(pl.multiple_of(head * GROUP * LANES, GROUP * LANES), GROUP * LANES)
        pairs += [(q_hbm.at[0, 0, :, columns], q.at[i]), (g_hbm.at[0, 0, :, columns], g.at[i])]
    fetch(pairs, sems)
    sign = jnp.where(core == 0, -1.0, 1.0).astype(f32)

    count = X * GROUP
    lane = lax.broadcasted_iota(jnp.int32, (POS, TILE), 1)
    spread = (lane % POS == lax.broadcasted_iota(jnp.int32, (POS, TILE), 0)).astype(bf16)
    head_of = lax.broadcasted_iota(jnp.int32, (count, TILE), 0)
    lane = lax.broadcasted_iota(jnp.int32, (count, TILE), 1)
    lse_rows = dot(lse[...], spread, ((0,), (0,)))
    delta_rows = dot(delta[...], spread, ((0,), (0,))) * sign
    row = lax.broadcasted_iota(jnp.int32, (STAT_ROWS, LANES), 0)
    for i in range(4):
        ref, slot = (own_ref, other_ref)[i // 2], i % 2
        for h in range(GROUP):
            columns = slice(h * LANES, (h + 1) * LANES)
            ref[slot, h * POS : (h + 1) * POS, :] = q[i, :, columns]
            grad = (g[i, :, columns].astype(f32) * sign).astype(bf16)
            ref[slot, TILE + h * POS : TILE + (h + 1) * POS, :] = grad
        keep = head_of == heads[i] * GROUP + lane // POS
        block = jnp.zeros((STAT_ROWS, LANES), f32)
        for n, rows in enumerate((lse_rows, delta_rows)):
            line = jnp.sum(jnp.where(keep, rows, 0.0), axis=0, keepdims=True)
            block = jnp.where(row == 2 * n, line[:, :LANES], block)
            block = jnp.where(row == 2 * n + 1, line[:, LANES:], block)
        ref[slot, 2 * TILE :, :] = block.astype(bf16)


def join_kernel(own_ref, other_ref, same_ref, odd_ref):
    for i, ref in enumerate((same_ref, odd_ref)):
        ref[0] = own_ref[i]
        ref[1] = other_ref[i]


def row_position(k):
    x = (lax.axis_index(ROW) + X - k) % X
    return (lax.axis_index("y") * X + x) * POS + lax.broadcasted_iota(jnp.int32, (1, TILE), 1) % POS


def key_positions(block, count):
    index = lax.broadcasted_iota(jnp.int32, (count, 1), 0)
    source = block * (count // POS) + index // POS
    ctx = source // 2 * X + 2 * lax.axis_index("xh") + source % 2
    return ctx * POS + index % POS


def row_stats(lengths_ref, block, k, j):
    block = block.astype(f32)
    lse = jnp.concatenate([block[0:1], block[1:2]], axis=1) * LOG2E
    delta = jnp.concatenate([block[2:3], block[3:4]], axis=1)
    core = lax.axis_index("pair")
    response = core + j - 2 * core * j
    return jnp.where(row_position(k) < lengths_ref[0, 1 + response], lse, DEAD), delta


def cell(key, value, query, grad, lse, delta, allowed=None):
    scores = dot(key, query, ((1,), (1,)))
    weights = jnp.exp2(scores * (SCALE * LOG2E) - lse)
    if allowed is not None:
        weights = jnp.where(allowed, weights, 0.0)
    weight_grads = dot(value, grad, ((1,), (1,)))
    score_grads = (weights * (weight_grads - delta)).astype(bf16)
    return weights.astype(bf16), score_grads


def staged(blocks, first, second):
    for i, block in enumerate(blocks):
        first(*block, i % 2)
        if i:
            second(*blocks[i - 1], (i - 1) % 2)
    second(*blocks[-1], (len(blocks) - 1) % 2)


def tile_rows(tile):
    return slice(tile * TILE, (tile + 1) * TILE)


def prompt_kernel(first_half, lengths_ref, qa, qb, kv_ref, *refs):
    if first_half:
        key_sum, value_sum = refs[:2]
    else:
        key_sum, value_sum, out_ref = refs[:3]
    query_rows, grad_rows, lse_ref, delta_ref, weights, score_grads = refs[-6:]
    for n, ref in enumerate((qa, qb)):
        for j in range(2):
            t = j * 2 + n
            at = tile_rows(t)
            query_rows[at, :] = ref[j, 0:TILE, :]
            grad_rows[at, :] = ref[j, TILE : 2 * TILE, :]
            k = n if first_half else 2 + n
            lse, delta = row_stats(lengths_ref, ref[j, 2 * TILE :, :], k, j)
            lse_ref[t : t + 1, :], delta_ref[t : t + 1, :] = lse, delta
    per = PROMPT_BLOCK // PROMPT

    def first(c, slot):
        rows = slice(c * per, (c + 1) * per)
        key = kv_ref[rows, 0:PROMPT, :].reshape(PROMPT_BLOCK, LANES)
        value = kv_ref[rows, PROMPT : 2 * PROMPT, :].reshape(PROMPT_BLOCK, LANES)
        for t in range(X):
            at = tile_rows(t)
            weights[slot, :, at], score_grads[slot, :, at] = cell(
                key, value, query_rows[at, :], grad_rows[at, :], lse_ref[t : t + 1, :], delta_ref[t : t + 1, :]
            )

    def second(c, slot):
        value_grad = dot(weights[slot], grad_rows[...], ((1,), (0,)))
        key_grad = dot(score_grads[slot], query_rows[...], ((1,), (0,)))
        at = slice(c * PROMPT_BLOCK, (c + 1) * PROMPT_BLOCK)
        if first_half:
            key_sum[at, :], value_sum[at, :] = key_grad, value_grad
        else:
            shape = (per, PROMPT, LANES)
            to = slice(c * per, (c + 1) * per)
            out_ref[to, 0:PROMPT, :] = ((key_sum[at, :] + key_grad) * SCALE).astype(bf16).reshape(shape)
            out_ref[to, PROMPT:, :] = (value_sum[at, :] + value_grad).astype(bf16).reshape(shape)

    staged([(c,) for c in range(PEERS_N // per)], first, second)


def resp_kernel(
    kv_ref, side_ref, prompt_ref, query_a, grad_a, lse_a, delta_a, query_b, grad_b, lse_b, delta_b,
    out_hbm, margin_ref, weights, score_grads, parts, sems,
):
    halves = ((query_a, grad_a, lse_a, delta_a), (query_b, grad_b, lse_b, delta_b))
    copies = [pltpu.make_async_copy(prompt_ref, out_hbm.at[:, 0 : 2 * PROMPT, :], sems.at[0])]
    copies[0].start()
    margin = jnp.sum(kv_ref[:, KV_ROWS:, :].astype(f32), axis=(0, 1), keepdims=True).reshape(1, LANES)
    margin = jnp.sum(margin, axis=1, keepdims=True)
    margin_ref[...] = jnp.broadcast_to(margin, margin_ref.shape)
    per = BLOCK // POS
    blocks = PEERS_N // per
    sources = ((kv_ref, 2 * PROMPT), (side_ref, 0))

    def first(j, c, slot):
        ref, start = sources[j]
        rows = slice(c * per, (c + 1) * per)
        key = ref[rows, start : start + POS, :].reshape(BLOCK, LANES)
        value = ref[rows, start + POS : start + SIDE, :].reshape(BLOCK, LANES)
        positions = key_positions(c, BLOCK)
        for k in range(X):
            query_rows, grad_rows, lse_ref, delta_ref = halves[k // 2]
            t = j * 2 + k % 2
            at, to = tile_rows(t), tile_rows(k)
            weights[slot, :, to], score_grads[slot, :, to] = cell(
                key,
                value,
                query_rows[at, :],
                grad_rows[at, :],
                lse_ref[t : t + 1, :],
                delta_ref[t : t + 1, :],
                positions <= row_position(k),
            )

    def second(j, c, slot):
        rows = slice(j * 2 * TILE, (j + 1) * 2 * TILE)
        value_grad, key_grad = None, None
        for n, (query_rows, grad_rows, _, _) in enumerate(halves):
            columns = slice(n * 2 * TILE, (n + 1) * 2 * TILE)
            value_term = dot(weights[slot, :, columns], grad_rows[rows, :], ((1,), (0,)))
            key_term = dot(score_grads[slot, :, columns], query_rows[rows, :], ((1,), (0,)))
            value_grad = value_term if n == 0 else value_grad + value_term
            key_grad = key_term if n == 0 else key_grad + key_term
        key_grad *= SCALE
        shape = (per, POS, LANES)
        n = j * blocks + c
        parts[n, :, 0:POS, :] = key_grad.astype(bf16).reshape(shape)
        parts[n, :, POS:, :] = value_grad.astype(bf16).reshape(shape)
        start = 2 * PROMPT + j * SIDE
        to = out_hbm.at[c * per : (c + 1) * per, start : start + SIDE, :]
        copies.append(pltpu.make_async_copy(parts.at[n], to, sems.at[1 + n]))
        copies[-1].start()

    staged([(j, c) for j in range(2) for c in range(blocks)], first, second)
    for copy in copies:
        copy.wait()


def query_kernel(k, lengths_ref, margin_ref, q_ref, kv_ref, side_ref, out_ref):
    items = []
    for j in range(2):
        resp, start = ((kv_ref, 2 * PROMPT), (side_ref, 0))[j]
        items += [(j, kv_ref, c, PROMPT, 0) for c in range(PEERS_N * PROMPT // BLOCK)]
        items += [(j, resp, c, POS, start) for c in range(PEERS_N * POS // BLOCK)]
    totals, waiting = [None, None], None
    for item in items + [None]:
        if item:
            j, ref, c, count, start = item
            per = BLOCK // count
            rows = slice(c * per, (c + 1) * per)
            key = ref[rows, start : start + count, :].reshape(BLOCK, LANES)
            value = ref[rows, start + count : start + 2 * count, :].reshape(BLOCK, LANES)
            allowed = key_positions(c, BLOCK) <= row_position(k) if count == POS else None
            lse, delta = row_stats(lengths_ref, q_ref[j, 2 * TILE :, :], k, j)
            _, score_grads = cell(
                key, value, q_ref[j, 0:TILE, :], q_ref[j, TILE : 2 * TILE, :], lse, delta, allowed
            )
        if waiting:
            n, grads, keys = waiting
            term = dot(keys, grads, ((0,), (0,)))
            totals[n] = term if totals[n] is None else totals[n] + term
        waiting = (j, score_grads, key)
    for j in range(2):
        out_ref[tile_rows(j), :] = jnp.transpose(totals[j] * SCALE).astype(bf16)
    if k == 2:
        out_ref[2 * TILE :, :] = split_margin(margin_ref[0:1, 0:1], STAT_ROWS)


def final_kernel(
    lengths_ref, margin_ref, d0, d1, d2, d3, part_ref, pk_hbm, pv_hbm, q_hbm, rk_hbm, rv_hbm, gate_ref,
    pk, pv, q, rk, rv, sems,
):
    gate = gate_of(margin_ref[0:1, 0:1], d2[2 * TILE :, :])
    gate_ref[0] = gate[0, 0]
    core = lax.axis_index("pair")
    even = lax.axis_index("xl") == 0
    outs = ((q, q_hbm), (pk, pk_hbm), (pv, pv_hbm), (rk, rk_hbm), (rv, rv_hbm))
    copies = [pltpu.make_async_copy(ref, hbm.at[0], sems.at[i]) for i, (ref, hbm) in enumerate(outs)]
    for j in range(2):
        response = core + j - 2 * core * j
        for h in range(GROUP):
            rows = slice(j * TILE + h * POS, j * TILE + (h + 1) * POS)
            same = gate * (d0[rows, :].astype(f32) + d2[rows, :].astype(f32))
            odd = gate * (d1[rows, :].astype(f32) + d3[rows, :].astype(f32))
            first, second = jnp.where(even, same, odd), jnp.where(even, odd, same)
            q[response, :, h * LANES : (h + 1) * LANES] = first.astype(bf16)
            q[response, :, (GROUP + h) * LANES : (GROUP + h + 1) * LANES] = second.astype(bf16)
    copies[0].start()
    live = lax.axis_index(CTX) * PROMPT + lax.broadcasted_iota(jnp.int32, (PROMPT, LANES), 0) < lengths_ref[0, 0]
    for xl in range(2):
        columns = slice(xl * LANES, (xl + 1) * LANES)
        total = part_ref[xl].astype(f32)
        for y in range(1, ROWS_Y):
            total += part_ref[y * 2 + xl].astype(f32)
        total = total * gate
        pk[:, columns] = jnp.where(live, total[0:PROMPT], 0.0).astype(bf16)
        pv[:, columns] = jnp.where(live, total[PROMPT : 2 * PROMPT], 0.0).astype(bf16)
        for j in range(2):
            response = core + j - 2 * core * j
            at = 2 * PROMPT + j * SIDE
            rk[response, :, columns] = total[at : at + POS].astype(bf16)
            rv[response, :, columns] = total[at + POS : at + SIDE].astype(bf16)
    for copy in copies[1:]:
        copy.start()
    for copy in copies:
        copy.wait()


def swap(values):
    return lax.all_to_all(values, PEERS, split_axis=0, concat_axis=0, tiled=True)


def cross(values):
    return lax.ppermute(values, "pair", [(0, 1), (1, 0)])


def shift(values, by):
    return lax.ppermute(values, ROW, [(i, (i + by) % X) for i in range(X)])


def prompt_call(lengths, rows, kv):
    shape = jax.ShapeDtypeStruct
    count = X * TILE
    tables = (
        shape((count, LANES), bf16),
        shape((count, LANES), bf16),
        shape((X, TILE), f32),
        shape((X, TILE), f32),
    )
    sums = (shape((PEERS_N * PROMPT, LANES), f32),) * 2
    scratch = (pltpu.VMEM((2, PROMPT_BLOCK, count), bf16), pltpu.VMEM((2, PROMPT_BLOCK, count), bf16))
    cost = dict(flops=2 * 2 * 2048 * 1024 * 128 * 2, size=2 * 2**20, scratch=scratch)
    key_sum, value_sum, *first = call(functools.partial(prompt_kernel, True), sums + tables, "svvv", **cost)(
        lengths, rows[0], rows[1], kv
    )
    part, *second = call(
        functools.partial(prompt_kernel, False),
        (shape((PEERS_N, 2 * PROMPT, LANES), bf16),) + tables,
        "svvvvv",
        **cost,
    )(lengths, rows[2], rows[3], kv, key_sum, value_sum)
    return part, *first, *second


def resp_call(kv, side, prompt_part, *rows):
    shape = jax.ShapeDtypeStruct
    blocks = 2 * PEERS_N * POS // BLOCK
    return call(
        resp_kernel,
        (
            shape((PEERS_N, KV_ROWS, LANES), bf16),
            shape((8, LANES), f32),
        ),
        "v" * 11,
        out_spaces="av",
        scratch=(
            pltpu.VMEM((2, BLOCK, X * TILE), bf16),
            pltpu.VMEM((2, BLOCK, X * TILE), bf16),
            pltpu.VMEM((blocks, BLOCK // POS, SIDE, LANES), bf16),
            pltpu.SemaphoreType.DMA((blocks + 1,)),
        ),
        flops=4 * 2 * 1024 * 1024 * 128 * 2,
        size=3 * 2**20,
    )(kv, side, prompt_part, *rows)


def query_call(k, lengths, margin, rows, kv, side):
    extra = STAT_ROWS if k == 2 else 0
    return call(
        functools.partial(query_kernel, k),
        jax.ShapeDtypeStruct((2 * TILE + extra, LANES), bf16),
        "svvvv",
        flops=3 * 2 * 512 * 1536 * 128 * 2,
        size=3 * 2**20,
    )(lengths, margin, rows, kv, side)


def per_device(
    prompt_keys,
    prompt_values,
    queries,
    resp_keys,
    resp_values,
    resp_grads,
    resp_lse,
    resp_delta,
    logratio,
    lengths,
):
    shape = jax.ShapeDtypeStruct
    kv = call(
        kv_pack_kernel,
        shape((PEERS_N, KV_ROWS + MARGIN_ROWS, LANES), bf16),
        "aaaaaa",
        size=2 * 2**20,
        limit=60,
        scratch=(
            pltpu.SMEM((1, 3), jnp.int32),
            pltpu.VMEM((2, POS), f32),
            pltpu.VMEM((PROMPT, 2 * LANES), bf16),
            pltpu.VMEM((PROMPT, 2 * LANES), bf16),
            pltpu.VMEM((POS, X * LANES), bf16),
            pltpu.VMEM((POS, X * LANES), bf16),
            pltpu.SemaphoreType.DMA((6,)),
        ),
    )(lengths, logratio, prompt_keys, prompt_values, resp_keys, resp_values)
    kv = swap(kv)

    block = shape((2, QUERY_ROWS, LANES), bf16)
    own, other = call(
        query_pack_kernel,
        (block, block),
        "aaaa",
        size=2 * 2**20,
        scratch=(
            pltpu.VMEM((4, POS, GROUP * LANES), bf16),
            pltpu.VMEM((4, POS, GROUP * LANES), bf16),
            pltpu.VMEM((POS, X * GROUP), bf16),
            pltpu.VMEM((POS, X * GROUP), bf16),
            pltpu.SemaphoreType.DMA((10,)),
        ),
    )(queries, resp_grads, resp_lse, resp_delta)
    same, odd = call(join_kernel, (block, block), "vv", size=2**20)(own, cross(other))
    rows = (same, shift(odd, 1), shift(same, 2), shift(odd, 3))

    side = cross(kv[:, KV_ROWS - SIDE : KV_ROWS, :])
    prompt_part, *tables = prompt_call(lengths, rows, kv)
    part, margin = resp_call(kv, side, prompt_part, *tables)
    grads = [query_call(k, lengths, margin, rows[k], kv, side) for k in range(X)]
    part = swap(part)
    back = [grads[0]] + [shift(grads[k], X - k) for k in range(1, X)]
    prompt_out, resp_out = shape((1, PROMPT, 2 * LANES), bf16), shape((1, 2, POS, 2 * LANES), bf16)
    query_out = shape((1, 2, POS, 2 * GROUP * LANES), bf16)
    outs = (prompt_out, prompt_out, query_out, resp_out, resp_out)
    return call(
        final_kernel,
        outs + (shape((1,), f32),),
        "svvvvvv",
        out_spaces="aaaaas",
        scratch=[pltpu.VMEM(out.shape[1:], bf16) for out in outs]
        + [pltpu.SemaphoreType.DMA((5,))],
        size=2 * 2**20,
    )(lengths, margin, *back, part)


def solution(mesh):
    batch, pair, ctx = mesh.devices.shape
    split = Mesh(mesh.devices.reshape(batch, pair, ctx // X, 2, 2), ("batch", "pair", "y", "xh", "xl"))
    prompt_spec = P("batch", CTX, "pair")
    resp_spec = P("batch", "pair", CTX, None)
    out_spec = P("batch", None, CTX, "pair")
    return jax.shard_map(
        per_device,
        mesh=split,
        in_specs=(
            prompt_spec,
            prompt_spec,
            resp_spec,
            resp_spec,
            resp_spec,
            resp_spec,
            resp_spec,
            resp_spec,
            P("batch", None, CTX),
            P("batch", None),
        ),
        out_specs=(prompt_spec, prompt_spec, out_spec, out_spec, out_spec, P("batch")),
        check_vma=False,
    )
```

```python
import functools

import jax
import jax.numpy as jnp
from jax import lax
from jax.experimental import pallas as pl
from jax.experimental.pallas import tpu as pltpu
from jax.sharding import Mesh, PartitionSpec as P

beta_coef = 0.1
f32, bf16 = jnp.float32, jnp.bfloat16
LANES = 128
CTX = ("y", "xh", "xl")
ROW = ("xh", "xl")
PEERS = ("y", "xl")

X = 4
ROWS_Y = 8
PEERS_N = 16
POS = 32
PROMPT = 64
GROUP = 8
TILE = POS * GROUP
STAT_ROWS = 16
QUERY_ROWS = 2 * TILE + STAT_ROWS
SIDE = 2 * POS
KV_ROWS = 2 * PROMPT + 2 * SIDE
LOG2E = 1.4426950408889634
SCALE = LANES**-0.5
DEAD = 1e30
BLOCK = 512
PROMPT_BLOCK = 256
MARGIN_ROWS = 8


def dot(a, b, dims):
    return lax.dot_general(a, b, (dims, ((), ())), preferred_element_type=f32)


def call(kernel, out_shape, spaces, flops=0, scratch=(), size=0, limit=24, out_spaces=""):
    space = {"v": pltpu.VMEM, "s": pltpu.SMEM, "a": pl.ANY}
    many = isinstance(out_shape, tuple)
    out_spaces = out_spaces or "v" * (len(out_shape) if many else 1)
    out_specs = tuple(pl.BlockSpec(memory_space=space[s]) for s in out_spaces)
    return pl.pallas_call(
        kernel,
        out_shape=out_shape,
        in_specs=[pl.BlockSpec(memory_space=space[s]) for s in spaces],
        out_specs=out_specs if many else out_specs[0],
        scratch_shapes=list(scratch),
        compiler_params=pltpu.CompilerParams(vmem_limit_bytes=limit * 2**20),
        cost_estimate=pl.CostEstimate(flops=flops, bytes_accessed=size, transcendentals=0),
    )


def fetch(pairs, sems):
    copies = [pltpu.make_async_copy(a, b, sems.at[i]) for i, (a, b) in enumerate(pairs)]
    for copy in copies:
        copy.start()
    for copy in copies:
        copy.wait()


def split_margin(margin, rows):
    high = margin.astype(bf16).astype(f32)
    middle = (margin - high).astype(bf16).astype(f32)
    low = margin - high - middle
    lane = lax.broadcasted_iota(jnp.int32, (rows, LANES), 1)
    row = lax.broadcasted_iota(jnp.int32, (rows, LANES), 0)
    block = jnp.where(lane == 0, high, jnp.where(lane == 1, middle, jnp.where(lane == 2, low, 0.0)))
    return jnp.where(row == 0, block, 0.0).astype(bf16)


def gate_of(margin, block):
    other = jnp.sum(block.astype(f32), axis=0, keepdims=True)
    margin = margin + jnp.sum(other, axis=1, keepdims=True)
    return beta_coef * jax.nn.sigmoid(-beta_coef * margin)


def kv_pack_kernel(
    lengths_hbm, logratio_hbm, pk_hbm, pv_hbm, rk_hbm, rv_hbm, kv_hbm, lengths, logratio, pk, pv, rk, rv, kv_ref, sems
):
    pairs = (
        (lengths_hbm, lengths),
        (logratio_hbm.at[0], logratio),
        (pk_hbm.at[0], pk),
        (pv_hbm.at[0], pv),
        (rk_hbm.at[0, 0], rk),
        (rv_hbm.at[0, 0], rv),
    )
    fetch(pairs, sems)
    first_core = lax.axis_index("pair") == 0
    ctx = lax.axis_index(CTX)
    position = ctx * POS + lax.broadcasted_iota(jnp.int32, (1, POS), 1)
    chosen = jnp.where(position < lengths[0, 1], logratio[0:1, :], 0.0)
    rejected = jnp.where(position < lengths[0, 2], logratio[1:2, :], 0.0)
    margin = jnp.sum(chosen - rejected, axis=1, keepdims=True)
    block = split_margin(margin, MARGIN_ROWS)
    live = ctx * PROMPT + lax.broadcasted_iota(jnp.int32, (PROMPT, LANES), 0) < lengths[0, 0]
    for xl in range(2):
        columns = slice(xl * LANES, (xl + 1) * LANES)
        others = slice((2 + xl) * LANES, (3 + xl) * LANES)
        parts = [jnp.where(live, pk[:, columns].astype(f32), 0.0).astype(bf16), pv[:, columns]]
        low_head = [ref[:, columns].astype(f32) for ref in (rk, rv)]
        high_head = [ref[:, others].astype(f32) for ref in (rk, rv)]
        parts += [jnp.where(first_core, a, b).astype(bf16) for a, b in zip(low_head, high_head)]
        parts += [jnp.where(first_core, b, a).astype(bf16) for a, b in zip(low_head, high_head)]
        parts += [block]
        at = 0
        for part in parts:
            kv_ref[xl, at : at + part.shape[0], :] = part
            at += part.shape[0]
    copies = [
        pltpu.make_async_copy(kv_ref, kv_hbm.at[2 * y : 2 * y + 2], sems.at[6 + y]) for y in range(ROWS_Y)
    ]
    for copy in copies:
        copy.start()
    for copy in copies:
        copy.wait()


def query_pack_kernel(q_hbm, g_hbm, lse_hbm, delta_hbm, own_ref, other_ref, q, g, lse, delta, sems):
    core, parity = lax.axis_index("pair"), lax.axis_index("xl")
    pairs = [(lse_hbm.at[0, 0], lse), (delta_hbm.at[0, 0], delta)]
    heads = []
    for i in range(4):
        head = 2 * (core if i < 2 else 1 - core) + (parity + i) % 2
        heads.append(head)
        columns = pl.ds(pl.multiple_of(head * GROUP * LANES, GROUP * LANES), GROUP * LANES)
        pairs += [(q_hbm.at[0, 0, :, columns], q.at[i]), (g_hbm.at[0, 0, :, columns], g.at[i])]
    fetch(pairs, sems)
    sign = jnp.where(core == 0, -1.0, 1.0).astype(f32)

    count = X * GROUP
    lane = lax.broadcasted_iota(jnp.int32, (POS, TILE), 1)
    spread = (lane % POS == lax.broadcasted_iota(jnp.int32, (POS, TILE), 0)).astype(bf16)
    head_of = lax.broadcasted_iota(jnp.int32, (count, TILE), 0)
    lane = lax.broadcasted_iota(jnp.int32, (count, TILE), 1)
    lse_rows = dot(lse[...], spread, ((0,), (0,)))
    delta_rows = dot(delta[...], spread, ((0,), (0,))) * sign
    row = lax.broadcasted_iota(jnp.int32, (STAT_ROWS, LANES), 0)
    for i in range(4):
        ref, slot = (own_ref, other_ref)[i // 2], i % 2
        for h in range(GROUP):
            columns = slice(h * LANES, (h + 1) * LANES)
            ref[slot, h * POS : (h + 1) * POS, :] = q[i, :, columns]
            grad = (g[i, :, columns].astype(f32) * sign).astype(bf16)
            ref[slot, TILE + h * POS : TILE + (h + 1) * POS, :] = grad
        keep = head_of == heads[i] * GROUP + lane // POS
        block = jnp.zeros((STAT_ROWS, LANES), f32)
        for n, rows in enumerate((lse_rows, delta_rows)):
            line = jnp.sum(jnp.where(keep, rows, 0.0), axis=0, keepdims=True)
            block = jnp.where(row == 2 * n, line[:, :LANES], block)
            block = jnp.where(row == 2 * n + 1, line[:, LANES:], block)
        ref[slot, 2 * TILE :, :] = block.astype(bf16)


def join_kernel(own_ref, other_ref, same_ref, odd_ref):
    for i, ref in enumerate((same_ref, odd_ref)):
        ref[0] = own_ref[i]
        ref[1] = other_ref[i]


def row_position(k):
    x = (lax.axis_index(ROW) + X - k) % X
    return (lax.axis_index("y") * X + x) * POS + lax.broadcasted_iota(jnp.int32, (1, TILE), 1) % POS


def key_positions(block, count):
    index = lax.broadcasted_iota(jnp.int32, (count, 1), 0)
    source = block * (count // POS) + index // POS
    ctx = source // 2 * X + 2 * lax.axis_index("xh") + source % 2
    return ctx * POS + index % POS


def row_stats(lengths_ref, block, k, j):
    block = block.astype(f32)
    lse = jnp.concatenate([block[0:1], block[1:2]], axis=1) * LOG2E
    delta = jnp.concatenate([block[2:3], block[3:4]], axis=1)
    core = lax.axis_index("pair")
    response = core + j - 2 * core * j
    return jnp.where(row_position(k) < lengths_ref[0, 1 + response], lse, DEAD), delta


def cell(key, value, query, grad, lse, delta, allowed=None):
    scores = dot(key, query, ((1,), (1,)))
    weights = jnp.exp2(scores * (SCALE * LOG2E) - lse)
    if allowed is not None:
        weights = jnp.where(allowed, weights, 0.0)
    weight_grads = dot(value, grad, ((1,), (1,)))
    score_grads = (weights * (weight_grads - delta)).astype(bf16)
    return weights.astype(bf16), score_grads


def staged(blocks, first, second):
    for i, block in enumerate(blocks):
        first(*block, i % 2)
        if i:
            second(*blocks[i - 1], (i - 1) % 2)
    second(*blocks[-1], (len(blocks) - 1) % 2)


def tile_rows(tile):
    return slice(tile * TILE, (tile + 1) * TILE)


def prompt_kernel(first_half, lengths_ref, qa, qb, kv_ref, *refs):
    if first_half:
        key_sum, value_sum = refs[:2]
    else:
        key_sum, value_sum, out_ref = refs[:3]
    query_rows, grad_rows, lse_ref, delta_ref, weights, score_grads = refs[-6:]
    for n, ref in enumerate((qa, qb)):
        for j in range(2):
            t = j * 2 + n
            at = tile_rows(t)
            query_rows[at, :] = ref[j, 0:TILE, :]
            grad_rows[at, :] = ref[j, TILE : 2 * TILE, :]
            k = n if first_half else 2 + n
            lse, delta = row_stats(lengths_ref, ref[j, 2 * TILE :, :], k, j)
            lse_ref[t : t + 1, :], delta_ref[t : t + 1, :] = lse, delta
    per = PROMPT_BLOCK // PROMPT

    def first(c, slot):
        rows = slice(c * per, (c + 1) * per)
        key = kv_ref[rows, 0:PROMPT, :].reshape(PROMPT_BLOCK, LANES)
        value = kv_ref[rows, PROMPT : 2 * PROMPT, :].reshape(PROMPT_BLOCK, LANES)
        for t in range(X):
            at = tile_rows(t)
            weights[slot, :, at], score_grads[slot, :, at] = cell(
                key, value, query_rows[at, :], grad_rows[at, :], lse_ref[t : t + 1, :], delta_ref[t : t + 1, :]
            )

    def second(c, slot):
        value_grad = dot(weights[slot], grad_rows[...], ((1,), (0,)))
        key_grad = dot(score_grads[slot], query_rows[...], ((1,), (0,)))
        at = slice(c * PROMPT_BLOCK, (c + 1) * PROMPT_BLOCK)
        if first_half:
            key_sum[at, :], value_sum[at, :] = key_grad, value_grad
        else:
            shape = (per, PROMPT, LANES)
            to = slice(c * per, (c + 1) * per)
            out_ref[to, 0:PROMPT, :] = ((key_sum[at, :] + key_grad) * SCALE).astype(bf16).reshape(shape)
            out_ref[to, PROMPT:, :] = (value_sum[at, :] + value_grad).astype(bf16).reshape(shape)

    staged([(c,) for c in range(PEERS_N // per)], first, second)


def resp_kernel(
    kv_ref, side_ref, prompt_ref, query_a, grad_a, lse_a, delta_a, query_b, grad_b, lse_b, delta_b,
    out_hbm, margin_ref, weights, score_grads, parts, sems,
):
    halves = ((query_a, grad_a, lse_a, delta_a), (query_b, grad_b, lse_b, delta_b))
    copies = [pltpu.make_async_copy(prompt_ref, out_hbm.at[:, 0 : 2 * PROMPT, :], sems.at[0])]
    copies[0].start()
    margin = jnp.sum(kv_ref[:, KV_ROWS:, :].astype(f32), axis=(0, 1), keepdims=True).reshape(1, LANES)
    margin = jnp.sum(margin, axis=1, keepdims=True)
    margin_ref[...] = jnp.broadcast_to(margin, margin_ref.shape)
    per = BLOCK // POS
    blocks = PEERS_N // per
    sources = ((kv_ref, 2 * PROMPT), (side_ref, 0))

    def first(j, c, slot):
        ref, start = sources[j]
        rows = slice(c * per, (c + 1) * per)
        key = ref[rows, start : start + POS, :].reshape(BLOCK, LANES)
        value = ref[rows, start + POS : start + SIDE, :].reshape(BLOCK, LANES)
        positions = key_positions(c, BLOCK)
        for k in range(X):
            query_rows, grad_rows, lse_ref, delta_ref = halves[k // 2]
            t = j * 2 + k % 2
            at, to = tile_rows(t), tile_rows(k)
            weights[slot, :, to], score_grads[slot, :, to] = cell(
                key,
                value,
                query_rows[at, :],
                grad_rows[at, :],
                lse_ref[t : t + 1, :],
                delta_ref[t : t + 1, :],
                positions <= row_position(k),
            )

    def second(j, c, slot):
        rows = slice(j * 2 * TILE, (j + 1) * 2 * TILE)
        value_grad, key_grad = None, None
        for n, (query_rows, grad_rows, _, _) in enumerate(halves):
            columns = slice(n * 2 * TILE, (n + 1) * 2 * TILE)
            value_term = dot(weights[slot, :, columns], grad_rows[rows, :], ((1,), (0,)))
            key_term = dot(score_grads[slot, :, columns], query_rows[rows, :], ((1,), (0,)))
            value_grad = value_term if n == 0 else value_grad + value_term
            key_grad = key_term if n == 0 else key_grad + key_term
        key_grad *= SCALE
        shape = (per, POS, LANES)
        n = j * blocks + c
        parts[n, :, 0:POS, :] = key_grad.astype(bf16).reshape(shape)
        parts[n, :, POS:, :] = value_grad.astype(bf16).reshape(shape)
        start = 2 * PROMPT + j * SIDE
        to = out_hbm.at[c * per : (c + 1) * per, start : start + SIDE, :]
        copies.append(pltpu.make_async_copy(parts.at[n], to, sems.at[1 + n]))
        copies[-1].start()

    staged([(j, c) for j in range(2) for c in range(blocks)], first, second)
    for copy in copies:
        copy.wait()


def query_kernel(k, lengths_ref, margin_ref, q_ref, kv_ref, side_ref, out_ref):
    items = []
    for j in range(2):
        resp, start = ((kv_ref, 2 * PROMPT), (side_ref, 0))[j]
        items += [(j, kv_ref, c, PROMPT, 0) for c in range(PEERS_N * PROMPT // BLOCK)]
        items += [(j, resp, c, POS, start) for c in range(PEERS_N * POS // BLOCK)]
    totals, waiting = [None, None], None
    for item in items + [None]:
        if item:
            j, ref, c, count, start = item
            per = BLOCK // count
            rows = slice(c * per, (c + 1) * per)
            key = ref[rows, start : start + count, :].reshape(BLOCK, LANES)
            value = ref[rows, start + count : start + 2 * count, :].reshape(BLOCK, LANES)
            allowed = key_positions(c, BLOCK) <= row_position(k) if count == POS else None
            lse, delta = row_stats(lengths_ref, q_ref[j, 2 * TILE :, :], k, j)
            _, score_grads = cell(
                key, value, q_ref[j, 0:TILE, :], q_ref[j, TILE : 2 * TILE, :], lse, delta, allowed
            )
        if waiting:
            n, grads, keys = waiting
            term = dot(keys, grads, ((0,), (0,)))
            totals[n] = term if totals[n] is None else totals[n] + term
        waiting = (j, score_grads, key)
    for j in range(2):
        out_ref[tile_rows(j), :] = jnp.transpose(totals[j] * SCALE).astype(bf16)
    if k == 2:
        out_ref[2 * TILE :, :] = split_margin(margin_ref[0:1, 0:1], STAT_ROWS)


def kv_final_kernel(lengths_ref, margin_ref, d2, part_ref, pk_ref, pv_ref, rk_ref, rv_ref):
    gate = gate_of(margin_ref[0:1, 0:1], d2[2 * TILE :, :])
    core = lax.axis_index("pair")
    live = lax.axis_index(CTX) * PROMPT + lax.broadcasted_iota(jnp.int32, (PROMPT, LANES), 0) < lengths_ref[0, 0]
    for xl in range(2):
        columns = slice(xl * LANES, (xl + 1) * LANES)
        total = part_ref[xl].astype(f32)
        for y in range(1, ROWS_Y):
            total += part_ref[y * 2 + xl].astype(f32)
        total = total * gate
        pk_ref[0, :, columns] = jnp.where(live, total[0:PROMPT], 0.0).astype(bf16)
        pv_ref[0, :, columns] = jnp.where(live, total[PROMPT : 2 * PROMPT], 0.0).astype(bf16)
        for j in range(2):
            response = core + j - 2 * core * j
            at = 2 * PROMPT + j * SIDE
            rk_ref[0, response, :, columns] = total[at : at + POS].astype(bf16)
            rv_ref[0, response, :, columns] = total[at + POS : at + SIDE].astype(bf16)


def query_final_kernel(margin_ref, d0, d1, d2, d3, out_ref, gate_ref):
    gate = gate_of(margin_ref[0:1, 0:1], d2[2 * TILE :, :])
    gate_ref[0] = gate[0, 0]
    core = lax.axis_index("pair")
    even = lax.axis_index("xl") == 0
    for j in range(2):
        response = core + j - 2 * core * j
        for h in range(GROUP):
            rows = slice(j * TILE + h * POS, j * TILE + (h + 1) * POS)
            same = gate * (d0[rows, :].astype(f32) + d2[rows, :].astype(f32))
            odd = gate * (d1[rows, :].astype(f32) + d3[rows, :].astype(f32))
            first, second = jnp.where(even, same, odd), jnp.where(even, odd, same)
            out_ref[0, response, :, h * LANES : (h + 1) * LANES] = first.astype(bf16)
            out_ref[0, response, :, (GROUP + h) * LANES : (GROUP + h + 1) * LANES] = second.astype(bf16)


def swap(values):
    return lax.all_to_all(values, PEERS, split_axis=0, concat_axis=0, tiled=True)


def cross(values):
    return lax.ppermute(values, "pair", [(0, 1), (1, 0)])


def shift(values, by):
    return lax.ppermute(values, ROW, [(i, (i + by) % X) for i in range(X)])


def prompt_call(lengths, rows, kv):
    shape = jax.ShapeDtypeStruct
    count = X * TILE
    tables = (
        shape((count, LANES), bf16),
        shape((count, LANES), bf16),
        shape((X, TILE), f32),
        shape((X, TILE), f32),
    )
    sums = (shape((PEERS_N * PROMPT, LANES), f32),) * 2
    scratch = (pltpu.VMEM((2, PROMPT_BLOCK, count), bf16), pltpu.VMEM((2, PROMPT_BLOCK, count), bf16))
    cost = dict(flops=2 * 2 * 2048 * 1024 * 128 * 2, size=2 * 2**20, scratch=scratch)
    key_sum, value_sum, *first = call(functools.partial(prompt_kernel, True), sums + tables, "svvv", **cost)(
        lengths, rows[0], rows[1], kv
    )
    part, *second = call(
        functools.partial(prompt_kernel, False),
        (shape((PEERS_N, 2 * PROMPT, LANES), bf16),) + tables,
        "svvvvv",
        **cost,
    )(lengths, rows[2], rows[3], kv, key_sum, value_sum)
    return part, *first, *second


def resp_call(kv, side, prompt_part, *rows):
    shape = jax.ShapeDtypeStruct
    blocks = 2 * PEERS_N * POS // BLOCK
    return call(
        resp_kernel,
        (
            shape((PEERS_N, KV_ROWS, LANES), bf16),
            shape((8, LANES), f32),
        ),
        "v" * 11,
        out_spaces="av",
        scratch=(
            pltpu.VMEM((2, BLOCK, X * TILE), bf16),
            pltpu.VMEM((2, BLOCK, X * TILE), bf16),
            pltpu.VMEM((blocks, BLOCK // POS, SIDE, LANES), bf16),
            pltpu.SemaphoreType.DMA((blocks + 1,)),
        ),
        flops=4 * 2 * 1024 * 1024 * 128 * 2,
        size=3 * 2**20,
    )(kv, side, prompt_part, *rows)


def query_call(k, lengths, margin, rows, kv, side):
    extra = STAT_ROWS if k == 2 else 0
    return call(
        functools.partial(query_kernel, k),
        jax.ShapeDtypeStruct((2 * TILE + extra, LANES), bf16),
        "svvvv",
        flops=3 * 2 * 512 * 1536 * 128 * 2,
        size=3 * 2**20,
    )(lengths, margin, rows, kv, side)


def per_device(
    prompt_keys,
    prompt_values,
    queries,
    resp_keys,
    resp_values,
    resp_grads,
    resp_lse,
    resp_delta,
    logratio,
    lengths,
):
    shape = jax.ShapeDtypeStruct
    kv = call(
        kv_pack_kernel,
        shape((PEERS_N, KV_ROWS + MARGIN_ROWS, LANES), bf16),
        "aaaaaa",
        out_spaces="a",
        size=2 * 2**20,
        limit=60,
        scratch=(
            pltpu.SMEM((1, 3), jnp.int32),
            pltpu.VMEM((2, POS), f32),
            pltpu.VMEM((PROMPT, 2 * LANES), bf16),
            pltpu.VMEM((PROMPT, 2 * LANES), bf16),
            pltpu.VMEM((POS, X * LANES), bf16),
            pltpu.VMEM((POS, X * LANES), bf16),
            pltpu.VMEM((2, KV_ROWS + MARGIN_ROWS, LANES), bf16),
            pltpu.SemaphoreType.DMA((6 + ROWS_Y,)),
        ),
    )(lengths, logratio, prompt_keys, prompt_values, resp_keys, resp_values)
    kv = swap(kv)

    block = shape((2, QUERY_ROWS, LANES), bf16)
    own, other = call(
        query_pack_kernel,
        (block, block),
        "aaaa",
        size=2 * 2**20,
        scratch=(
            pltpu.VMEM((4, POS, GROUP * LANES), bf16),
            pltpu.VMEM((4, POS, GROUP * LANES), bf16),
            pltpu.VMEM((POS, X * GROUP), bf16),
            pltpu.VMEM((POS, X * GROUP), bf16),
            pltpu.SemaphoreType.DMA((10,)),
        ),
    )(queries, resp_grads, resp_lse, resp_delta)
    same, odd = call(join_kernel, (block, block), "vv", size=2**20)(own, cross(other))
    rows = (same, shift(odd, 1), shift(same, 2), shift(odd, 3))

    side = cross(kv[:, KV_ROWS - SIDE : KV_ROWS, :])
    prompt_part, *tables = prompt_call(lengths, rows, kv)
    part, margin = resp_call(kv, side, prompt_part, *tables)
    grads = [query_call(k, lengths, margin, rows[k], kv, side) for k in range(X)]
    part = swap(part)
    back = [grads[0]] + [shift(grads[k], X - k) for k in range(1, X)]
    query_grad, gate = call(
        query_final_kernel,
        (shape((1, 2, POS, 2 * GROUP * LANES), bf16), shape((1,), f32)),
        "vvvvv",
        out_spaces="vs",
        size=2**20,
    )(margin, *back)
    outs = (shape((1, PROMPT, 2 * LANES), bf16),) * 2 + (shape((1, 2, POS, 2 * LANES), bf16),) * 2
    pk_grad, pv_grad, key_grad, value_grad = call(kv_final_kernel, outs, "svvv", size=2**20)(
        lengths, margin, back[2], part
    )
    return pk_grad, pv_grad, query_grad, key_grad, value_grad, gate


def solution(mesh):
    batch, pair, ctx = mesh.devices.shape
    split = Mesh(mesh.devices.reshape(batch, pair, ctx // X, 2, 2), ("batch", "pair", "y", "xh", "xl"))
    prompt_spec = P("batch", CTX, "pair")
    resp_spec = P("batch", "pair", CTX, None)
    out_spec = P("batch", None, CTX, "pair")
    return jax.shard_map(
        per_device,
        mesh=split,
        in_specs=(
            prompt_spec,
            prompt_spec,
            resp_spec,
            resp_spec,
            resp_spec,
            resp_spec,
            resp_spec,
            resp_spec,
            P("batch", None, CTX),
            P("batch", None),
        ),
        out_specs=(prompt_spec, prompt_spec, out_spec, out_spec, out_spec, P("batch")),
        check_vma=False,
    )
```

```python
import functools

import jax
import jax.numpy as jnp
from jax import lax
from jax.experimental import pallas as pl
from jax.experimental.pallas import tpu as pltpu
from jax.sharding import Mesh, PartitionSpec as P

beta_coef = 0.1
f32, bf16 = jnp.float32, jnp.bfloat16
LANES = 128
CTX = ("y", "xh", "xl")
ROW = ("xh", "xl")
PEERS = ("y", "xl")

X = 4
ROWS_Y = 8
PEERS_N = 16
POS = 32
PROMPT = 64
GROUP = 8
TILE = POS * GROUP
STAT_ROWS = 16
QUERY_ROWS = 2 * TILE + STAT_ROWS
SIDE = 2 * POS
KV_ROWS = 2 * PROMPT + 2 * SIDE
LOG2E = 1.4426950408889634
SCALE = LANES**-0.5
DEAD = 1e30
BLOCK = 512
PROMPT_BLOCK = 256
MARGIN_ROWS = 8


def dot(a, b, dims):
    return lax.dot_general(a, b, (dims, ((), ())), preferred_element_type=f32)


def call(kernel, out_shape, spaces, flops=0, scratch=(), size=0, limit=24, out_spaces=""):
    space = {"v": pltpu.VMEM, "s": pltpu.SMEM, "a": pl.ANY}
    many = isinstance(out_shape, tuple)
    out_spaces = out_spaces or "v" * (len(out_shape) if many else 1)
    out_specs = tuple(pl.BlockSpec(memory_space=space[s]) for s in out_spaces)
    return pl.pallas_call(
        kernel,
        out_shape=out_shape,
        in_specs=[pl.BlockSpec(memory_space=space[s]) for s in spaces],
        out_specs=out_specs if many else out_specs[0],
        scratch_shapes=list(scratch),
        compiler_params=pltpu.CompilerParams(vmem_limit_bytes=limit * 2**20),
        cost_estimate=pl.CostEstimate(flops=flops, bytes_accessed=size, transcendentals=0),
    )


def fetch(pairs, sems):
    copies = [pltpu.make_async_copy(a, b, sems.at[i]) for i, (a, b) in enumerate(pairs)]
    for copy in copies:
        copy.start()
    for copy in copies:
        copy.wait()


def split_margin(margin, rows):
    high = margin.astype(bf16).astype(f32)
    middle = (margin - high).astype(bf16).astype(f32)
    low = margin - high - middle
    lane = lax.broadcasted_iota(jnp.int32, (rows, LANES), 1)
    row = lax.broadcasted_iota(jnp.int32, (rows, LANES), 0)
    block = jnp.where(lane == 0, high, jnp.where(lane == 1, middle, jnp.where(lane == 2, low, 0.0)))
    return jnp.where(row == 0, block, 0.0).astype(bf16)


def gate_of(margin, block):
    other = jnp.sum(block.astype(f32), axis=0, keepdims=True)
    margin = margin + jnp.sum(other, axis=1, keepdims=True)
    return beta_coef * jax.nn.sigmoid(-beta_coef * margin)


def kv_pack_kernel(
    lengths_hbm, logratio_hbm, pk_hbm, pv_hbm, rk_hbm, rv_hbm, kv_hbm, lengths, logratio, pk, pv, rk, rv, kv_ref, sems
):
    pairs = (
        (lengths_hbm, lengths),
        (logratio_hbm.at[0], logratio),
        (pk_hbm.at[0], pk),
        (pv_hbm.at[0], pv),
        (rk_hbm.at[0, 0], rk),
        (rv_hbm.at[0, 0], rv),
    )
    fetch(pairs, sems)
    first_core = lax.axis_index("pair") == 0
    ctx = lax.axis_index(CTX)
    position = ctx * POS + lax.broadcasted_iota(jnp.int32, (1, POS), 1)
    chosen = jnp.where(position < lengths[0, 1], logratio[0:1, :], 0.0)
    rejected = jnp.where(position < lengths[0, 2], logratio[1:2, :], 0.0)
    margin = jnp.sum(chosen - rejected, axis=1, keepdims=True)
    block = split_margin(margin, MARGIN_ROWS)
    live = ctx * PROMPT + lax.broadcasted_iota(jnp.int32, (PROMPT, LANES), 0) < lengths[0, 0]
    for xl in range(2):
        columns = slice(xl * LANES, (xl + 1) * LANES)
        others = slice((2 + xl) * LANES, (3 + xl) * LANES)
        parts = [jnp.where(live, pk[:, columns].astype(f32), 0.0).astype(bf16), pv[:, columns]]
        low_head = [ref[:, columns].astype(f32) for ref in (rk, rv)]
        high_head = [ref[:, others].astype(f32) for ref in (rk, rv)]
        parts += [jnp.where(first_core, a, b).astype(bf16) for a, b in zip(low_head, high_head)]
        parts += [jnp.where(first_core, b, a).astype(bf16) for a, b in zip(low_head, high_head)]
        parts += [block]
        at = 0
        for part in parts:
            kv_ref[xl, at : at + part.shape[0], :] = part
            at += part.shape[0]
    copies = [
        pltpu.make_async_copy(kv_ref, kv_hbm.at[2 * y : 2 * y + 2], sems.at[6 + y]) for y in range(ROWS_Y)
    ]
    for copy in copies:
        copy.start()
    for copy in copies:
        copy.wait()


def query_pack_kernel(q_hbm, g_hbm, lse_hbm, delta_hbm, own_ref, other_ref, q, g, lse, delta, sems):
    core, parity = lax.axis_index("pair"), lax.axis_index("xl")
    pairs = [(lse_hbm.at[0, 0], lse), (delta_hbm.at[0, 0], delta)]
    heads = []
    for i in range(4):
        head = 2 * (core if i < 2 else 1 - core) + (parity + i) % 2
        heads.append(head)
        columns = pl.ds(pl.multiple_of(head * GROUP * LANES, GROUP * LANES), GROUP * LANES)
        pairs += [(q_hbm.at[0, 0, :, columns], q.at[i]), (g_hbm.at[0, 0, :, columns], g.at[i])]
    fetch(pairs, sems)
    sign = jnp.where(core == 0, -1.0, 1.0).astype(f32)

    count = X * GROUP
    lane = lax.broadcasted_iota(jnp.int32, (POS, TILE), 1)
    spread = (lane % POS == lax.broadcasted_iota(jnp.int32, (POS, TILE), 0)).astype(bf16)
    head_of = lax.broadcasted_iota(jnp.int32, (count, TILE), 0)
    lane = lax.broadcasted_iota(jnp.int32, (count, TILE), 1)
    lse_rows = dot(lse[...], spread, ((0,), (0,)))
    delta_rows = dot(delta[...], spread, ((0,), (0,))) * sign
    row = lax.broadcasted_iota(jnp.int32, (STAT_ROWS, LANES), 0)
    for i in range(4):
        ref, slot = (own_ref, other_ref)[i // 2], i % 2
        for h in range(GROUP):
            columns = slice(h * LANES, (h + 1) * LANES)
            ref[slot, h * POS : (h + 1) * POS, :] = q[i, :, columns]
            grad = (g[i, :, columns].astype(f32) * sign).astype(bf16)
            ref[slot, TILE + h * POS : TILE + (h + 1) * POS, :] = grad
        keep = head_of == heads[i] * GROUP + lane // POS
        block = jnp.zeros((STAT_ROWS, LANES), f32)
        for n, rows in enumerate((lse_rows, delta_rows)):
            line = jnp.sum(jnp.where(keep, rows, 0.0), axis=0, keepdims=True)
            block = jnp.where(row == 2 * n, line[:, :LANES], block)
            block = jnp.where(row == 2 * n + 1, line[:, LANES:], block)
        ref[slot, 2 * TILE :, :] = block.astype(bf16)


def join_kernel(own_ref, other_ref, same_ref, odd_ref):
    for i, ref in enumerate((same_ref, odd_ref)):
        ref[0] = own_ref[i]
        ref[1] = other_ref[i]


def row_position(k):
    x = (lax.axis_index(ROW) + X - k) % X
    return (lax.axis_index("y") * X + x) * POS + lax.broadcasted_iota(jnp.int32, (1, TILE), 1) % POS


def key_positions(block, count):
    index = lax.broadcasted_iota(jnp.int32, (count, 1), 0)
    source = block * (count // POS) + index // POS
    ctx = source // 2 * X + 2 * lax.axis_index("xh") + source % 2
    return ctx * POS + index % POS


def row_stats(lengths_ref, block, k, j):
    block = block.astype(f32)
    lse = jnp.concatenate([block[0:1], block[1:2]], axis=1) * LOG2E
    delta = jnp.concatenate([block[2:3], block[3:4]], axis=1)
    core = lax.axis_index("pair")
    response = core + j - 2 * core * j
    return jnp.where(row_position(k) < lengths_ref[0, 1 + response], lse, DEAD), delta


def cell(key, value, query, grad, lse, delta, allowed=None):
    scores = dot(key, query, ((1,), (1,)))
    weights = jnp.exp2(scores * (SCALE * LOG2E) - lse)
    if allowed is not None:
        weights = jnp.where(allowed, weights, 0.0)
    weight_grads = dot(value, grad, ((1,), (1,)))
    score_grads = (weights * (weight_grads - delta)).astype(bf16)
    return weights.astype(bf16), score_grads


def staged(blocks, first, second):
    for i, block in enumerate(blocks):
        first(*block, i % 2)
        if i:
            second(*blocks[i - 1], (i - 1) % 2)
    second(*blocks[-1], (len(blocks) - 1) % 2)


def tile_rows(tile):
    return slice(tile * TILE, (tile + 1) * TILE)


def prompt_kernel(first_half, lengths_ref, qa, qb, kv_ref, *refs):
    if first_half:
        key_sum, value_sum = refs[:2]
    else:
        key_sum, value_sum, out_ref = refs[:3]
    query_rows, grad_rows, lse_ref, delta_ref, weights, score_grads = refs[-6:]
    for n, ref in enumerate((qa, qb)):
        for j in range(2):
            t = j * 2 + n
            at = tile_rows(t)
            query_rows[at, :] = ref[j, 0:TILE, :]
            grad_rows[at, :] = ref[j, TILE : 2 * TILE, :]
            k = 2 * n if first_half else 2 * n + 1
            lse, delta = row_stats(lengths_ref, ref[j, 2 * TILE :, :], k, j)
            lse_ref[t : t + 1, :], delta_ref[t : t + 1, :] = lse, delta
    per = PROMPT_BLOCK // PROMPT

    def first(c, slot):
        rows = slice(c * per, (c + 1) * per)
        key = kv_ref[rows, 0:PROMPT, :].reshape(PROMPT_BLOCK, LANES)
        value = kv_ref[rows, PROMPT : 2 * PROMPT, :].reshape(PROMPT_BLOCK, LANES)
        for t in range(X):
            at = tile_rows(t)
            weights[slot, :, at], score_grads[slot, :, at] = cell(
                key, value, query_rows[at, :], grad_rows[at, :], lse_ref[t : t + 1, :], delta_ref[t : t + 1, :]
            )

    def second(c, slot):
        value_grad = dot(weights[slot], grad_rows[...], ((1,), (0,)))
        key_grad = dot(score_grads[slot], query_rows[...], ((1,), (0,)))
        at = slice(c * PROMPT_BLOCK, (c + 1) * PROMPT_BLOCK)
        if first_half:
            key_sum[at, :], value_sum[at, :] = key_grad, value_grad
        else:
            shape = (per, PROMPT, LANES)
            to = slice(c * per, (c + 1) * per)
            out_ref[to, 0:PROMPT, :] = ((key_sum[at, :] + key_grad) * SCALE).astype(bf16).reshape(shape)
            out_ref[to, PROMPT:, :] = (value_sum[at, :] + value_grad).astype(bf16).reshape(shape)

    staged([(c,) for c in range(PEERS_N // per)], first, second)


def resp_kernel(
    kv_ref, side_ref, prompt_ref, query_a, grad_a, lse_a, delta_a, query_b, grad_b, lse_b, delta_b,
    out_hbm, margin_ref, weights, score_grads, parts, sems,
):
    halves = ((query_a, grad_a, lse_a, delta_a), (query_b, grad_b, lse_b, delta_b))
    copies = [pltpu.make_async_copy(prompt_ref, out_hbm.at[:, 0 : 2 * PROMPT, :], sems.at[0])]
    copies[0].start()
    margin = jnp.sum(kv_ref[:, KV_ROWS:, :].astype(f32), axis=(0, 1), keepdims=True).reshape(1, LANES)
    margin = jnp.sum(margin, axis=1, keepdims=True)
    margin_ref[...] = jnp.broadcast_to(margin, margin_ref.shape)
    per = BLOCK // POS
    blocks = PEERS_N // per
    sources = ((kv_ref, 2 * PROMPT), (side_ref, 0))

    def first(j, c, slot):
        ref, start = sources[j]
        rows = slice(c * per, (c + 1) * per)
        key = ref[rows, start : start + POS, :].reshape(BLOCK, LANES)
        value = ref[rows, start + POS : start + SIDE, :].reshape(BLOCK, LANES)
        positions = key_positions(c, BLOCK)
        for k in range(X):
            query_rows, grad_rows, lse_ref, delta_ref = halves[k % 2]
            t = j * 2 + k // 2
            at, to = tile_rows(t), tile_rows(k % 2 * 2 + k // 2)
            weights[slot, :, to], score_grads[slot, :, to] = cell(
                key,
                value,
                query_rows[at, :],
                grad_rows[at, :],
                lse_ref[t : t + 1, :],
                delta_ref[t : t + 1, :],
                positions <= row_position(k),
            )

    def second(j, c, slot):
        rows = slice(j * 2 * TILE, (j + 1) * 2 * TILE)
        value_grad, key_grad = None, None
        for n, (query_rows, grad_rows, _, _) in enumerate(halves):
            columns = slice(n * 2 * TILE, (n + 1) * 2 * TILE)
            value_term = dot(weights[slot, :, columns], grad_rows[rows, :], ((1,), (0,)))
            key_term = dot(score_grads[slot, :, columns], query_rows[rows, :], ((1,), (0,)))
            value_grad = value_term if n == 0 else value_grad + value_term
            key_grad = key_term if n == 0 else key_grad + key_term
        key_grad *= SCALE
        shape = (per, POS, LANES)
        n = j * blocks + c
        parts[n, :, 0:POS, :] = key_grad.astype(bf16).reshape(shape)
        parts[n, :, POS:, :] = value_grad.astype(bf16).reshape(shape)
        start = 2 * PROMPT + j * SIDE
        to = out_hbm.at[c * per : (c + 1) * per, start : start + SIDE, :]
        copies.append(pltpu.make_async_copy(parts.at[n], to, sems.at[1 + n]))
        copies[-1].start()

    staged([(j, c) for j in range(2) for c in range(blocks)], first, second)
    for copy in copies:
        copy.wait()


def query_kernel(k, lengths_ref, margin_ref, q_ref, kv_ref, side_ref, out_ref):
    items = []
    for j in range(2):
        resp, start = ((kv_ref, 2 * PROMPT), (side_ref, 0))[j]
        items += [(j, kv_ref, c, PROMPT, 0) for c in range(PEERS_N * PROMPT // BLOCK)]
        items += [(j, resp, c, POS, start) for c in range(PEERS_N * POS // BLOCK)]
    totals, waiting = [None, None], None
    for item in items + [None]:
        if item:
            j, ref, c, count, start = item
            per = BLOCK // count
            rows = slice(c * per, (c + 1) * per)
            key = ref[rows, start : start + count, :].reshape(BLOCK, LANES)
            value = ref[rows, start + count : start + 2 * count, :].reshape(BLOCK, LANES)
            allowed = key_positions(c, BLOCK) <= row_position(k) if count == POS else None
            lse, delta = row_stats(lengths_ref, q_ref[j, 2 * TILE :, :], k, j)
            _, score_grads = cell(
                key, value, q_ref[j, 0:TILE, :], q_ref[j, TILE : 2 * TILE, :], lse, delta, allowed
            )
        if waiting:
            n, grads, keys = waiting
            term = dot(keys, grads, ((0,), (0,)))
            totals[n] = term if totals[n] is None else totals[n] + term
        waiting = (j, score_grads, key)
    for j in range(2):
        out_ref[tile_rows(j), :] = jnp.transpose(totals[j] * SCALE).astype(bf16)
    if k == 2:
        out_ref[2 * TILE :, :] = split_margin(margin_ref[0:1, 0:1], STAT_ROWS)


def kv_final_kernel(lengths_ref, margin_ref, d2, part_ref, pk_ref, pv_ref, rk_ref, rv_ref):
    gate = gate_of(margin_ref[0:1, 0:1], d2[2 * TILE :, :])
    core = lax.axis_index("pair")
    live = lax.axis_index(CTX) * PROMPT + lax.broadcasted_iota(jnp.int32, (PROMPT, LANES), 0) < lengths_ref[0, 0]
    for xl in range(2):
        columns = slice(xl * LANES, (xl + 1) * LANES)
        total = part_ref[xl].astype(f32)
        for y in range(1, ROWS_Y):
            total += part_ref[y * 2 + xl].astype(f32)
        total = total * gate
        pk_ref[0, :, columns] = jnp.where(live, total[0:PROMPT], 0.0).astype(bf16)
        pv_ref[0, :, columns] = jnp.where(live, total[PROMPT : 2 * PROMPT], 0.0).astype(bf16)
        for j in range(2):
            response = core + j - 2 * core * j
            at = 2 * PROMPT + j * SIDE
            rk_ref[0, response, :, columns] = total[at : at + POS].astype(bf16)
            rv_ref[0, response, :, columns] = total[at + POS : at + SIDE].astype(bf16)


def query_final_kernel(margin_ref, d0, d1, d2, d3, out_ref, gate_ref):
    gate = gate_of(margin_ref[0:1, 0:1], d2[2 * TILE :, :])
    gate_ref[0] = gate[0, 0]
    core = lax.axis_index("pair")
    even = lax.axis_index("xl") == 0
    for j in range(2):
        response = core + j - 2 * core * j
        for h in range(GROUP):
            rows = slice(j * TILE + h * POS, j * TILE + (h + 1) * POS)
            same = gate * (d0[rows, :].astype(f32) + d2[rows, :].astype(f32))
            odd = gate * (d1[rows, :].astype(f32) + d3[rows, :].astype(f32))
            first, second = jnp.where(even, same, odd), jnp.where(even, odd, same)
            out_ref[0, response, :, h * LANES : (h + 1) * LANES] = first.astype(bf16)
            out_ref[0, response, :, (GROUP + h) * LANES : (GROUP + h + 1) * LANES] = second.astype(bf16)


def swap(values):
    return lax.all_to_all(values, PEERS, split_axis=0, concat_axis=0, tiled=True)


def cross(values):
    return lax.ppermute(values, "pair", [(0, 1), (1, 0)])


def shift(values, by):
    return lax.ppermute(values, ROW, [(i, (i + by) % X) for i in range(X)])


def prompt_call(lengths, rows, kv):
    shape = jax.ShapeDtypeStruct
    count = X * TILE
    tables = (
        shape((count, LANES), bf16),
        shape((count, LANES), bf16),
        shape((X, TILE), f32),
        shape((X, TILE), f32),
    )
    sums = (shape((PEERS_N * PROMPT, LANES), f32),) * 2
    scratch = (pltpu.VMEM((2, PROMPT_BLOCK, count), bf16), pltpu.VMEM((2, PROMPT_BLOCK, count), bf16))
    cost = dict(flops=2 * 2 * 2048 * 1024 * 128 * 2, size=2 * 2**20, scratch=scratch)
    key_sum, value_sum, *first = call(functools.partial(prompt_kernel, True), sums + tables, "svvv", **cost)(
        lengths, rows[0], rows[2], kv
    )
    key_sum, source = lax.optimization_barrier((key_sum, kv))
    side = cross(source[:, KV_ROWS - SIDE : KV_ROWS, :])
    part, *second = call(
        functools.partial(prompt_kernel, False),
        (shape((PEERS_N, 2 * PROMPT, LANES), bf16),) + tables,
        "svvvvv",
        **cost,
    )(lengths, rows[1], rows[3], kv, key_sum, value_sum)
    return side, part, *first, *second


def resp_call(kv, side, prompt_part, *rows):
    shape = jax.ShapeDtypeStruct
    blocks = 2 * PEERS_N * POS // BLOCK
    return call(
        resp_kernel,
        (
            shape((PEERS_N, KV_ROWS, LANES), bf16),
            shape((8, LANES), f32),
        ),
        "v" * 11,
        out_spaces="av",
        scratch=(
            pltpu.VMEM((2, BLOCK, X * TILE), bf16),
            pltpu.VMEM((2, BLOCK, X * TILE), bf16),
            pltpu.VMEM((blocks, BLOCK // POS, SIDE, LANES), bf16),
            pltpu.SemaphoreType.DMA((blocks + 1,)),
        ),
        flops=4 * 2 * 1024 * 1024 * 128 * 2,
        size=3 * 2**20,
    )(kv, side, prompt_part, *rows)


def query_call(k, lengths, margin, rows, kv, side):
    extra = STAT_ROWS if k == 2 else 0
    return call(
        functools.partial(query_kernel, k),
        jax.ShapeDtypeStruct((2 * TILE + extra, LANES), bf16),
        "svvvv",
        flops=3 * 2 * 512 * 1536 * 128 * 2,
        size=3 * 2**20,
    )(lengths, margin, rows, kv, side)


def per_device(
    prompt_keys,
    prompt_values,
    queries,
    resp_keys,
    resp_values,
    resp_grads,
    resp_lse,
    resp_delta,
    logratio,
    lengths,
):
    shape = jax.ShapeDtypeStruct
    kv = call(
        kv_pack_kernel,
        shape((PEERS_N, KV_ROWS + MARGIN_ROWS, LANES), bf16),
        "aaaaaa",
        out_spaces="a",
        size=2 * 2**20,
        limit=60,
        scratch=(
            pltpu.SMEM((1, 3), jnp.int32),
            pltpu.VMEM((2, POS), f32),
            pltpu.VMEM((PROMPT, 2 * LANES), bf16),
            pltpu.VMEM((PROMPT, 2 * LANES), bf16),
            pltpu.VMEM((POS, X * LANES), bf16),
            pltpu.VMEM((POS, X * LANES), bf16),
            pltpu.VMEM((2, KV_ROWS + MARGIN_ROWS, LANES), bf16),
            pltpu.SemaphoreType.DMA((6 + ROWS_Y,)),
        ),
    )(lengths, logratio, prompt_keys, prompt_values, resp_keys, resp_values)
    kv = swap(kv)

    block = shape((2, QUERY_ROWS, LANES), bf16)
    own, other = call(
        query_pack_kernel,
        (block, block),
        "aaaa",
        size=2 * 2**20,
        scratch=(
            pltpu.VMEM((4, POS, GROUP * LANES), bf16),
            pltpu.VMEM((4, POS, GROUP * LANES), bf16),
            pltpu.VMEM((POS, X * GROUP), bf16),
            pltpu.VMEM((POS, X * GROUP), bf16),
            pltpu.SemaphoreType.DMA((10,)),
        ),
    )(queries, resp_grads, resp_lse, resp_delta)
    same, odd = call(join_kernel, (block, block), "vv", size=2**20)(own, cross(other))
    rows = (same, shift(odd, 1), shift(same, 2), shift(odd, 3))

    side, prompt_part, *tables = prompt_call(lengths, rows, kv)
    part, margin = resp_call(kv, side, prompt_part, *tables)
    grads = [query_call(k, lengths, margin, rows[k], kv, side) for k in range(X)]
    part = swap(part)
    back = [grads[0]] + [shift(grads[k], X - k) for k in range(1, X)]
    query_grad, gate = call(
        query_final_kernel,
        (shape((1, 2, POS, 2 * GROUP * LANES), bf16), shape((1,), f32)),
        "vvvvv",
        out_spaces="vs",
        size=2**20,
    )(margin, *back)
    outs = (shape((1, PROMPT, 2 * LANES), bf16),) * 2 + (shape((1, 2, POS, 2 * LANES), bf16),) * 2
    pk_grad, pv_grad, key_grad, value_grad = call(kv_final_kernel, outs, "svvv", size=2**20)(
        lengths, margin, back[2], part
    )
    return pk_grad, pv_grad, query_grad, key_grad, value_grad, gate


def solution(mesh):
    batch, pair, ctx = mesh.devices.shape
    split = Mesh(mesh.devices.reshape(batch, pair, ctx // X, 2, 2), ("batch", "pair", "y", "xh", "xl"))
    prompt_spec = P("batch", CTX, "pair")
    resp_spec = P("batch", "pair", CTX, None)
    out_spec = P("batch", None, CTX, "pair")
    return jax.shard_map(
        per_device,
        mesh=split,
        in_specs=(
            prompt_spec,
            prompt_spec,
            resp_spec,
            resp_spec,
            resp_spec,
            resp_spec,
            resp_spec,
            resp_spec,
            P("batch", None, CTX),
            P("batch", None),
        ),
        out_specs=(prompt_spec, prompt_spec, out_spec, out_spec, out_spec, P("batch")),
        check_vma=False,
    )
```

```python
import functools

import jax
import jax.numpy as jnp
from jax import lax
from jax.experimental import pallas as pl
from jax.experimental.pallas import tpu as pltpu
from jax.sharding import Mesh, PartitionSpec as P

beta_coef = 0.1
f32, bf16 = jnp.float32, jnp.bfloat16
LANES = 128
CTX = ("y", "xh", "xl")
ROW = ("xh", "xl")
PEERS = ("y", "xl")

X = 4
ROWS_Y = 8
PEERS_N = 16
POS = 32
PROMPT = 64
GROUP = 8
TILE = POS * GROUP
STAT_ROWS = 16
QUERY_ROWS = 2 * TILE + STAT_ROWS
SIDE = 2 * POS
KV_ROWS = 2 * PROMPT + 2 * SIDE
LOG2E = 1.4426950408889634
SCALE = LANES**-0.5
DEAD = 1e30
BLOCK = 512
MARGIN_ROWS = 8


def dot(a, b, dims):
    return lax.dot_general(a, b, (dims, ((), ())), preferred_element_type=f32)


def call(kernel, out_shape, spaces, flops=0, scratch=(), size=0, limit=24, out_spaces=""):
    space = {"v": pltpu.VMEM, "s": pltpu.SMEM, "a": pl.ANY}
    many = isinstance(out_shape, tuple)
    out_spaces = out_spaces or "v" * (len(out_shape) if many else 1)
    out_specs = tuple(pl.BlockSpec(memory_space=space[s]) for s in out_spaces)
    return pl.pallas_call(
        kernel,
        out_shape=out_shape,
        in_specs=[pl.BlockSpec(memory_space=space[s]) for s in spaces],
        out_specs=out_specs if many else out_specs[0],
        scratch_shapes=list(scratch),
        compiler_params=pltpu.CompilerParams(vmem_limit_bytes=limit * 2**20),
        cost_estimate=pl.CostEstimate(flops=flops, bytes_accessed=size, transcendentals=0),
    )


def fetch(pairs, sems):
    copies = [pltpu.make_async_copy(a, b, sems.at[i]) for i, (a, b) in enumerate(pairs)]
    for copy in copies:
        copy.start()
    for copy in copies:
        copy.wait()


def split_margin(margin, rows):
    high = margin.astype(bf16).astype(f32)
    middle = (margin - high).astype(bf16).astype(f32)
    low = margin - high - middle
    lane = lax.broadcasted_iota(jnp.int32, (rows, LANES), 1)
    row = lax.broadcasted_iota(jnp.int32, (rows, LANES), 0)
    block = jnp.where(lane == 0, high, jnp.where(lane == 1, middle, jnp.where(lane == 2, low, 0.0)))
    return jnp.where(row == 0, block, 0.0).astype(bf16)


def gate_of(margin, block):
    other = jnp.sum(block.astype(f32), axis=0, keepdims=True)
    margin = margin + jnp.sum(other, axis=1, keepdims=True)
    return beta_coef * jax.nn.sigmoid(-beta_coef * margin)


def kv_pack_kernel(
    lengths_hbm, logratio_hbm, pk_hbm, pv_hbm, rk_hbm, rv_hbm, kv_hbm, lengths, logratio, pk, pv, rk, rv, kv_ref, sems
):
    pairs = (
        (lengths_hbm, lengths),
        (logratio_hbm.at[0], logratio),
        (pk_hbm.at[0], pk),
        (pv_hbm.at[0], pv),
        (rk_hbm.at[0, 0], rk),
        (rv_hbm.at[0, 0], rv),
    )
    fetch(pairs, sems)
    first_core = lax.axis_index("pair") == 0
    ctx = lax.axis_index(CTX)
    position = ctx * POS + lax.broadcasted_iota(jnp.int32, (1, POS), 1)
    chosen = jnp.where(position < lengths[0, 1], logratio[0:1, :], 0.0)
    rejected = jnp.where(position < lengths[0, 2], logratio[1:2, :], 0.0)
    margin = jnp.sum(chosen - rejected, axis=1, keepdims=True)
    block = split_margin(margin, MARGIN_ROWS)
    live = ctx * PROMPT + lax.broadcasted_iota(jnp.int32, (PROMPT, LANES), 0) < lengths[0, 0]
    for xl in range(2):
        columns = slice(xl * LANES, (xl + 1) * LANES)
        others = slice((2 + xl) * LANES, (3 + xl) * LANES)
        parts = [jnp.where(live, pk[:, columns].astype(f32), 0.0).astype(bf16), pv[:, columns]]
        low_head = [ref[:, columns].astype(f32) for ref in (rk, rv)]
        high_head = [ref[:, others].astype(f32) for ref in (rk, rv)]
        parts += [jnp.where(first_core, a, b).astype(bf16) for a, b in zip(low_head, high_head)]
        parts += [jnp.where(first_core, b, a).astype(bf16) for a, b in zip(low_head, high_head)]
        parts += [block]
        at = 0
        for part in parts:
            kv_ref[xl, at : at + part.shape[0], :] = part
            at += part.shape[0]
    copies = [
        pltpu.make_async_copy(kv_ref, kv_hbm.at[2 * y : 2 * y + 2], sems.at[6 + y]) for y in range(ROWS_Y)
    ]
    for copy in copies:
        copy.start()
    for copy in copies:
        copy.wait()


def query_pack_kernel(q_hbm, g_hbm, lse_hbm, delta_hbm, own_ref, other_ref, q, g, lse, delta, sems):
    core, parity = lax.axis_index("pair"), lax.axis_index("xl")
    pairs = [(lse_hbm.at[0, 0], lse), (delta_hbm.at[0, 0], delta)]
    heads = []
    for i in range(4):
        head = 2 * (core if i < 2 else 1 - core) + (parity + i) % 2
        heads.append(head)
        columns = pl.ds(pl.multiple_of(head * GROUP * LANES, GROUP * LANES), GROUP * LANES)
        pairs += [(q_hbm.at[0, 0, :, columns], q.at[i]), (g_hbm.at[0, 0, :, columns], g.at[i])]
    fetch(pairs, sems)
    sign = jnp.where(core == 0, -1.0, 1.0).astype(f32)

    count = X * GROUP
    lane = lax.broadcasted_iota(jnp.int32, (POS, TILE), 1)
    spread = (lane % POS == lax.broadcasted_iota(jnp.int32, (POS, TILE), 0)).astype(bf16)
    head_of = lax.broadcasted_iota(jnp.int32, (count, TILE), 0)
    lane = lax.broadcasted_iota(jnp.int32, (count, TILE), 1)
    lse_rows = dot(lse[...], spread, ((0,), (0,)))
    delta_rows = dot(delta[...], spread, ((0,), (0,))) * sign
    row = lax.broadcasted_iota(jnp.int32, (STAT_ROWS, LANES), 0)
    for i in range(4):
        ref, slot = (own_ref, other_ref)[i // 2], i % 2
        for h in range(GROUP):
            columns = slice(h * LANES, (h + 1) * LANES)
            ref[slot, h * POS : (h + 1) * POS, :] = q[i, :, columns]
            grad = (g[i, :, columns].astype(f32) * sign).astype(bf16)
            ref[slot, TILE + h * POS : TILE + (h + 1) * POS, :] = grad
        keep = head_of == heads[i] * GROUP + lane // POS
        block = jnp.zeros((STAT_ROWS, LANES), f32)
        for n, rows in enumerate((lse_rows, delta_rows)):
            line = jnp.sum(jnp.where(keep, rows, 0.0), axis=0, keepdims=True)
            block = jnp.where(row == 2 * n, line[:, :LANES], block)
            block = jnp.where(row == 2 * n + 1, line[:, LANES:], block)
        ref[slot, 2 * TILE :, :] = block.astype(bf16)


def join_kernel(own_ref, other_ref, same_ref, odd_ref):
    for i, ref in enumerate((same_ref, odd_ref)):
        ref[0] = own_ref[i]
        ref[1] = other_ref[i]


def row_position(k):
    x = (lax.axis_index(ROW) + X - k) % X
    return (lax.axis_index("y") * X + x) * POS + lax.broadcasted_iota(jnp.int32, (1, TILE), 1) % POS


def key_positions(block, count):
    index = lax.broadcasted_iota(jnp.int32, (count, 1), 0)
    source = block * (count // POS) + index // POS
    ctx = source // 2 * X + 2 * lax.axis_index("xh") + source % 2
    return ctx * POS + index % POS


def row_stats(lengths_ref, block, k, j):
    block = block.astype(f32)
    lse = jnp.concatenate([block[0:1], block[1:2]], axis=1) * LOG2E
    delta = jnp.concatenate([block[2:3], block[3:4]], axis=1)
    core = lax.axis_index("pair")
    response = core + j - 2 * core * j
    return jnp.where(row_position(k) < lengths_ref[0, 1 + response], lse, DEAD), delta


def cell(key, value, query, grad, lse, delta, allowed=None):
    scores = dot(key, query, ((1,), (1,)))
    weights = jnp.exp2(scores * (SCALE * LOG2E) - lse)
    if allowed is not None:
        weights = jnp.where(allowed, weights, 0.0)
    weight_grads = dot(value, grad, ((1,), (1,)))
    score_grads = (weights * (weight_grads - delta)).astype(bf16)
    return weights.astype(bf16), score_grads


def staged(blocks, first, second):
    for i, block in enumerate(blocks):
        first(*block, i % 2)
        if i:
            second(*blocks[i - 1], (i - 1) % 2)
    second(*blocks[-1], (len(blocks) - 1) % 2)


def tile_rows(tile):
    return slice(tile * TILE, (tile + 1) * TILE)


def prompt_kernel(
    lengths_ref, q0, q1, q2, q3, kv_ref, out_ref, query_rows, grad_rows, lse_ref, delta_ref, weights, score_grads
):
    for k, ref in enumerate((q0, q1, q2, q3)):
        for j in range(2):
            t = j * X + k
            at = tile_rows(t)
            query_rows[at, :] = ref[j, 0:TILE, :]
            grad_rows[at, :] = ref[j, TILE : 2 * TILE, :]
            lse, delta = row_stats(lengths_ref, ref[j, 2 * TILE :, :], k, j)
            lse_ref[t : t + 1, :], delta_ref[t : t + 1, :] = lse, delta
    per = BLOCK // PROMPT

    def first(c, slot):
        rows = slice(c * per, (c + 1) * per)
        key = kv_ref[rows, 0:PROMPT, :].reshape(BLOCK, LANES)
        value = kv_ref[rows, PROMPT : 2 * PROMPT, :].reshape(BLOCK, LANES)
        for t in range(2 * X):
            at = tile_rows(t)
            weights[slot, :, at], score_grads[slot, :, at] = cell(
                key, value, query_rows[at, :], grad_rows[at, :], lse_ref[t : t + 1, :], delta_ref[t : t + 1, :]
            )

    def second(c, slot):
        value_grad = dot(weights[slot], grad_rows[...], ((1,), (0,)))
        key_grad = dot(score_grads[slot], query_rows[...], ((1,), (0,))) * SCALE
        shape = (per, PROMPT, LANES)
        to = slice(c * per, (c + 1) * per)
        out_ref[to, 0:PROMPT, :] = key_grad.astype(bf16).reshape(shape)
        out_ref[to, PROMPT:, :] = value_grad.astype(bf16).reshape(shape)

    staged([(c,) for c in range(PEERS_N // per)], first, second)


def resp_kernel(
    kv_ref, side_ref, prompt_ref, query_rows, grad_rows, lse_ref, delta_ref,
    out_hbm, margin_ref, weights, score_grads, parts, sems,
):
    copies = [pltpu.make_async_copy(prompt_ref, out_hbm.at[:, 0 : 2 * PROMPT, :], sems.at[0])]
    copies[0].start()
    margin = jnp.sum(kv_ref[:, KV_ROWS:, :].astype(f32), axis=(0, 1), keepdims=True).reshape(1, LANES)
    margin = jnp.sum(margin, axis=1, keepdims=True)
    margin_ref[...] = jnp.broadcast_to(margin, margin_ref.shape)
    per = BLOCK // POS
    blocks = PEERS_N // per
    sources = ((kv_ref, 2 * PROMPT), (side_ref, 0))

    def first(j, c, slot):
        ref, start = sources[j]
        rows = slice(c * per, (c + 1) * per)
        key = ref[rows, start : start + POS, :].reshape(BLOCK, LANES)
        value = ref[rows, start + POS : start + SIDE, :].reshape(BLOCK, LANES)
        positions = key_positions(c, BLOCK)
        for k in range(X):
            t = j * X + k
            at, to = tile_rows(t), tile_rows(k)
            weights[slot, :, to], score_grads[slot, :, to] = cell(
                key,
                value,
                query_rows[at, :],
                grad_rows[at, :],
                lse_ref[t : t + 1, :],
                delta_ref[t : t + 1, :],
                positions <= row_position(k),
            )

    def second(j, c, slot):
        rows = slice(j * X * TILE, (j + 1) * X * TILE)
        value_grad = dot(weights[slot], grad_rows[rows, :], ((1,), (0,)))
        key_grad = dot(score_grads[slot], query_rows[rows, :], ((1,), (0,))) * SCALE
        shape = (per, POS, LANES)
        n = j * blocks + c
        parts[n, :, 0:POS, :] = key_grad.astype(bf16).reshape(shape)
        parts[n, :, POS:, :] = value_grad.astype(bf16).reshape(shape)
        start = 2 * PROMPT + j * SIDE
        to = out_hbm.at[c * per : (c + 1) * per, start : start + SIDE, :]
        copies.append(pltpu.make_async_copy(parts.at[n], to, sems.at[1 + n]))
        copies[-1].start()

    staged([(j, c) for j in range(2) for c in range(blocks)], first, second)
    for copy in copies:
        copy.wait()


def query_kernel(k, lengths_ref, margin_ref, q_ref, kv_ref, side_ref, out_ref):
    items = []
    for j in range(2):
        resp, start = ((kv_ref, 2 * PROMPT), (side_ref, 0))[j]
        items += [(j, kv_ref, c, PROMPT, 0) for c in range(PEERS_N * PROMPT // BLOCK)]
        items += [(j, resp, c, POS, start) for c in range(PEERS_N * POS // BLOCK)]
    totals, waiting = [None, None], None
    for item in items + [None]:
        if item:
            j, ref, c, count, start = item
            per = BLOCK // count
            rows = slice(c * per, (c + 1) * per)
            key = ref[rows, start : start + count, :].reshape(BLOCK, LANES)
            value = ref[rows, start + count : start + 2 * count, :].reshape(BLOCK, LANES)
            allowed = key_positions(c, BLOCK) <= row_position(k) if count == POS else None
            lse, delta = row_stats(lengths_ref, q_ref[j, 2 * TILE :, :], k, j)
            _, score_grads = cell(
                key, value, q_ref[j, 0:TILE, :], q_ref[j, TILE : 2 * TILE, :], lse, delta, allowed
            )
        if waiting:
            n, grads, keys = waiting
            term = dot(keys, grads, ((0,), (0,)))
            totals[n] = term if totals[n] is None else totals[n] + term
        waiting = (j, score_grads, key)
    for j in range(2):
        out_ref[tile_rows(j), :] = jnp.transpose(totals[j] * SCALE).astype(bf16)
    if k == 2:
        out_ref[2 * TILE :, :] = split_margin(margin_ref[0:1, 0:1], STAT_ROWS)


def kv_final_kernel(lengths_ref, margin_ref, d2, part_ref, pk_ref, pv_ref, rk_ref, rv_ref):
    gate = gate_of(margin_ref[0:1, 0:1], d2[2 * TILE :, :])
    core = lax.axis_index("pair")
    live = lax.axis_index(CTX) * PROMPT + lax.broadcasted_iota(jnp.int32, (PROMPT, LANES), 0) < lengths_ref[0, 0]
    for xl in range(2):
        columns = slice(xl * LANES, (xl + 1) * LANES)
        total = part_ref[xl].astype(f32)
        for y in range(1, ROWS_Y):
            total += part_ref[y * 2 + xl].astype(f32)
        total = total * gate
        pk_ref[0, :, columns] = jnp.where(live, total[0:PROMPT], 0.0).astype(bf16)
        pv_ref[0, :, columns] = jnp.where(live, total[PROMPT : 2 * PROMPT], 0.0).astype(bf16)
        for j in range(2):
            response = core + j - 2 * core * j
            at = 2 * PROMPT + j * SIDE
            rk_ref[0, response, :, columns] = total[at : at + POS].astype(bf16)
            rv_ref[0, response, :, columns] = total[at + POS : at + SIDE].astype(bf16)


def query_final_kernel(margin_ref, d0, d1, d2, d3, out_ref, gate_ref):
    gate = gate_of(margin_ref[0:1, 0:1], d2[2 * TILE :, :])
    gate_ref[0] = gate[0, 0]
    core = lax.axis_index("pair")
    even = lax.axis_index("xl") == 0
    for j in range(2):
        response = core + j - 2 * core * j
        for h in range(GROUP):
            rows = slice(j * TILE + h * POS, j * TILE + (h + 1) * POS)
            same = gate * (d0[rows, :].astype(f32) + d2[rows, :].astype(f32))
            odd = gate * (d1[rows, :].astype(f32) + d3[rows, :].astype(f32))
            first, second = jnp.where(even, same, odd), jnp.where(even, odd, same)
            out_ref[0, response, :, h * LANES : (h + 1) * LANES] = first.astype(bf16)
            out_ref[0, response, :, (GROUP + h) * LANES : (GROUP + h + 1) * LANES] = second.astype(bf16)


def swap(values):
    return lax.all_to_all(values, PEERS, split_axis=0, concat_axis=0, tiled=True)


def cross(values):
    return lax.ppermute(values, "pair", [(0, 1), (1, 0)])


def shift(values, by):
    return lax.ppermute(values, ROW, [(i, (i + by) % X) for i in range(X)])


def prompt_call(lengths, rows, kv):
    shape = jax.ShapeDtypeStruct
    count = 2 * X * TILE
    return call(
        prompt_kernel,
        (
            shape((PEERS_N, 2 * PROMPT, LANES), bf16),
            shape((count, LANES), bf16),
            shape((count, LANES), bf16),
            shape((2 * X, TILE), f32),
            shape((2 * X, TILE), f32),
        ),
        "svvvvv",
        scratch=(pltpu.VMEM((2, BLOCK, count), bf16), pltpu.VMEM((2, BLOCK, count), bf16)),
        flops=4 * 2 * 2048 * 1024 * 128 * 2,
        size=3 * 2**20,
    )(lengths, *rows, kv)


def resp_call(kv, side, prompt_part, *rows):
    shape = jax.ShapeDtypeStruct
    blocks = 2 * PEERS_N * POS // BLOCK
    return call(
        resp_kernel,
        (
            shape((PEERS_N, KV_ROWS, LANES), bf16),
            shape((8, LANES), f32),
        ),
        "vvvvvvv",
        out_spaces="av",
        scratch=(
            pltpu.VMEM((2, BLOCK, X * TILE), bf16),
            pltpu.VMEM((2, BLOCK, X * TILE), bf16),
            pltpu.VMEM((blocks, BLOCK // POS, SIDE, LANES), bf16),
            pltpu.SemaphoreType.DMA((blocks + 1,)),
        ),
        flops=4 * 2 * 1024 * 1024 * 128 * 2,
        size=3 * 2**20,
    )(kv, side, prompt_part, *rows)


def query_call(k, lengths, margin, rows, kv, side):
    extra = STAT_ROWS if k == 2 else 0
    return call(
        functools.partial(query_kernel, k),
        jax.ShapeDtypeStruct((2 * TILE + extra, LANES), bf16),
        "svvvv",
        flops=3 * 2 * 512 * 1536 * 128 * 2,
        size=3 * 2**20,
    )(lengths, margin, rows, kv, side)


def per_device(
    prompt_keys,
    prompt_values,
    queries,
    resp_keys,
    resp_values,
    resp_grads,
    resp_lse,
    resp_delta,
    logratio,
    lengths,
):
    shape = jax.ShapeDtypeStruct
    kv = call(
        kv_pack_kernel,
        shape((PEERS_N, KV_ROWS + MARGIN_ROWS, LANES), bf16),
        "aaaaaa",
        out_spaces="a",
        size=2 * 2**20,
        limit=60,
        scratch=(
            pltpu.SMEM((1, 3), jnp.int32),
            pltpu.VMEM((2, POS), f32),
            pltpu.VMEM((PROMPT, 2 * LANES), bf16),
            pltpu.VMEM((PROMPT, 2 * LANES), bf16),
            pltpu.VMEM((POS, X * LANES), bf16),
            pltpu.VMEM((POS, X * LANES), bf16),
            pltpu.VMEM((2, KV_ROWS + MARGIN_ROWS, LANES), bf16),
            pltpu.SemaphoreType.DMA((6 + ROWS_Y,)),
        ),
    )(lengths, logratio, prompt_keys, prompt_values, resp_keys, resp_values)
    kv = swap(kv)

    block = shape((2, QUERY_ROWS, LANES), bf16)
    own, other = call(
        query_pack_kernel,
        (block, block),
        "aaaa",
        size=2 * 2**20,
        scratch=(
            pltpu.VMEM((4, POS, GROUP * LANES), bf16),
            pltpu.VMEM((4, POS, GROUP * LANES), bf16),
            pltpu.VMEM((POS, X * GROUP), bf16),
            pltpu.VMEM((POS, X * GROUP), bf16),
            pltpu.SemaphoreType.DMA((10,)),
        ),
    )(queries, resp_grads, resp_lse, resp_delta)
    same, odd = call(join_kernel, (block, block), "vv", size=2**20)(own, cross(other))
    far = shift(same, 2)
    rows = (same, shift(odd, 1), far, shift(odd, 3))

    side = cross(kv[:, KV_ROWS - SIDE : KV_ROWS, :])
    prompt_part, *tables = prompt_call(lengths, rows, kv)
    part, margin = resp_call(kv, side, prompt_part, *tables)
    grads = [query_call(k, lengths, margin, rows[k], kv, side) for k in range(X)]
    part = swap(part)
    back = [grads[0]] + [shift(grads[k], X - k) for k in range(1, X)]
    query_grad, gate = call(
        query_final_kernel,
        (shape((1, 2, POS, 2 * GROUP * LANES), bf16), shape((1,), f32)),
        "vvvvv",
        out_spaces="vs",
        size=2**20,
    )(margin, *back)
    outs = (shape((1, PROMPT, 2 * LANES), bf16),) * 2 + (shape((1, 2, POS, 2 * LANES), bf16),) * 2
    pk_grad, pv_grad, key_grad, value_grad = call(kv_final_kernel, outs, "svvv", size=2**20)(
        lengths, margin, back[2], part
    )
    return pk_grad, pv_grad, query_grad, key_grad, value_grad, gate


def solution(mesh):
    batch, pair, ctx = mesh.devices.shape
    split = Mesh(mesh.devices.reshape(batch, pair, ctx // X, 2, 2), ("batch", "pair", "y", "xh", "xl"))
    prompt_spec = P("batch", CTX, "pair")
    resp_spec = P("batch", "pair", CTX, None)
    out_spec = P("batch", None, CTX, "pair")
    return jax.shard_map(
        per_device,
        mesh=split,
        in_specs=(
            prompt_spec,
            prompt_spec,
            resp_spec,
            resp_spec,
            resp_spec,
            resp_spec,
            resp_spec,
            resp_spec,
            P("batch", None, CTX),
            P("batch", None),
        ),
        out_specs=(prompt_spec, prompt_spec, out_spec, out_spec, out_spec, P("batch")),
        check_vma=False,
    )
```

```python
import functools

import jax
import jax.numpy as jnp
from jax import lax
from jax.experimental import pallas as pl
from jax.experimental.pallas import tpu as pltpu
from jax.sharding import Mesh, PartitionSpec as P

beta_coef = 0.1
f32, bf16 = jnp.float32, jnp.bfloat16
LANES = 128
CTX = ("y", "xh", "xl")
ROW = ("xh", "xl")
PEERS = ("y", "xl")

X = 4
ROWS_Y = 8
PEERS_N = 16
POS = 32
PROMPT = 64
GROUP = 8
TILE = POS * GROUP
STAT_ROWS = 16
QUERY_ROWS = 2 * TILE + STAT_ROWS
SIDE = 2 * POS
KV_ROWS = 2 * PROMPT + 2 * SIDE
LOG2E = 1.4426950408889634
SCALE = LANES**-0.5
DEAD = 1e30
BLOCK = 512
PROMPT_BLOCK = 256
MARGIN_ROWS = 8


def dot(a, b, dims):
    return lax.dot_general(a, b, (dims, ((), ())), preferred_element_type=f32)


def call(kernel, out_shape, spaces, flops=0, scratch=(), size=0, limit=24, out_spaces=""):
    space = {"v": pltpu.VMEM, "s": pltpu.SMEM, "a": pl.ANY}
    many = isinstance(out_shape, tuple)
    out_spaces = out_spaces or "v" * (len(out_shape) if many else 1)
    out_specs = tuple(pl.BlockSpec(memory_space=space[s]) for s in out_spaces)
    return pl.pallas_call(
        kernel,
        out_shape=out_shape,
        in_specs=[pl.BlockSpec(memory_space=space[s]) for s in spaces],
        out_specs=out_specs if many else out_specs[0],
        scratch_shapes=list(scratch),
        compiler_params=pltpu.CompilerParams(vmem_limit_bytes=limit * 2**20),
        cost_estimate=pl.CostEstimate(flops=flops, bytes_accessed=size, transcendentals=0),
    )


def fetch(pairs, sems):
    copies = [pltpu.make_async_copy(a, b, sems.at[i]) for i, (a, b) in enumerate(pairs)]
    for copy in copies:
        copy.start()
    for copy in copies:
        copy.wait()


def split_margin(margin, rows):
    high = margin.astype(bf16).astype(f32)
    middle = (margin - high).astype(bf16).astype(f32)
    low = margin - high - middle
    lane = lax.broadcasted_iota(jnp.int32, (rows, LANES), 1)
    row = lax.broadcasted_iota(jnp.int32, (rows, LANES), 0)
    block = jnp.where(lane == 0, high, jnp.where(lane == 1, middle, jnp.where(lane == 2, low, 0.0)))
    return jnp.where(row == 0, block, 0.0).astype(bf16)


def gate_of(margin, block):
    other = jnp.sum(block.astype(f32), axis=0, keepdims=True)
    margin = margin + jnp.sum(other, axis=1, keepdims=True)
    return beta_coef * jax.nn.sigmoid(-beta_coef * margin)


def kv_pack_kernel(
    lengths_hbm, logratio_hbm, pk_hbm, pv_hbm, rk_hbm, rv_hbm, kv_hbm, lengths, logratio, pk, pv, rk, rv, kv_ref, sems
):
    pairs = (
        (lengths_hbm, lengths),
        (logratio_hbm.at[0], logratio),
        (pk_hbm.at[0], pk),
        (pv_hbm.at[0], pv),
        (rk_hbm.at[0, 0], rk),
        (rv_hbm.at[0, 0], rv),
    )
    fetch(pairs, sems)
    first_core = lax.axis_index("pair") == 0
    ctx = lax.axis_index(CTX)
    position = ctx * POS + lax.broadcasted_iota(jnp.int32, (1, POS), 1)
    chosen = jnp.where(position < lengths[0, 1], logratio[0:1, :], 0.0)
    rejected = jnp.where(position < lengths[0, 2], logratio[1:2, :], 0.0)
    margin = jnp.sum(chosen - rejected, axis=1, keepdims=True)
    block = split_margin(margin, MARGIN_ROWS)
    live = ctx * PROMPT + lax.broadcasted_iota(jnp.int32, (PROMPT, LANES), 0) < lengths[0, 0]
    for xl in range(2):
        columns = slice(xl * LANES, (xl + 1) * LANES)
        others = slice((2 + xl) * LANES, (3 + xl) * LANES)
        parts = [jnp.where(live, pk[:, columns].astype(f32), 0.0).astype(bf16), pv[:, columns]]
        low_head = [ref[:, columns].astype(f32) for ref in (rk, rv)]
        high_head = [ref[:, others].astype(f32) for ref in (rk, rv)]
        parts += [jnp.where(first_core, a, b).astype(bf16) for a, b in zip(low_head, high_head)]
        parts += [jnp.where(first_core, b, a).astype(bf16) for a, b in zip(low_head, high_head)]
        parts += [block]
        at = 0
        for part in parts:
            kv_ref[xl, at : at + part.shape[0], :] = part
            at += part.shape[0]
    copies = [
        pltpu.make_async_copy(kv_ref, kv_hbm.at[2 * y : 2 * y + 2], sems.at[6 + y]) for y in range(ROWS_Y)
    ]
    for copy in copies:
        copy.start()
    for copy in copies:
        copy.wait()


def query_pack_kernel(q_hbm, g_hbm, lse_hbm, delta_hbm, own_ref, other_ref, q, g, lse, delta, sems):
    core, parity = lax.axis_index("pair"), lax.axis_index("xl")
    pairs = [(lse_hbm.at[0, 0], lse), (delta_hbm.at[0, 0], delta)]
    heads = []
    for i in range(4):
        head = 2 * (core if i < 2 else 1 - core) + (parity + i) % 2
        heads.append(head)
        columns = pl.ds(pl.multiple_of(head * GROUP * LANES, GROUP * LANES), GROUP * LANES)
        pairs += [(q_hbm.at[0, 0, :, columns], q.at[i]), (g_hbm.at[0, 0, :, columns], g.at[i])]
    fetch(pairs, sems)
    sign = jnp.where(core == 0, -1.0, 1.0).astype(f32)

    count = X * GROUP
    lane = lax.broadcasted_iota(jnp.int32, (POS, TILE), 1)
    spread = (lane % POS == lax.broadcasted_iota(jnp.int32, (POS, TILE), 0)).astype(bf16)
    head_of = lax.broadcasted_iota(jnp.int32, (count, TILE), 0)
    lane = lax.broadcasted_iota(jnp.int32, (count, TILE), 1)
    lse_rows = dot(lse[...], spread, ((0,), (0,)))
    delta_rows = dot(delta[...], spread, ((0,), (0,))) * sign
    row = lax.broadcasted_iota(jnp.int32, (STAT_ROWS, LANES), 0)
    for i in range(4):
        ref, slot = (own_ref, other_ref)[i // 2], i % 2
        for h in range(GROUP):
            columns = slice(h * LANES, (h + 1) * LANES)
            ref[slot, h * POS : (h + 1) * POS, :] = q[i, :, columns]
            grad = (g[i, :, columns].astype(f32) * sign).astype(bf16)
            ref[slot, TILE + h * POS : TILE + (h + 1) * POS, :] = grad
        keep = head_of == heads[i] * GROUP + lane // POS
        block = jnp.zeros((STAT_ROWS, LANES), f32)
        for n, rows in enumerate((lse_rows, delta_rows)):
            line = jnp.sum(jnp.where(keep, rows, 0.0), axis=0, keepdims=True)
            block = jnp.where(row == 2 * n, line[:, :LANES], block)
            block = jnp.where(row == 2 * n + 1, line[:, LANES:], block)
        ref[slot, 2 * TILE :, :] = block.astype(bf16)


def join_kernel(own_ref, other_ref, same_ref, odd_ref):
    for i, ref in enumerate((same_ref, odd_ref)):
        ref[0] = own_ref[i]
        ref[1] = other_ref[i]


def row_position(k):
    x = (lax.axis_index(ROW) + X - k) % X
    return (lax.axis_index("y") * X + x) * POS + lax.broadcasted_iota(jnp.int32, (1, TILE), 1) % POS


def key_positions(block, count):
    index = lax.broadcasted_iota(jnp.int32, (count, 1), 0)
    source = block * (count // POS) + index // POS
    ctx = source // 2 * X + 2 * lax.axis_index("xh") + source % 2
    return ctx * POS + index % POS


def row_stats(lengths_ref, block, k, j):
    block = block.astype(f32)
    lse = jnp.concatenate([block[0:1], block[1:2]], axis=1) * LOG2E
    delta = jnp.concatenate([block[2:3], block[3:4]], axis=1)
    core = lax.axis_index("pair")
    response = core + j - 2 * core * j
    return jnp.where(row_position(k) < lengths_ref[0, 1 + response], lse, DEAD), delta


def cell(key, value, query, grad, lse, delta, allowed=None):
    scores = dot(key, query, ((1,), (1,)))
    weights = jnp.exp2(scores * (SCALE * LOG2E) - lse)
    if allowed is not None:
        weights = jnp.where(allowed, weights, 0.0)
    weight_grads = dot(value, grad, ((1,), (1,)))
    score_grads = (weights * (weight_grads - delta)).astype(bf16)
    return weights.astype(bf16), score_grads


def staged(blocks, first, second):
    for i, block in enumerate(blocks):
        first(*block, i % 2)
        if i:
            second(*blocks[i - 1], (i - 1) % 2)
    second(*blocks[-1], (len(blocks) - 1) % 2)


def tile_rows(tile):
    return slice(tile * TILE, (tile + 1) * TILE)


def fill_tables(first_half, lengths_ref, sources, query_rows, grad_rows, lse_ref, delta_ref):
    for n, ref in enumerate(sources):
        for j in range(2):
            t = j * 2 + n
            at = tile_rows(t)
            query_rows[at, :] = ref[j, 0:TILE, :]
            grad_rows[at, :] = ref[j, TILE : 2 * TILE, :]
            k = 2 * n if first_half else 2 * n + 1
            lse, delta = row_stats(lengths_ref, ref[j, 2 * TILE :, :], k, j)
            lse_ref[t : t + 1, :], delta_ref[t : t + 1, :] = lse, delta


def tables_kernel(lengths_ref, qa, qb, *tables):
    fill_tables(True, lengths_ref, (qa, qb), *tables)


def prompt_kernel(first_half, *refs):
    if first_half:
        query_rows, grad_rows, lse_ref, delta_ref, kv_ref, key_sum, value_sum, weights, score_grads = refs
    else:
        lengths_ref, qa, qb, kv_ref, key_sum, value_sum, out_ref = refs[:7]
        query_rows, grad_rows, lse_ref, delta_ref, weights, score_grads = refs[7:]
        fill_tables(False, lengths_ref, (qa, qb), query_rows, grad_rows, lse_ref, delta_ref)
    per = PROMPT_BLOCK // PROMPT

    def first(c, slot):
        rows = slice(c * per, (c + 1) * per)
        key = kv_ref[rows, 0:PROMPT, :].reshape(PROMPT_BLOCK, LANES)
        value = kv_ref[rows, PROMPT : 2 * PROMPT, :].reshape(PROMPT_BLOCK, LANES)
        for t in range(X):
            at = tile_rows(t)
            weights[slot, :, at], score_grads[slot, :, at] = cell(
                key, value, query_rows[at, :], grad_rows[at, :], lse_ref[t : t + 1, :], delta_ref[t : t + 1, :]
            )

    def second(c, slot):
        value_grad = dot(weights[slot], grad_rows[...], ((1,), (0,)))
        key_grad = dot(score_grads[slot], query_rows[...], ((1,), (0,)))
        at = slice(c * PROMPT_BLOCK, (c + 1) * PROMPT_BLOCK)
        if first_half:
            key_sum[at, :], value_sum[at, :] = key_grad, value_grad
        else:
            shape = (per, PROMPT, LANES)
            to = slice(c * per, (c + 1) * per)
            out_ref[to, 0:PROMPT, :] = ((key_sum[at, :] + key_grad) * SCALE).astype(bf16).reshape(shape)
            out_ref[to, PROMPT:, :] = (value_sum[at, :] + value_grad).astype(bf16).reshape(shape)

    staged([(c,) for c in range(PEERS_N // per)], first, second)


def resp_kernel(
    kv_ref, side_ref, prompt_ref, query_a, grad_a, lse_a, delta_a, query_b, grad_b, lse_b, delta_b,
    out_hbm, margin_ref, weights, score_grads, parts, sems,
):
    halves = ((query_a, grad_a, lse_a, delta_a), (query_b, grad_b, lse_b, delta_b))
    copies = [pltpu.make_async_copy(prompt_ref, out_hbm.at[:, 0 : 2 * PROMPT, :], sems.at[0])]
    copies[0].start()
    margin = jnp.sum(kv_ref[:, KV_ROWS:, :].astype(f32), axis=(0, 1), keepdims=True).reshape(1, LANES)
    margin = jnp.sum(margin, axis=1, keepdims=True)
    margin_ref[...] = jnp.broadcast_to(margin, margin_ref.shape)
    per = BLOCK // POS
    blocks = PEERS_N // per
    sources = ((kv_ref, 2 * PROMPT), (side_ref, 0))

    def first(j, c, slot):
        ref, start = sources[j]
        rows = slice(c * per, (c + 1) * per)
        key = ref[rows, start : start + POS, :].reshape(BLOCK, LANES)
        value = ref[rows, start + POS : start + SIDE, :].reshape(BLOCK, LANES)
        positions = key_positions(c, BLOCK)
        for k in range(X):
            query_rows, grad_rows, lse_ref, delta_ref = halves[k % 2]
            t = j * 2 + k // 2
            at, to = tile_rows(t), tile_rows(k % 2 * 2 + k // 2)
            weights[slot, :, to], score_grads[slot, :, to] = cell(
                key,
                value,
                query_rows[at, :],
                grad_rows[at, :],
                lse_ref[t : t + 1, :],
                delta_ref[t : t + 1, :],
                positions <= row_position(k),
            )

    def second(j, c, slot):
        rows = slice(j * 2 * TILE, (j + 1) * 2 * TILE)
        value_grad, key_grad = None, None
        for n, (query_rows, grad_rows, _, _) in enumerate(halves):
            columns = slice(n * 2 * TILE, (n + 1) * 2 * TILE)
            value_term = dot(weights[slot, :, columns], grad_rows[rows, :], ((1,), (0,)))
            key_term = dot(score_grads[slot, :, columns], query_rows[rows, :], ((1,), (0,)))
            value_grad = value_term if n == 0 else value_grad + value_term
            key_grad = key_term if n == 0 else key_grad + key_term
        key_grad *= SCALE
        shape = (per, POS, LANES)
        n = j * blocks + c
        parts[n, :, 0:POS, :] = key_grad.astype(bf16).reshape(shape)
        parts[n, :, POS:, :] = value_grad.astype(bf16).reshape(shape)
        start = 2 * PROMPT + j * SIDE
        to = out_hbm.at[c * per : (c + 1) * per, start : start + SIDE, :]
        copies.append(pltpu.make_async_copy(parts.at[n], to, sems.at[1 + n]))
        copies[-1].start()

    staged([(j, c) for j in range(2) for c in range(blocks)], first, second)
    for copy in copies:
        copy.wait()


def query_kernel(k, lengths_ref, margin_ref, q_ref, kv_ref, side_ref, out_ref):
    items = []
    for j in range(2):
        resp, start = ((kv_ref, 2 * PROMPT), (side_ref, 0))[j]
        items += [(j, kv_ref, c, PROMPT, 0) for c in range(PEERS_N * PROMPT // BLOCK)]
        items += [(j, resp, c, POS, start) for c in range(PEERS_N * POS // BLOCK)]
    totals, waiting = [None, None], None
    for item in items + [None]:
        if item:
            j, ref, c, count, start = item
            per = BLOCK // count
            rows = slice(c * per, (c + 1) * per)
            key = ref[rows, start : start + count, :].reshape(BLOCK, LANES)
            value = ref[rows, start + count : start + 2 * count, :].reshape(BLOCK, LANES)
            allowed = key_positions(c, BLOCK) <= row_position(k) if count == POS else None
            lse, delta = row_stats(lengths_ref, q_ref[j, 2 * TILE :, :], k, j)
            _, score_grads = cell(
                key, value, q_ref[j, 0:TILE, :], q_ref[j, TILE : 2 * TILE, :], lse, delta, allowed
            )
        if waiting:
            n, grads, keys = waiting
            term = dot(keys, grads, ((0,), (0,)))
            totals[n] = term if totals[n] is None else totals[n] + term
        waiting = (j, score_grads, key)
    for j in range(2):
        out_ref[tile_rows(j), :] = jnp.transpose(totals[j] * SCALE).astype(bf16)
    if k == 2:
        out_ref[2 * TILE :, :] = split_margin(margin_ref[0:1, 0:1], STAT_ROWS)


def kv_final_kernel(lengths_ref, margin_ref, d2, part_ref, pk_ref, pv_ref, rk_ref, rv_ref):
    gate = gate_of(margin_ref[0:1, 0:1], d2[2 * TILE :, :])
    core = lax.axis_index("pair")
    live = lax.axis_index(CTX) * PROMPT + lax.broadcasted_iota(jnp.int32, (PROMPT, LANES), 0) < lengths_ref[0, 0]
    for xl in range(2):
        columns = slice(xl * LANES, (xl + 1) * LANES)
        total = part_ref[xl].astype(f32)
        for y in range(1, ROWS_Y):
            total += part_ref[y * 2 + xl].astype(f32)
        total = total * gate
        pk_ref[0, :, columns] = jnp.where(live, total[0:PROMPT], 0.0).astype(bf16)
        pv_ref[0, :, columns] = jnp.where(live, total[PROMPT : 2 * PROMPT], 0.0).astype(bf16)
        for j in range(2):
            response = core + j - 2 * core * j
            at = 2 * PROMPT + j * SIDE
            rk_ref[0, response, :, columns] = total[at : at + POS].astype(bf16)
            rv_ref[0, response, :, columns] = total[at + POS : at + SIDE].astype(bf16)


def query_final_kernel(margin_ref, d0, d1, d2, d3, out_ref, gate_ref):
    gate = gate_of(margin_ref[0:1, 0:1], d2[2 * TILE :, :])
    gate_ref[0] = gate[0, 0]
    core = lax.axis_index("pair")
    even = lax.axis_index("xl") == 0
    for j in range(2):
        response = core + j - 2 * core * j
        for h in range(GROUP):
            rows = slice(j * TILE + h * POS, j * TILE + (h + 1) * POS)
            same = gate * (d0[rows, :].astype(f32) + d2[rows, :].astype(f32))
            odd = gate * (d1[rows, :].astype(f32) + d3[rows, :].astype(f32))
            first, second = jnp.where(even, same, odd), jnp.where(even, odd, same)
            out_ref[0, response, :, h * LANES : (h + 1) * LANES] = first.astype(bf16)
            out_ref[0, response, :, (GROUP + h) * LANES : (GROUP + h + 1) * LANES] = second.astype(bf16)


def swap(values):
    return lax.all_to_all(values, PEERS, split_axis=0, concat_axis=0, tiled=True)


def cross(values):
    return lax.ppermute(values, "pair", [(0, 1), (1, 0)])


def shift(values, by):
    return lax.ppermute(values, ROW, [(i, (i + by) % X) for i in range(X)])


def prompt_call(lengths, rows, kv):
    shape = jax.ShapeDtypeStruct
    count = X * TILE
    tables = (
        shape((count, LANES), bf16),
        shape((count, LANES), bf16),
        shape((X, TILE), f32),
        shape((X, TILE), f32),
    )
    sums = (shape((PEERS_N * PROMPT, LANES), f32),) * 2
    scratch = (pltpu.VMEM((2, PROMPT_BLOCK, count), bf16), pltpu.VMEM((2, PROMPT_BLOCK, count), bf16))
    cost = dict(flops=2 * 2 * 2048 * 1024 * 128 * 2, size=2 * 2**20, scratch=scratch)
    first = call(tables_kernel, tables, "svv", size=2**20)(lengths, rows[0], rows[2])
    key_sum, value_sum = call(functools.partial(prompt_kernel, True), sums, "vvvvv", **cost)(*first, kv)
    key_sum, source = lax.optimization_barrier((key_sum, kv))
    side = cross(source[:, KV_ROWS - SIDE : KV_ROWS, :])
    part, *second = call(
        functools.partial(prompt_kernel, False),
        (shape((PEERS_N, 2 * PROMPT, LANES), bf16),) + tables,
        "svvvvv",
        **cost,
    )(lengths, rows[1], rows[3], kv, key_sum, value_sum)
    return side, part, *first, *second


def resp_call(kv, side, prompt_part, *rows):
    shape = jax.ShapeDtypeStruct
    blocks = 2 * PEERS_N * POS // BLOCK
    return call(
        resp_kernel,
        (
            shape((PEERS_N, KV_ROWS, LANES), bf16),
            shape((8, LANES), f32),
        ),
        "v" * 11,
        out_spaces="av",
        scratch=(
            pltpu.VMEM((2, BLOCK, X * TILE), bf16),
            pltpu.VMEM((2, BLOCK, X * TILE), bf16),
            pltpu.VMEM((blocks, BLOCK // POS, SIDE, LANES), bf16),
            pltpu.SemaphoreType.DMA((blocks + 1,)),
        ),
        flops=4 * 2 * 1024 * 1024 * 128 * 2,
        size=3 * 2**20,
    )(kv, side, prompt_part, *rows)


def query_call(k, lengths, margin, rows, kv, side):
    extra = STAT_ROWS if k == 2 else 0
    return call(
        functools.partial(query_kernel, k),
        jax.ShapeDtypeStruct((2 * TILE + extra, LANES), bf16),
        "svvvv",
        flops=3 * 2 * 512 * 1536 * 128 * 2,
        size=3 * 2**20,
    )(lengths, margin, rows, kv, side)


def per_device(
    prompt_keys,
    prompt_values,
    queries,
    resp_keys,
    resp_values,
    resp_grads,
    resp_lse,
    resp_delta,
    logratio,
    lengths,
):
    shape = jax.ShapeDtypeStruct
    kv = call(
        kv_pack_kernel,
        shape((PEERS_N, KV_ROWS + MARGIN_ROWS, LANES), bf16),
        "aaaaaa",
        out_spaces="a",
        size=2 * 2**20,
        limit=60,
        scratch=(
            pltpu.SMEM((1, 3), jnp.int32),
            pltpu.VMEM((2, POS), f32),
            pltpu.VMEM((PROMPT, 2 * LANES), bf16),
            pltpu.VMEM((PROMPT, 2 * LANES), bf16),
            pltpu.VMEM((POS, X * LANES), bf16),
            pltpu.VMEM((POS, X * LANES), bf16),
            pltpu.VMEM((2, KV_ROWS + MARGIN_ROWS, LANES), bf16),
            pltpu.SemaphoreType.DMA((6 + ROWS_Y,)),
        ),
    )(lengths, logratio, prompt_keys, prompt_values, resp_keys, resp_values)
    kv = swap(kv)

    block = shape((2, QUERY_ROWS, LANES), bf16)
    own, other = call(
        query_pack_kernel,
        (block, block),
        "aaaa",
        size=2 * 2**20,
        scratch=(
            pltpu.VMEM((4, POS, GROUP * LANES), bf16),
            pltpu.VMEM((4, POS, GROUP * LANES), bf16),
            pltpu.VMEM((POS, X * GROUP), bf16),
            pltpu.VMEM((POS, X * GROUP), bf16),
            pltpu.SemaphoreType.DMA((10,)),
        ),
    )(queries, resp_grads, resp_lse, resp_delta)
    same, odd = call(join_kernel, (block, block), "vv", size=2**20)(own, cross(other))
    rows = (same, shift(odd, 1), shift(same, 2), shift(odd, 3))

    side, prompt_part, *tables = prompt_call(lengths, rows, kv)
    part, margin = resp_call(kv, side, prompt_part, *tables)
    grads = [query_call(k, lengths, margin, rows[k], kv, side) for k in range(X)]
    part = swap(part)
    back = [grads[0]] + [shift(grads[k], X - k) for k in range(1, X)]
    query_grad, gate = call(
        query_final_kernel,
        (shape((1, 2, POS, 2 * GROUP * LANES), bf16), shape((1,), f32)),
        "vvvvv",
        out_spaces="vs",
        size=2**20,
    )(margin, *back)
    outs = (shape((1, PROMPT, 2 * LANES), bf16),) * 2 + (shape((1, 2, POS, 2 * LANES), bf16),) * 2
    pk_grad, pv_grad, key_grad, value_grad = call(kv_final_kernel, outs, "svvv", size=2**20)(
        lengths, margin, back[2], part
    )
    return pk_grad, pv_grad, query_grad, key_grad, value_grad, gate


def solution(mesh):
    batch, pair, ctx = mesh.devices.shape
    split = Mesh(mesh.devices.reshape(batch, pair, ctx // X, 2, 2), ("batch", "pair", "y", "xh", "xl"))
    prompt_spec = P("batch", CTX, "pair")
    resp_spec = P("batch", "pair", CTX, None)
    out_spec = P("batch", None, CTX, "pair")
    return jax.shard_map(
        per_device,
        mesh=split,
        in_specs=(
            prompt_spec,
            prompt_spec,
            resp_spec,
            resp_spec,
            resp_spec,
            resp_spec,
            resp_spec,
            resp_spec,
            P("batch", None, CTX),
            P("batch", None),
        ),
        out_specs=(prompt_spec, prompt_spec, out_spec, out_spec, out_spec, P("batch")),
        check_vma=False,
    )
```

```python
import functools

import jax
import jax.numpy as jnp
from jax import lax
from jax.experimental import pallas as pl
from jax.experimental.pallas import tpu as pltpu
from jax.sharding import Mesh, PartitionSpec as P

beta_coef = 0.1
f32, bf16 = jnp.float32, jnp.bfloat16
LANES = 128
CTX = ("y", "xh", "xl")
ROW = ("xh", "xl")
PEERS = ("y", "xl")

X = 4
ROWS_Y = 8
PEERS_N = 16
POS = 32
PROMPT = 64
GROUP = 8
TILE = POS * GROUP
STAT_ROWS = 16
QUERY_ROWS = 2 * TILE + STAT_ROWS
SIDE = 2 * POS
KV_ROWS = 2 * PROMPT + 2 * SIDE
LOG2E = 1.4426950408889634
SCALE = LANES**-0.5
DEAD = 1e30
BLOCK = 512
PROMPT_BLOCK = 512
MARGIN_ROWS = 8


def dot(a, b, dims):
    return lax.dot_general(a, b, (dims, ((), ())), preferred_element_type=f32)


def call(kernel, out_shape, spaces, flops=0, scratch=(), size=0, limit=24, out_spaces=""):
    space = {"v": pltpu.VMEM, "s": pltpu.SMEM, "a": pl.ANY}
    many = isinstance(out_shape, tuple)
    out_spaces = out_spaces or "v" * (len(out_shape) if many else 1)
    out_specs = tuple(pl.BlockSpec(memory_space=space[s]) for s in out_spaces)
    return pl.pallas_call(
        kernel,
        out_shape=out_shape,
        in_specs=[pl.BlockSpec(memory_space=space[s]) for s in spaces],
        out_specs=out_specs if many else out_specs[0],
        scratch_shapes=list(scratch),
        compiler_params=pltpu.CompilerParams(vmem_limit_bytes=limit * 2**20),
        cost_estimate=pl.CostEstimate(flops=flops, bytes_accessed=size, transcendentals=0),
    )


def fetch(pairs, sems):
    copies = [pltpu.make_async_copy(a, b, sems.at[i]) for i, (a, b) in enumerate(pairs)]
    for copy in copies:
        copy.start()
    for copy in copies:
        copy.wait()


def split_margin(margin, rows):
    high = margin.astype(bf16).astype(f32)
    middle = (margin - high).astype(bf16).astype(f32)
    low = margin - high - middle
    lane = lax.broadcasted_iota(jnp.int32, (rows, LANES), 1)
    row = lax.broadcasted_iota(jnp.int32, (rows, LANES), 0)
    block = jnp.where(lane == 0, high, jnp.where(lane == 1, middle, jnp.where(lane == 2, low, 0.0)))
    return jnp.where(row == 0, block, 0.0).astype(bf16)


def gate_of(margin, block):
    other = jnp.sum(block.astype(f32), axis=0, keepdims=True)
    margin = margin + jnp.sum(other, axis=1, keepdims=True)
    return beta_coef * jax.nn.sigmoid(-beta_coef * margin)


def kv_pack_kernel(
    lengths_hbm, logratio_hbm, pk_hbm, pv_hbm, rk_hbm, rv_hbm, kv_ref, lengths, logratio, pk, pv, rk, rv, sems
):
    pairs = (
        (lengths_hbm, lengths),
        (logratio_hbm.at[0], logratio),
        (pk_hbm.at[0], pk),
        (pv_hbm.at[0], pv),
        (rk_hbm.at[0, 0], rk),
        (rv_hbm.at[0, 0], rv),
    )
    fetch(pairs, sems)
    first_core = lax.axis_index("pair") == 0
    ctx = lax.axis_index(CTX)
    position = ctx * POS + lax.broadcasted_iota(jnp.int32, (1, POS), 1)
    chosen = jnp.where(position < lengths[0, 1], logratio[0:1, :], 0.0)
    rejected = jnp.where(position < lengths[0, 2], logratio[1:2, :], 0.0)
    margin = jnp.sum(chosen - rejected, axis=1, keepdims=True)
    block = split_margin(margin, MARGIN_ROWS)
    live = ctx * PROMPT + lax.broadcasted_iota(jnp.int32, (PROMPT, LANES), 0) < lengths[0, 0]
    for xl in range(2):
        columns = slice(xl * LANES, (xl + 1) * LANES)
        others = slice((2 + xl) * LANES, (3 + xl) * LANES)
        parts = [jnp.where(live, pk[:, columns].astype(f32), 0.0).astype(bf16), pv[:, columns]]
        low_head = [ref[:, columns].astype(f32) for ref in (rk, rv)]
        high_head = [ref[:, others].astype(f32) for ref in (rk, rv)]
        parts += [jnp.where(first_core, a, b).astype(bf16) for a, b in zip(low_head, high_head)]
        parts += [jnp.where(first_core, b, a).astype(bf16) for a, b in zip(low_head, high_head)]
        parts += [block]
        for y in range(ROWS_Y):
            at = 0
            for part in parts:
                kv_ref[y * 2 + xl, at : at + part.shape[0], :] = part
                at += part.shape[0]


def query_pack_kernel(q_hbm, g_hbm, lse_hbm, delta_hbm, own_ref, other_ref, q, g, lse, delta, sems):
    core, parity = lax.axis_index("pair"), lax.axis_index("xl")
    pairs = [(lse_hbm.at[0, 0], lse), (delta_hbm.at[0, 0], delta)]
    heads = []
    for i in range(4):
        head = 2 * (core if i < 2 else 1 - core) + (parity + i) % 2
        heads.append(head)
        columns = pl.ds(pl.multiple_of(head * GROUP * LANES, GROUP * LANES), GROUP * LANES)
        pairs += [(q_hbm.at[0, 0, :, columns], q.at[i]), (g_hbm.at[0, 0, :, columns], g.at[i])]
    fetch(pairs, sems)
    sign = jnp.where(core == 0, -1.0, 1.0).astype(f32)

    count = X * GROUP
    lane = lax.broadcasted_iota(jnp.int32, (POS, TILE), 1)
    spread = (lane % POS == lax.broadcasted_iota(jnp.int32, (POS, TILE), 0)).astype(bf16)
    head_of = lax.broadcasted_iota(jnp.int32, (count, TILE), 0)
    lane = lax.broadcasted_iota(jnp.int32, (count, TILE), 1)
    lse_rows = dot(lse[...], spread, ((0,), (0,)))
    delta_rows = dot(delta[...], spread, ((0,), (0,))) * sign
    row = lax.broadcasted_iota(jnp.int32, (STAT_ROWS, LANES), 0)
    for i in range(4):
        ref, slot = (own_ref, other_ref)[i // 2], i % 2
        for h in range(GROUP):
            columns = slice(h * LANES, (h + 1) * LANES)
            ref[slot, h * POS : (h + 1) * POS, :] = q[i, :, columns]
            grad = (g[i, :, columns].astype(f32) * sign).astype(bf16)
            ref[slot, TILE + h * POS : TILE + (h + 1) * POS, :] = grad
        keep = head_of == heads[i] * GROUP + lane // POS
        block = jnp.zeros((STAT_ROWS, LANES), f32)
        for n, rows in enumerate((lse_rows, delta_rows)):
            line = jnp.sum(jnp.where(keep, rows, 0.0), axis=0, keepdims=True)
            block = jnp.where(row == 2 * n, line[:, :LANES], block)
            block = jnp.where(row == 2 * n + 1, line[:, LANES:], block)
        ref[slot, 2 * TILE :, :] = block.astype(bf16)


def join_kernel(own_ref, other_ref, same_ref, odd_ref):
    for i, ref in enumerate((same_ref, odd_ref)):
        ref[0] = own_ref[i]
        ref[1] = other_ref[i]


def row_position(k):
    x = (lax.axis_index(ROW) + X - k) % X
    return (lax.axis_index("y") * X + x) * POS + lax.broadcasted_iota(jnp.int32, (1, TILE), 1) % POS


def key_positions(block, count):
    index = lax.broadcasted_iota(jnp.int32, (count, 1), 0)
    source = block * (count // POS) + index // POS
    ctx = source // 2 * X + 2 * lax.axis_index("xh") + source % 2
    return ctx * POS + index % POS


def row_stats(lengths_ref, block, k, j):
    block = block.astype(f32)
    lse = jnp.concatenate([block[0:1], block[1:2]], axis=1) * LOG2E
    delta = jnp.concatenate([block[2:3], block[3:4]], axis=1)
    core = lax.axis_index("pair")
    response = core + j - 2 * core * j
    return jnp.where(row_position(k) < lengths_ref[0, 1 + response], lse, DEAD), delta


def cell(key, value, query, grad, lse, delta, allowed=None):
    scores = dot(key, query, ((1,), (1,)))
    weights = jnp.exp2(scores * (SCALE * LOG2E) - lse)
    if allowed is not None:
        weights = jnp.where(allowed, weights, 0.0)
    weight_grads = dot(value, grad, ((1,), (1,)))
    score_grads = (weights * (weight_grads - delta)).astype(bf16)
    return weights.astype(bf16), score_grads


def staged(blocks, first, second):
    for i, block in enumerate(blocks):
        first(*block, i % 2)
        if i:
            second(*blocks[i - 1], (i - 1) % 2)
    second(*blocks[-1], (len(blocks) - 1) % 2)


def tile_rows(tile):
    return slice(tile * TILE, (tile + 1) * TILE)


def fill_tables(first_half, lengths_ref, sources, query_rows, grad_rows, lse_ref, delta_ref):
    for n, ref in enumerate(sources):
        for j in range(2):
            t = j * 2 + n
            at = tile_rows(t)
            query_rows[at, :] = ref[j, 0:TILE, :]
            grad_rows[at, :] = ref[j, TILE : 2 * TILE, :]
            k = 2 * n if first_half else 2 * n + 1
            lse, delta = row_stats(lengths_ref, ref[j, 2 * TILE :, :], k, j)
            lse_ref[t : t + 1, :], delta_ref[t : t + 1, :] = lse, delta


def tables_kernel(lengths_ref, qa, qb, *tables):
    fill_tables(True, lengths_ref, (qa, qb), *tables)


def prompt_kernel(first_half, *refs):
    if first_half:
        query_rows, grad_rows, lse_ref, delta_ref, kv_ref, key_sum, value_sum, weights, score_grads = refs
    else:
        lengths_ref, qa, qb, kv_ref, key_sum, value_sum, out_ref = refs[:7]
        query_rows, grad_rows, lse_ref, delta_ref, weights, score_grads = refs[7:]
        fill_tables(False, lengths_ref, (qa, qb), query_rows, grad_rows, lse_ref, delta_ref)
    per = PROMPT_BLOCK // PROMPT

    def first(c, slot):
        rows = slice(c * per, (c + 1) * per)
        key = kv_ref[rows, 0:PROMPT, :].reshape(PROMPT_BLOCK, LANES)
        value = kv_ref[rows, PROMPT : 2 * PROMPT, :].reshape(PROMPT_BLOCK, LANES)
        for t in range(X):
            at = tile_rows(t)
            weights[slot, :, at], score_grads[slot, :, at] = cell(
                key, value, query_rows[at, :], grad_rows[at, :], lse_ref[t : t + 1, :], delta_ref[t : t + 1, :]
            )

    def second(c, slot):
        value_grad = dot(weights[slot], grad_rows[...], ((1,), (0,)))
        key_grad = dot(score_grads[slot], query_rows[...], ((1,), (0,)))
        at = slice(c * PROMPT_BLOCK, (c + 1) * PROMPT_BLOCK)
        if first_half:
            key_sum[at, :], value_sum[at, :] = key_grad, value_grad
        else:
            shape = (per, PROMPT, LANES)
            to = slice(c * per, (c + 1) * per)
            out_ref[to, 0:PROMPT, :] = ((key_sum[at, :] + key_grad) * SCALE).astype(bf16).reshape(shape)
            out_ref[to, PROMPT:, :] = (value_sum[at, :] + value_grad).astype(bf16).reshape(shape)

    staged([(c,) for c in range(PEERS_N // per)], first, second)


def resp_kernel(
    kv_ref, side_ref, prompt_ref, query_a, grad_a, lse_a, delta_a, query_b, grad_b, lse_b, delta_b,
    out_hbm, margin_ref, weights, score_grads, parts, sems,
):
    halves = ((query_a, grad_a, lse_a, delta_a), (query_b, grad_b, lse_b, delta_b))
    copies = [pltpu.make_async_copy(prompt_ref, out_hbm.at[:, 0 : 2 * PROMPT, :], sems.at[0])]
    copies[0].start()
    margin = jnp.sum(kv_ref[:, KV_ROWS:, :].astype(f32), axis=(0, 1), keepdims=True).reshape(1, LANES)
    margin = jnp.sum(margin, axis=1, keepdims=True)
    margin_ref[...] = jnp.broadcast_to(margin, margin_ref.shape)
    per = BLOCK // POS
    blocks = PEERS_N // per
    sources = ((kv_ref, 2 * PROMPT), (side_ref, 0))

    def first(j, c, slot):
        ref, start = sources[j]
        rows = slice(c * per, (c + 1) * per)
        key = ref[rows, start : start + POS, :].reshape(BLOCK, LANES)
        value = ref[rows, start + POS : start + SIDE, :].reshape(BLOCK, LANES)
        positions = key_positions(c, BLOCK)
        for k in range(X):
            query_rows, grad_rows, lse_ref, delta_ref = halves[k % 2]
            t = j * 2 + k // 2
            at, to = tile_rows(t), tile_rows(k % 2 * 2 + k // 2)
            weights[slot, :, to], score_grads[slot, :, to] = cell(
                key,
                value,
                query_rows[at, :],
                grad_rows[at, :],
                lse_ref[t : t + 1, :],
                delta_ref[t : t + 1, :],
                positions <= row_position(k),
            )

    def second(j, c, slot):
        rows = slice(j * 2 * TILE, (j + 1) * 2 * TILE)
        value_grad, key_grad = None, None
        for n, (query_rows, grad_rows, _, _) in enumerate(halves):
            columns = slice(n * 2 * TILE, (n + 1) * 2 * TILE)
            value_term = dot(weights[slot, :, columns], grad_rows[rows, :], ((1,), (0,)))
            key_term = dot(score_grads[slot, :, columns], query_rows[rows, :], ((1,), (0,)))
            value_grad = value_term if n == 0 else value_grad + value_term
            key_grad = key_term if n == 0 else key_grad + key_term
        key_grad *= SCALE
        shape = (per, POS, LANES)
        n = j * blocks + c
        parts[n, :, 0:POS, :] = key_grad.astype(bf16).reshape(shape)
        parts[n, :, POS:, :] = value_grad.astype(bf16).reshape(shape)
        start = 2 * PROMPT + j * SIDE
        to = out_hbm.at[c * per : (c + 1) * per, start : start + SIDE, :]
        copies.append(pltpu.make_async_copy(parts.at[n], to, sems.at[1 + n]))
        copies[-1].start()

    staged([(j, c) for j in range(2) for c in range(blocks)], first, second)
    for copy in copies:
        copy.wait()


def query_kernel(k, lengths_ref, margin_ref, q_ref, kv_ref, side_ref, out_ref):
    items = []
    for j in range(2):
        resp, start = ((kv_ref, 2 * PROMPT), (side_ref, 0))[j]
        items += [(j, kv_ref, c, PROMPT, 0) for c in range(PEERS_N * PROMPT // BLOCK)]
        items += [(j, resp, c, POS, start) for c in range(PEERS_N * POS // BLOCK)]
    totals, waiting = [None, None], None
    for item in items + [None]:
        if item:
            j, ref, c, count, start = item
            per = BLOCK // count
            rows = slice(c * per, (c + 1) * per)
            key = ref[rows, start : start + count, :].reshape(BLOCK, LANES)
            value = ref[rows, start + count : start + 2 * count, :].reshape(BLOCK, LANES)
            allowed = key_positions(c, BLOCK) <= row_position(k) if count == POS else None
            lse, delta = row_stats(lengths_ref, q_ref[j, 2 * TILE :, :], k, j)
            _, score_grads = cell(
                key, value, q_ref[j, 0:TILE, :], q_ref[j, TILE : 2 * TILE, :], lse, delta, allowed
            )
        if waiting:
            n, grads, keys = waiting
            term = dot(keys, grads, ((0,), (0,)))
            totals[n] = term if totals[n] is None else totals[n] + term
        waiting = (j, score_grads, key)
    for j in range(2):
        out_ref[tile_rows(j), :] = jnp.transpose(totals[j] * SCALE).astype(bf16)
    if k == 2:
        out_ref[2 * TILE :, :] = split_margin(margin_ref[0:1, 0:1], STAT_ROWS)


def kv_final_kernel(lengths_ref, margin_ref, d2, part_ref, pk_ref, pv_ref, rk_ref, rv_ref):
    gate = gate_of(margin_ref[0:1, 0:1], d2[2 * TILE :, :])
    core = lax.axis_index("pair")
    live = lax.axis_index(CTX) * PROMPT + lax.broadcasted_iota(jnp.int32, (PROMPT, LANES), 0) < lengths_ref[0, 0]
    for xl in range(2):
        columns = slice(xl * LANES, (xl + 1) * LANES)
        total = part_ref[xl].astype(f32)
        for y in range(1, ROWS_Y):
            total += part_ref[y * 2 + xl].astype(f32)
        total = total * gate
        pk_ref[0, :, columns] = jnp.where(live, total[0:PROMPT], 0.0).astype(bf16)
        pv_ref[0, :, columns] = jnp.where(live, total[PROMPT : 2 * PROMPT], 0.0).astype(bf16)
        for j in range(2):
            response = core + j - 2 * core * j
            at = 2 * PROMPT + j * SIDE
            rk_ref[0, response, :, columns] = total[at : at + POS].astype(bf16)
            rv_ref[0, response, :, columns] = total[at + POS : at + SIDE].astype(bf16)


def query_final_kernel(margin_ref, d0, d1, d2, d3, out_ref, gate_ref):
    gate = gate_of(margin_ref[0:1, 0:1], d2[2 * TILE :, :])
    gate_ref[0] = gate[0, 0]
    core = lax.axis_index("pair")
    even = lax.axis_index("xl") == 0
    for j in range(2):
        response = core + j - 2 * core * j
        for h in range(GROUP):
            rows = slice(j * TILE + h * POS, j * TILE + (h + 1) * POS)
            same = gate * (d0[rows, :].astype(f32) + d2[rows, :].astype(f32))
            odd = gate * (d1[rows, :].astype(f32) + d3[rows, :].astype(f32))
            first, second = jnp.where(even, same, odd), jnp.where(even, odd, same)
            out_ref[0, response, :, h * LANES : (h + 1) * LANES] = first.astype(bf16)
            out_ref[0, response, :, (GROUP + h) * LANES : (GROUP + h + 1) * LANES] = second.astype(bf16)


def swap(values):
    return lax.all_to_all(values, PEERS, split_axis=0, concat_axis=0, tiled=True)


def cross(values):
    return lax.ppermute(values, "pair", [(0, 1), (1, 0)])


def shift(values, by):
    return lax.ppermute(values, ROW, [(i, (i + by) % X) for i in range(X)])


def prompt_call(lengths, rows, kv):
    shape = jax.ShapeDtypeStruct
    count = X * TILE
    tables = (
        shape((count, LANES), bf16),
        shape((count, LANES), bf16),
        shape((X, TILE), f32),
        shape((X, TILE), f32),
    )
    sums = (shape((PEERS_N * PROMPT, LANES), f32),) * 2
    scratch = (pltpu.VMEM((2, PROMPT_BLOCK, count), bf16), pltpu.VMEM((2, PROMPT_BLOCK, count), bf16))
    cost = dict(flops=2 * 2 * 2048 * 1024 * 128 * 2, size=2 * 2**20, scratch=scratch)
    first = call(tables_kernel, tables, "svv", size=2**20)(lengths, rows[0], rows[2])
    key_sum, value_sum = call(functools.partial(prompt_kernel, True), sums, "vvvvv", **cost)(*first, kv)
    key_sum, source = lax.optimization_barrier((key_sum, kv))
    side = cross(source[:, KV_ROWS - SIDE : KV_ROWS, :])
    part, *second = call(
        functools.partial(prompt_kernel, False),
        (shape((PEERS_N, 2 * PROMPT, LANES), bf16),) + tables,
        "svvvvv",
        **cost,
    )(lengths, rows[1], rows[3], kv, key_sum, value_sum)
    return side, part, *first, *second


def resp_call(kv, side, prompt_part, *rows):
    shape = jax.ShapeDtypeStruct
    blocks = 2 * PEERS_N * POS // BLOCK
    return call(
        resp_kernel,
        (
            shape((PEERS_N, KV_ROWS, LANES), bf16),
            shape((8, LANES), f32),
        ),
        "v" * 11,
        out_spaces="av",
        scratch=(
            pltpu.VMEM((2, BLOCK, X * TILE), bf16),
            pltpu.VMEM((2, BLOCK, X * TILE), bf16),
            pltpu.VMEM((blocks, BLOCK // POS, SIDE, LANES), bf16),
            pltpu.SemaphoreType.DMA((blocks + 1,)),
        ),
        flops=4 * 2 * 1024 * 1024 * 128 * 2,
        size=3 * 2**20,
    )(kv, side, prompt_part, *rows)


def query_call(k, lengths, margin, rows, kv, side):
    extra = STAT_ROWS if k == 2 else 0
    return call(
        functools.partial(query_kernel, k),
        jax.ShapeDtypeStruct((2 * TILE + extra, LANES), bf16),
        "svvvv",
        flops=3 * 2 * 512 * 1536 * 128 * 2,
        size=3 * 2**20,
    )(lengths, margin, rows, kv, side)


def per_device(
    prompt_keys,
    prompt_values,
    queries,
    resp_keys,
    resp_values,
    resp_grads,
    resp_lse,
    resp_delta,
    logratio,
    lengths,
):
    shape = jax.ShapeDtypeStruct
    kv = call(
        kv_pack_kernel,
        shape((PEERS_N, KV_ROWS + MARGIN_ROWS, LANES), bf16),
        "aaaaaa",
        size=2 * 2**20,
        limit=60,
        scratch=(
            pltpu.SMEM((1, 3), jnp.int32),
            pltpu.VMEM((2, POS), f32),
            pltpu.VMEM((PROMPT, 2 * LANES), bf16),
            pltpu.VMEM((PROMPT, 2 * LANES), bf16),
            pltpu.VMEM((POS, X * LANES), bf16),
            pltpu.VMEM((POS, X * LANES), bf16),
            pltpu.SemaphoreType.DMA((6,)),
        ),
    )(lengths, logratio, prompt_keys, prompt_values, resp_keys, resp_values)
    kv = swap(kv)

    block = shape((2, QUERY_ROWS, LANES), bf16)
    own, other = call(
        query_pack_kernel,
        (block, block),
        "aaaa",
        size=2 * 2**20,
        scratch=(
            pltpu.VMEM((4, POS, GROUP * LANES), bf16),
            pltpu.VMEM((4, POS, GROUP * LANES), bf16),
            pltpu.VMEM((POS, X * GROUP), bf16),
            pltpu.VMEM((POS, X * GROUP), bf16),
            pltpu.SemaphoreType.DMA((10,)),
        ),
    )(queries, resp_grads, resp_lse, resp_delta)
    same, odd = call(join_kernel, (block, block), "vv", size=2**20)(own, cross(other))
    rows = (same, shift(odd, 1), shift(same, 2), shift(odd, 3))

    side, prompt_part, *tables = prompt_call(lengths, rows, kv)
    part, margin = resp_call(kv, side, prompt_part, *tables)
    grads = [query_call(k, lengths, margin, rows[k], kv, side) for k in range(X)]
    part = swap(part)
    back = [grads[0]] + [shift(grads[k], X - k) for k in range(1, X)]
    query_grad, gate = call(
        query_final_kernel,
        (shape((1, 2, POS, 2 * GROUP * LANES), bf16), shape((1,), f32)),
        "vvvvv",
        out_spaces="vs",
        size=2**20,
    )(margin, *back)
    outs = (shape((1, PROMPT, 2 * LANES), bf16),) * 2 + (shape((1, 2, POS, 2 * LANES), bf16),) * 2
    pk_grad, pv_grad, key_grad, value_grad = call(kv_final_kernel, outs, "svvv", size=2**20)(
        lengths, margin, back[2], part
    )
    return pk_grad, pv_grad, query_grad, key_grad, value_grad, gate


def solution(mesh):
    batch, pair, ctx = mesh.devices.shape
    split = Mesh(mesh.devices.reshape(batch, pair, ctx // X, 2, 2), ("batch", "pair", "y", "xh", "xl"))
    prompt_spec = P("batch", CTX, "pair")
    resp_spec = P("batch", "pair", CTX, None)
    out_spec = P("batch", None, CTX, "pair")
    return jax.shard_map(
        per_device,
        mesh=split,
        in_specs=(
            prompt_spec,
            prompt_spec,
            resp_spec,
            resp_spec,
            resp_spec,
            resp_spec,
            resp_spec,
            resp_spec,
            P("batch", None, CTX),
            P("batch", None),
        ),
        out_specs=(prompt_spec, prompt_spec, out_spec, out_spec, out_spec, P("batch")),
        check_vma=False,
    )
```
